128 devices in a mesh: wide: 16 (over z, x), narrow: 8 (over y, core).
Axes of the slice: x: 4, y: 4, z: 4, core: 2. Of those that a mesh axis runs over, the one named last changes fastest.
Arguments:
- solid_density_share: float32 [128, 256, 256], P('wide', 'narrow'), may hold values from 0.1 to 1
- primal_warmth_vector: float32 [128, 256, 256], P('wide', 'narrow'), may hold values from 0.5 to 2
- voxel_aim_scale: float32 [128, 256, 256], P('wide', 'narrow'), may hold values from 0.000375 to 0.009, as said below
- coolant_transfer_factor: float32 [128, 256, 256], P('wide', 'narrow'), may hold values from 0.0003 to 0.003
Outputs:
- adjoint_warmth_vector: float32 [128, 256, 256], P('wide', 'narrow')
- sensitivity: float32 [128, 256, 256], P('wide', 'narrow')
The draws below stay inside these ranges and needn't reach their ends.
Inputs may be any that keep to these rules, and one draw needn't show every extreme that they name: voxel_aim_scale is positive.
All inputs are finite; a program needn't handle non-finite values.
Results may differ from the reference program's by a relative error of at most 0.0003.
Values sent between devices are 32-bit elements; how exact they have to be, the bound alone decides.
A program may use at most 128 MiB of HBM per device.

```python
import math
import jax
import jax.numpy as jnp
from jax import lax

LEVELS = 4
SWEEPS = 3
COARSE_ITERS = 8
FILTER_SWEEPS = 4
RADIUS = 4
CELLS_ALONG_X = 128
CELLS_ALONG_Y = 256
CELLS_ALONG_Z = 256


def draw_voxel_aim_scale(key, part):
    key = jax.random.fold_in(key, 11)
    position_x = jnp.arange(CELLS_ALONG_X, dtype=jnp.float32)[:, None, None] / (CELLS_ALONG_X - 1)
    roughness = jnp.exp(jax.random.uniform(key, (CELLS_ALONG_X, CELLS_ALONG_Y, CELLS_ALONG_Z), jnp.float32, -0.6931472, 0.6931472))
    return 0.0015 * roughness * (1.0 + 2.0 * position_x)


def block_scale(rng, shape, shards, low, largest):
    def one(dim, parts):
        steps = jax.random.uniform(jax.random.fold_in(jax.random.fold_in(rng, 6), dim), (parts,), jnp.float32, low / len(shards), largest / len(shards))
        return jnp.repeat(jnp.exp(steps), shape[dim] // parts).reshape((-1,) + (1,) * (len(shape) - dim - 1))

    loudness = one(*shards[0])
    for cut in shards[1:]:
        loudness = loudness * one(*cut)
    return loudness


def setup_inputs(seed: int = 0) -> dict:
    arg_keys = jax.random.split(jax.random.key(seed), 5)
    return {
        "solid_density_share": jnp.clip(0.1 + 0.9 * jax.random.uniform(arg_keys[0], (CELLS_ALONG_X, CELLS_ALONG_Y, CELLS_ALONG_Z), jnp.float32) ** block_scale(arg_keys[0], (CELLS_ALONG_X, CELLS_ALONG_Y, CELLS_ALONG_Z), ((0, 16), (1, 8)), -0.2, 0.2), 0.1, 1.0),
        "primal_warmth_vector": jnp.clip(0.5 + 1.5 * jax.random.uniform(arg_keys[1], (CELLS_ALONG_X, CELLS_ALONG_Y, CELLS_ALONG_Z), jnp.float32) ** block_scale(arg_keys[1], (CELLS_ALONG_X, CELLS_ALONG_Y, CELLS_ALONG_Z), ((0, 16), (1, 8)), -0.2, 0.2), 0.5, 2.0),
        "voxel_aim_scale": draw_voxel_aim_scale(jax.random.fold_in(arg_keys[4], 71), 0),
        "coolant_transfer_factor": jnp.clip(jnp.exp(math.log(0.003) - 2.3025851 * jax.random.uniform(arg_keys[3], (CELLS_ALONG_X, CELLS_ALONG_Y, CELLS_ALONG_Z), jnp.float32) ** block_scale(arg_keys[3], (CELLS_ALONG_X, CELLS_ALONG_Y, CELLS_ALONG_Z), ((0, 16), (1, 8)), -0.2, 0.2)), 0.0003, 0.003),
    }


FLOOR_CONDUCTION = 0.001
OMEGA = 0.7
FILTER_OMEGA = 0.8

def boundary_flags(starts, counts, totals):
    indicator_numbers = []
    for across in range(3):
        position = starts[across] + jnp.arange(counts[across], dtype=jnp.int32)
        layout = [1, 1, 1]
        layout[across] = counts[across]
        upward = (position + 1 < totals[across]) & (position + 1 >= 0)
        downward = (position - 1 >= 0) & (position - 1 < totals[across])
        indicator_numbers.append(upward.reshape(layout))
        indicator_numbers.append(downward.reshape(layout))
    return indicator_numbers

def six_neighbours(padded):
    centre = padded[1:-1, 1:-1, 1:-1]
    beside = (padded[2:, 1:-1, 1:-1], padded[:-2, 1:-1, 1:-1], padded[1:-1, 2:, 1:-1], padded[1:-1, :-2, 1:-1], padded[1:-1, 1:-1, 2:], padded[1:-1, 1:-1, :-2])
    return (centre, beside)

def face_conductances(cond_padded, indicator_numbers):
    centre, beside = six_neighbours(cond_padded)
    up_faces = tuple((jnp.where(indicator_numbers[2 * across], 0.5 * (centre + beside[2 * across]), 0.0) for across in range(3)))
    down_faces = tuple((jnp.where(indicator_numbers[2 * across + 1], 0.5 * (beside[2 * across + 1] + centre), 0.0) for across in range(3)))
    return (up_faces, down_faces)

def six_blocks(values):
    extent = values.shape
    return values.reshape(extent[0] // 2, 2, extent[1] // 2, 2, extent[2] // 2, 2)

def coarsen(coeffs):
    sink_term, up_faces, down_faces = coeffs
    new_sink = lax.optimization_barrier(jnp.sum(six_blocks(sink_term), axis=(1, 3, 5)))
    new_up = (0.5 * lax.optimization_barrier(jnp.sum(six_blocks(up_faces[0])[:, 1], axis=(2, 4))), 0.5 * lax.optimization_barrier(jnp.sum(six_blocks(up_faces[1])[:, :, :, 1], axis=(1, 4))), 0.5 * lax.optimization_barrier(jnp.sum(six_blocks(up_faces[2])[:, :, :, :, :, 1], axis=(1, 3))))
    new_down = (0.5 * lax.optimization_barrier(jnp.sum(six_blocks(down_faces[0])[:, 0], axis=(2, 4))), 0.5 * lax.optimization_barrier(jnp.sum(six_blocks(down_faces[1])[:, :, :, 0], axis=(1, 4))), 0.5 * lax.optimization_barrier(jnp.sum(six_blocks(down_faces[2])[:, :, :, :, :, 0], axis=(1, 3))))
    return (new_sink, new_up, new_down)

def diagonal_of(coeffs):
    sink_term, up_faces, down_faces = coeffs
    return sink_term + up_faces[0] + down_faces[0] + up_faces[1] + down_faces[1] + up_faces[2] + down_faces[2]

def apply_operator(padded, coeffs):
    sink_term, up_faces, down_faces = coeffs
    centre, beside = six_neighbours(padded)
    result = sink_term * centre
    for across in range(3):
        result = result + up_faces[across] * (centre - beside[2 * across]) + down_faces[across] * (centre - beside[2 * across + 1])
    return result

def restrict(values):
    return lax.optimization_barrier(jnp.sum(six_blocks(values), axis=(1, 3, 5)))

def prolong(values):
    extent = values.shape
    spread = jnp.broadcast_to(values[:, None, :, None, :, None], (extent[0], 2, extent[1], 2, extent[2], 2))
    return spread.reshape(2 * extent[0], 2 * extent[1], 2 * extent[2])

def pad_all(values):
    return jnp.pad(values, 1)

def conjugate_solve(right_side, coeffs, extend, norm_sum, curve_sum):
    solution = jnp.zeros_like(right_side)
    residual = right_side
    direction = right_side
    norm_now = norm_sum(residual * residual)
    for count_iter in range(COARSE_ITERS):
        applied = apply_operator(extend(direction), coeffs)
        step_size = norm_now / curve_sum(direction * applied)
        solution = solution + step_size * direction
        residual = residual - step_size * applied
        if count_iter + 1 < COARSE_ITERS:
            norm_next = norm_sum(residual * residual)
            direction = residual + norm_next / norm_now * direction
            norm_now = norm_next
    return solution

def vcycle_pass(grid_level, right_side, grid_ladder, matrix_diagonal_list):
    coeffs = grid_ladder[grid_level]
    if grid_level == LEVELS - 1:
        return conjugate_solve(right_side, coeffs, pad_all, jnp.sum, jnp.sum)
    diagonal = matrix_diagonal_list[grid_level]
    current = OMEGA * right_side / diagonal
    for _ in range(SWEEPS - 1):
        current = current + OMEGA * (right_side - apply_operator(pad_all(current), coeffs)) / diagonal
    coarse_rhs = restrict(right_side - apply_operator(pad_all(current), coeffs))
    correction = vcycle_pass(grid_level + 1, coarse_rhs, grid_ladder, matrix_diagonal_list)
    current = current + prolong(correction)
    for _ in range(SWEEPS):
        current = current + OMEGA * (right_side - apply_operator(pad_all(current), coeffs)) / diagonal
    return current

def conduction_slope(temp_padded, adj_padded, indicator_numbers):
    temp_centre, temp_beside = six_neighbours(temp_padded)
    adj_centre, adj_beside = six_neighbours(adj_padded)
    running = jnp.zeros_like(temp_centre)
    for neighbour in range(6):
        product = (temp_centre - temp_beside[neighbour]) * (adj_centre - adj_beside[neighbour])
        running = running + jnp.where(indicator_numbers[neighbour], product, 0.0)
    return -0.5 * running

def filter_sweep(padded, source, indicator_numbers, strength):
    centre, beside = six_neighbours(padded)
    spread = jnp.zeros_like(centre)
    for neighbour in range(6):
        spread = spread + jnp.where(indicator_numbers[neighbour], beside[neighbour] - centre, 0.0)
    applied = centre - strength * spread
    return centre + FILTER_OMEGA * (source - applied) / (1.0 + 6.0 * strength)

def reference(solid_density_share, primal_warmth_vector, voxel_aim_scale, coolant_transfer_factor):
    conductivity = FLOOR_CONDUCTION + (1.0 - FLOOR_CONDUCTION) * solid_density_share * solid_density_share * solid_density_share
    extent = solid_density_share.shape
    indicator_numbers = boundary_flags((0, 0, 0), extent, extent)
    up_faces, down_faces = face_conductances(jnp.pad(conductivity, 1), indicator_numbers)
    grid_ladder = [(coolant_transfer_factor, up_faces, down_faces)]
    for grid_level in range(1, LEVELS):
        grid_ladder.append(coarsen(grid_ladder[-1]))
    matrix_diagonal_list = [diagonal_of(coeffs) for coeffs in grid_ladder[:-1]]
    adjoint_warmth_vector = vcycle_pass(0, voxel_aim_scale, grid_ladder, matrix_diagonal_list)
    prefilter_gradient = conduction_slope(jnp.pad(primal_warmth_vector, 1), jnp.pad(adjoint_warmth_vector, 1), indicator_numbers) * (3.0 * (1.0 - FLOOR_CONDUCTION)) * solid_density_share * solid_density_share
    thermal_energy_goal = jnp.sum(voxel_aim_scale * primal_warmth_vector)
    scaled = prefilter_gradient / (thermal_energy_goal / (CELLS_ALONG_X * CELLS_ALONG_Y * CELLS_ALONG_Z))
    strength = (RADIUS / (2.0 * math.sqrt(3.0))) ** 2
    relaxed_result = scaled
    for _ in range(FILTER_SWEEPS):
        relaxed_result = filter_sweep(jnp.pad(relaxed_result, 1), scaled, indicator_numbers, strength)
    return (adjoint_warmth_vector, relaxed_result)
```

```python
import functools
import math

import jax
import jax.numpy as jnp
from jax import lax
from jax.experimental import pallas as pl
from jax.experimental.pallas import tpu as pltpu
from jax.sharding import PartitionSpec as P

COARSE_ITERS = 8
RADIUS = 4
FLOOR_CONDUCTION = 0.001
OMEGA = 0.7
FILTER_OMEGA = 0.8
STRENGTH = (RADIUS / (2.0 * math.sqrt(3.0))) ** 2
MESH = pl.DeviceIdType.MESH
NW, NN = 16, 8
CELLS = 128 * 256 * 256
F32 = jnp.float32
HI = lax.Precision.HIGHEST
N_SEMS = 200


def near_peers(reach):
    return [
        (dw, dn)
        for dw in range(-reach, reach + 1)
        for dn in (-1, 0, 1)
        if (dw, dn) != (0, 0)
    ]


def all_peers():
    peers = [(dw % NW, dn % NN) for dw, dn in near_peers(3)]
    peers += [(0, k) for k in range(1, NN)] + [(k, 0) for k in range(1, NW)]
    return sorted(set(peers))


class Wire:
    def __init__(self, wide, narrow, send_sem, recv_sem):
        self.wide, self.narrow = wide, narrow
        self.send_sem, self.recv_sem = send_sem, recv_sem
        self.count = 0
        self.unsent = []

    def peer(self, dw, dn):
        return (lax.rem(self.wide + (dw + NW), NW), lax.rem(self.narrow + (dn + NN), NN))

    def send(self, src, dst, dw, dn):
        copy = pltpu.make_async_remote_copy(
            src_ref=src,
            dst_ref=dst,
            send_sem=self.send_sem.at[self.count],
            recv_sem=self.recv_sem.at[self.count],
            device_id=self.peer(dw, dn),
            device_id_type=MESH,
        )
        self.count += 1
        copy.start()
        self.unsent.append(copy)
        return copy

    def flush(self, keep=0):
        done = self.unsent[: len(self.unsent) - keep]
        self.unsent = self.unsent[len(self.unsent) - keep :]
        for copy in done:
            copy.wait_send()


def cut(own, halo, width, shift):
    if shift == 0:
        return pl.ds(halo, own), pl.ds(halo, own)
    if shift > 0:
        return pl.ds(halo + own - width, width), pl.ds(halo - width, width)
    return pl.ds(halo, width), pl.ds(halo + own, width)


def up_y(v):
    return pltpu.roll(v, v.shape[0] - 1, 0)


def down_y(v):
    return pltpu.roll(v, 1, 0)


def up_z(v):
    return pltpu.roll(v, v.shape[1] - 1, 1)


def down_z(v):
    return pltpu.roll(v, 1, 1)


def coupling(u, ux, uy, uz, i):
    centre = u[i]
    fy, fz = uy[i], uz[i]
    return centre, (
        (ux[i] * u[i + 1] + ux[i - 1] * u[i - 1])
        + (fy * up_y(centre) + down_y(fy * centre))
        + (fz * up_z(centre) + down_z(fz * centre))
    )


def sweep(src, dst, rhs, ux, uy, uz, weight, lo, hi):
    def body(i, carry):
        centre, pull = coupling(src, ux, uy, uz, i)
        dst[i] = (1.0 - OMEGA) * centre + weight[i] * (rhs[i] + pull)
        return carry

    lax.fori_loop(lo, hi, body, 0)


def residual_at(src, rhs, ux, uy, uz, diag, i):
    centre, pull = coupling(src, ux, uy, uz, i)
    return rhs[i] + pull - diag[i] * centre


def weights(sink, ux, uy, uz, diag, weight, lo, hi):
    def body(i, carry):
        fy, fz = uy[i], uz[i]
        total = sink[i] + (ux[i] + ux[i - 1]) + (fy + down_y(fy)) + (fz + down_z(fz))
        diag[i] = total
        weight[i] = OMEGA / total
        return carry

    lax.fori_loop(lo, hi, body, 0)


def dot(a, b):
    return jnp.dot(a, b, precision=HI, preferred_element_type=F32)


def pair_matrix(rows, cols, odd):
    k = lax.broadcasted_iota(jnp.int32, (rows, cols), 0)
    j = lax.broadcasted_iota(jnp.int32, (rows, cols), 1)
    hit = (k == 2 * j + 1) if odd else (k // 2 == j)
    return jnp.where(hit, 1.0, 0.0).astype(F32)


def spread_matrix(rows, cols):
    k = lax.broadcasted_iota(jnp.int32, (rows, cols), 0)
    j = lax.broadcasted_iota(jnp.int32, (rows, cols), 1)
    return jnp.where(k == j // 2, 1.0, 0.0).astype(F32)


def conjugate(rhs, coef_ref, out_ref):
    lane = lax.broadcasted_iota(jnp.int32, (NW, 8, 128), 2)
    low, high = lane < 96, lane >= 32
    sink, ux, uy, uz = (coef_ref[:, k] for k in range(4))

    def y_up(v):
        q = pltpu.roll(v, 96, 2)
        return jnp.where(low, q, pltpu.roll(q, 7, 1))

    def y_down(v):
        q = pltpu.roll(v, 32, 2)
        return jnp.where(high, q, pltpu.roll(q, 1, 1))

    def z_up(v):
        return pltpu.roll(v, 127, 2)

    def z_down(v):
        return pltpu.roll(v, 1, 2)

    def total(v):
        return jnp.sum(jnp.sum(v, axis=0), axis=(0, 1), keepdims=True)[None]

    edge = jnp.zeros((1, 8, 128), F32)
    dx = jnp.concatenate([edge, ux[:-1]], axis=0)
    diag = sink + (ux + dx) + (uy + y_down(uy)) + (uz + z_down(uz))

    def apply(p):
        above = jnp.concatenate([p[1:], edge], axis=0)
        px = ux * p
        below = jnp.concatenate([edge, px[:-1]], axis=0)
        return diag * p - (
            (ux * above + below)
            + (uy * y_up(p) + y_down(uy * p))
            + (uz * z_up(p) + z_down(uz * p))
        )

    def body(_, carry):
        solved, residual, direction, norm_now = carry
        applied = apply(direction)
        step = norm_now / total(direction * applied)
        solved = solved + step * direction
        residual = residual - step * applied
        norm_next = total(residual * residual)
        direction = residual + (norm_next / norm_now) * direction
        return solved, residual, direction, norm_next

    start = (jnp.zeros_like(rhs), rhs, rhs, total(rhs * rhs))
    solved, residual, direction, norm_now = lax.fori_loop(0, COARSE_ITERS - 1, body, start)
    step = norm_now / total(direction * apply(direction))
    out_ref[...] = solved + step * direction


def kernel(
    dens_in, temp_in, aim_in, sink_in, adj_out, sens_out,
    dens, temp, aim, sink, ux0, uy0, uz0, d0, w0, ua, ub, v0, zs, lift0,
    stage, pairs,
    c1, f1, v1, d1, w1, p1, q1, lift1,
    c2, f2, v2, d2, w2, p2, q2, lift2,
    ga, gb, ra, rb, solved3, rows3,
    in_sem, send_sem, recv_sem,
):
    wide, narrow = lax.axis_index("wide"), lax.axis_index("narrow")
    wire = Wire(wide, narrow, send_sem, recv_sem)
    barrier = pltpu.get_barrier_semaphore()
    peers = all_peers()
    for dw, dn in peers:
        pl.semaphore_signal(barrier, inc=1, device_id=wire.peer(dw, dn), device_id_type=MESH)

    own = (pl.ds(4, 8), pl.ds(8, 32))
    loads = []
    for k, (src, dst) in enumerate(
        ((dens_in, dens.at[own]), (sink_in, sink.at[own]), (aim_in, aim.at[own]),
         (temp_in, temp.at[pl.ds(1, 8), pl.ds(8, 32)]))
    ):
        load = pltpu.make_async_copy(src, dst, in_sem.at[k])
        load.start()
        loads.append(load)
    for load in loads:
        load.wait()
    pl.semaphore_wait(barrier, len(peers))

    def halo(ref, own_x, halo_x, width_x, own_y, lead=()):
        copies = []
        for dw, dn in near_peers(1):
            sx, tx = cut(own_x, halo_x, width_x, dw)
            sy, ty = cut(own_y, 8, 8, dn)
            copies.append(wire.send(ref.at[lead + (sx, sy)], ref.at[lead + (tx, ty)], dw, dn))
        return copies

    first = halo(dens, 8, 4, 4, 32) + halo(sink, 8, 4, 3, 32) + halo(aim, 8, 4, 3, 32)
    temps = []
    for dw, dn in ((1, 0), (-1, 0), (0, 1), (0, -1)):
        sx, tx = cut(8, 1, 1, dw)
        sy, ty = cut(32, 8, 8, dn)
        temps.append(wire.send(temp.at[sx, sy], temp.at[tx, ty], dw, dn))

    goal_part = jnp.sum(aim_in[...] * temp_in[...], axis=0)
    goal_part = jnp.sum(goal_part[:, :128] + goal_part[:, 128:], axis=0, keepdims=True)

    row0 = narrow * 32 - 8 + lax.broadcasted_iota(jnp.int32, (48, 256), 0)
    lane0 = lax.broadcasted_iota(jnp.int32, (48, 256), 1)
    hy = jnp.where((row0 == -1) | (row0 == 255), 0.0, 0.5).astype(F32)
    hz = jnp.where(lane0 == 255, 0.0, 0.5).astype(F32)

    def hx(i):
        g = wide * 8 - 4 + i
        return jnp.where((g == -1) | (g == 127), 0.0, 0.5).astype(F32)

    def conduct(i):
        s = dens[i]
        return FLOOR_CONDUCTION + (1.0 - FLOOR_CONDUCTION) * s * s * s

    for copy in first:
        copy.wait_recv()
    wire.flush()

    c_first = conduct(1)
    ux_first = (conduct(0) + c_first) * hx(0)
    ux0[0] = ux_first

    def coefficients(i, carry):
        c, ux_below = carry
        c_next = conduct(i + 1)
        ux = (c + c_next) * hx(i)
        uy = (c + up_y(c)) * hy
        uz = (c + up_z(c)) * hz
        diag = sink[i] + (ux + ux_below) + (uy + down_y(uy)) + (uz + down_z(uz))
        weight = OMEGA / diag
        ux0[i], uy0[i], uz0[i], d0[i], w0[i] = ux, uy, uz, diag, weight
        ua[i] = weight * aim[i]
        return c_next, ux

    lax.fori_loop(1, 15, coefficients, (c_first, ux_first))

    s1, s1_odd = pair_matrix(256, 128, False), pair_matrix(256, 128, True)
    rows = pl.ds(8, 32)
    for k in range(4):
        a, b = 4 + 2 * k, 5 + 2 * k
        stage[pl.ds(32 * k, 32)] = sink[a, rows] + sink[b, rows]
        stage[pl.ds(128 + 32 * k, 32)] = ux0[b, rows]
        stage[pl.ds(256 + 32 * k, 32)] = uy0[a, rows] + uy0[b, rows]
        stage[pl.ds(384 + 32 * k, 32)] = uz0[a, rows] + uz0[b, rows]
    pairs[pl.ds(0, 384)] = dot(stage[pl.ds(0, 384)], s1)
    pairs[pl.ds(384, 128)] = dot(stage[pl.ds(384, 128)], s1_odd)

    def even_odd(base, size):
        return (
            pairs[pl.ds(base, size // 2, stride=2)],
            pairs[pl.ds(base + 1, size // 2, stride=2)],
        )

    own1 = (pl.ds(6, 4), pl.ds(8, 16))
    for k in range(4):
        even, odd = even_odd(128 * k, 128)
        value = (even + odd, 0.5 * (even + odd), 0.5 * odd, 0.5 * (even + odd))[k]
        c1[(k,) + own1] = value.reshape(4, 16, 128)
    coarse1 = halo(c1, 4, 6, 4, 16, (slice(None),))
    for dn in (-1, 0, 1):
        sy, ty = cut(16, 8, 8, dn)
        coarse1.append(wire.send(c1.at[1, pl.ds(9, 1), sy], c1.at[1, pl.ds(1, 1), ty], 2, dn))

    sweep(ua, ub, aim, ux0, uy0, uz0, w0, 2, 14)
    sweep(ub, ua, aim, ux0, uy0, uz0, w0, 3, 13)

    def restrict0(k, carry):
        a = 4 + 2 * k
        r = residual_at(ua, aim, ux0, uy0, uz0, d0, a) + residual_at(
            ua, aim, ux0, uy0, uz0, d0, a + 1
        )
        stage[pl.ds(pl.multiple_of(32 * k, 32), 32)] = r[8:40]
        return carry

    lax.fori_loop(0, 4, restrict0, 0)
    pairs[pl.ds(0, 128)] = dot(stage[pl.ds(0, 128)], s1)
    even, odd = even_odd(0, 128)
    f1[own1] = (even + odd).reshape(4, 16, 128)
    right1 = halo(f1, 4, 6, 4, 16)
    v0[own] = ua[own]
    before0 = halo(v0, 8, 4, 4, 32)

    s2, s2_odd = pair_matrix(128, 128, False), pair_matrix(128, 128, True)
    rows1 = pl.ds(8, 16)
    for k in range(2):
        a, b = 6 + 2 * k, 7 + 2 * k
        stage[pl.ds(16 * k, 16), pl.ds(0, 128)] = c1[0, a, rows1] + c1[0, b, rows1]
        stage[pl.ds(32 + 16 * k, 16), pl.ds(0, 128)] = c1[1, b, rows1]
        stage[pl.ds(64 + 16 * k, 16), pl.ds(0, 128)] = c1[2, a, rows1] + c1[2, b, rows1]
        stage[pl.ds(96 + 16 * k, 16), pl.ds(0, 128)] = c1[3, a, rows1] + c1[3, b, rows1]
    pairs[pl.ds(0, 96)] = dot(stage[pl.ds(0, 96), pl.ds(0, 128)], s2)
    pairs[pl.ds(96, 32)] = dot(stage[pl.ds(96, 32), pl.ds(0, 128)], s2_odd)
    lane2 = lax.broadcasted_iota(jnp.int32, (16, 128), 1)
    own2 = (pl.ds(6, 2), pl.ds(8, 8))
    for k in range(4):
        even, odd = even_odd(32 * k, 32)
        if k == 0:
            value = jnp.where(lane2 < 64, even + odd, 1.0)
        else:
            value = 0.5 * odd if k == 2 else 0.5 * (even + odd)
        c2[(k,) + own2] = value.reshape(2, 8, 128)

    def blocks2(ref, lead=()):
        copies = []
        for dw, dn in near_peers(3):
            dst = ref.at[lead + (pl.ds(6 - 2 * dw, 2), pl.ds(8 - 8 * dn, 8))]
            copies.append(wire.send(ref.at[lead + own2], dst, dw, dn))
        return copies

    coarse2 = blocks2(c2, (slice(None),))

    k3 = lax.broadcasted_iota(jnp.int32, (128, 128), 0)
    j3 = lax.broadcasted_iota(jnp.int32, (128, 128), 1)
    s3 = jnp.where(k3 // 2 == j3 % 32, 1.0, 0.0).astype(F32)
    s3_odd = jnp.where(k3 == 2 * (j3 % 32) + 1, 1.0, 0.0).astype(F32)
    sub8 = lax.broadcasted_iota(jnp.int32, (8, 128), 0)
    lane8 = lax.broadcasted_iota(jnp.int32, (8, 128), 1)
    both_y = sub8 // 2 == lane8 // 32
    odd_y = sub8 == 2 * (lane8 // 32) + 1
    mine = sub8 == narrow

    def as_tile(row):
        return jnp.where(mine, jnp.broadcast_to(row, (8, 128)), 0.0)

    def to_row(values, matrix, mask):
        return jnp.sum(jnp.where(mask, dot(values, matrix), 0.0), axis=0, keepdims=True)

    rows2 = pl.ds(8, 8)
    tiles3 = (
        to_row(c2[0, 6, rows2] + c2[0, 7, rows2], s3, both_y),
        0.5 * to_row(c2[1, 7, rows2], s3, both_y),
        0.5 * to_row(c2[2, 6, rows2] + c2[2, 7, rows2], s3, odd_y),
        0.5 * to_row(c2[3, 6, rows2] + c2[3, 7, rows2], s3_odd, both_y),
        goal_part,
    )
    for k in range(5):
        ga[narrow, k] = as_tile(tiles3[k])
    gather_a = [wire.send(ga.at[narrow], ga.at[narrow], 0, dn) for dn in range(1, NN)]

    for copy in coarse1:
        copy.wait_recv()
    weights(c1.at[0], c1.at[1], c1.at[2], c1.at[3], d1, w1, 2, 14)

    for copy in right1:
        copy.wait_recv()

    level1 = (c1.at[1], c1.at[2], c1.at[3])

    def first1(i, carry):
        p1[i] = w1[i] * f1[i]
        return carry

    lax.fori_loop(3, 13, first1, 0)
    sweep(p1, q1, f1, *level1, w1, 4, 12)
    sweep(q1, p1, f1, *level1, w1, 5, 11)

    for k in range(2):
        a = 6 + 2 * k
        r = residual_at(p1, f1, *level1, d1, a) + residual_at(p1, f1, *level1, d1, a + 1)
        stage[pl.ds(16 * k, 16), pl.ds(0, 128)] = r[8:24]
    pairs[pl.ds(0, 32)] = dot(stage[pl.ds(0, 32), pl.ds(0, 128)], s2)
    even, odd = even_odd(0, 32)
    f2[own2] = (even + odd).reshape(2, 8, 128)
    right2 = blocks2(f2)
    v1[own1] = p1[own1]
    before1 = halo(v1, 4, 6, 4, 16)
    for dw in (-2, 2):
        for dn in (-1, 0, 1):
            sy, ty = cut(16, 8, 8, dn)
            src, dst = (9, 1) if dw > 0 else (6, 14)
            before1.append(
                wire.send(v1.at[pl.ds(src, 1), sy], v1.at[pl.ds(dst, 1), ty], dw, dn)
            )

    for copy in gather_a:
        copy.wait_recv()
    gb[wide] = jnp.sum(ga[...], axis=0)
    gather_b = [wire.send(gb.at[wide], gb.at[wide], dw, 0) for dw in range(1, NW)]

    for copy in coarse2:
        copy.wait_recv()
    weights(c2.at[0], c2.at[1], c2.at[2], c2.at[3], d2, w2, 1, 13)

    for copy in right2:
        copy.wait_recv()
    level2 = (c2.at[1], c2.at[2], c2.at[3])

    def first2(i, carry):
        p2[i] = w2[i] * f2[i]
        return carry

    lax.fori_loop(3, 11, first2, 0)
    sweep(p2, q2, f2, *level2, w2, 4, 10)
    sweep(q2, p2, f2, *level2, w2, 5, 9)
    r = residual_at(p2, f2, *level2, d2, 6) + residual_at(p2, f2, *level2, d2, 7)
    ra[narrow] = as_tile(to_row(r[8:16], s3, both_y))
    right3 = [wire.send(ra.at[narrow], ra.at[narrow], 0, dn) for dn in range(1, NN)]
    v2[own2] = p2[own2]
    before2 = blocks2(v2)

    for copy in right3:
        copy.wait_recv()
    rb[wide] = jnp.sum(ra[...], axis=0)
    right3 = [wire.send(rb.at[wide], rb.at[wide], dw, 0) for dw in range(1, NW)]
    for copy in gather_b:
        copy.wait_recv()
    goal = jnp.sum(jnp.sum(gb[:, 4], axis=0), axis=(0, 1), keepdims=True)
    for copy in right3:
        copy.wait_recv()

    conjugate(rb[...], gb, solved3)

    for a in range(7):
        layer = lax.rem(wide + (a - 3 + NW), NW)
        for b in range(3):
            line = lax.rem(narrow + (b - 1 + NN), NN)
            row = jnp.broadcast_to(solved3[layer, pl.ds(line, 1)], (8, 128))
            rows3[pl.ds(24 * a + 8 * b, 8)] = jnp.where(both_y, row, 0.0)
    e3 = jnp.where((k3 % 32) == j3 // 2, 1.0, 0.0).astype(F32)
    lift2[...] = dot(rows3[...], e3).reshape(7, 24, 128)
    for copy in before2:
        copy.wait_recv()

    def correct2(a, carry):
        p2[2 * a] = v2[2 * a] + lift2[a]
        p2[2 * a + 1] = v2[2 * a + 1] + lift2[a]
        return carry

    lax.fori_loop(0, 7, correct2, 0)
    sweep(p2, q2, f2, *level2, w2, 1, 13)
    sweep(q2, p2, f2, *level2, w2, 2, 12)
    sweep(p2, q2, f2, *level2, w2, 3, 11)

    e2 = spread_matrix(128, 128)
    wide_rows = dot(q2[pl.ds(3, 8)].reshape(192, 128), e2).reshape(8, 24, 128)[:, 4:20]
    for a in range(8):
        lift1[a, pl.ds(0, 16, stride=2)] = wide_rows[a]
        lift1[a, pl.ds(1, 16, stride=2)] = wide_rows[a]
    for copy in before1:
        copy.wait_recv()

    def correct1(i, carry):
        p1[i] = v1[i] + lift1[i // 2]
        return carry

    lax.fori_loop(1, 15, correct1, 0)
    sweep(p1, q1, f1, *level1, w1, 2, 14)
    sweep(q1, p1, f1, *level1, w1, 3, 13)
    sweep(p1, q1, f1, *level1, w1, 4, 12)

    e1 = spread_matrix(128, 256)
    lift = dot(q1[pl.ds(4, 8), pl.ds(0, 32)].reshape(256, 128), e1).reshape(8, 32, 256)
    for copy in before0:
        copy.wait_recv()
    for a in range(8):
        for half in range(2):
            part = lift[a, 4:28, 128 * half : 128 * half + 128]
            lift0[a, half, pl.ds(0, 24, stride=2)] = part
            lift0[a, half, pl.ds(1, 24, stride=2)] = part

    def correct0(i, carry):
        k = i // 2
        ua[i] = v0[i] + jnp.concatenate([lift0[k, 0], lift0[k, 1]], axis=1)
        return carry

    lax.fori_loop(0, 16, correct0, 0)
    sweep(ua, ub, aim, ux0, uy0, uz0, w0, 1, 15)
    sweep(ub, ua, aim, ux0, uy0, uz0, w0, 2, 14)
    sweep(ua, ub, aim, ux0, uy0, uz0, w0, 3, 13)
    adj_out[...] = ub[own]

    for copy in temps:
        copy.wait_recv()
    scale = (-0.5 * 3.0 * (1.0 - FLOOR_CONDUCTION)) * (CELLS / goal)
    my, mz = 2.0 * hy, 2.0 * hz

    def face_x(i):
        return (temp[i - 3] - temp[i - 2]) * (ub[i] - ub[i + 1]) * (2.0 * hx(i))

    def slope(i, below):
        t, a, s = temp[i - 3], ub[i], dens[i]
        above = face_x(i)
        fy = (t - up_y(t)) * (a - up_y(a)) * my
        fz = (t - up_z(t)) * (a - up_z(a)) * mz
        raw = (above + below) + (fy + down_y(fy)) + (fz + down_z(fz))
        zs[i, pl.ds(8, 32)] = (raw * scale * s * s)[8:40]
        return above

    lax.fori_loop(4, 12, slope, face_x(3))

    scaled = halo(zs, 8, 4, 4, 32)
    for copy in scaled:
        copy.wait_recv()
    first_layer = jnp.where(wide == 0, 4, 0)
    last_layer = jnp.where(wide == NW - 1, 11, 15)
    top, bottom = row0 == 255, row0 == 0
    right, left = lane0 == 255, lane0 == 0
    c1_filter = FILTER_OMEGA / (1.0 + 6.0 * STRENGTH)

    def filter_at(src, i):
        z = src[i]
        near = src[jnp.minimum(i + 1, last_layer)] + src[jnp.maximum(i - 1, first_layer)]
        near = near + (jnp.where(top, z, up_y(z)) + jnp.where(bottom, z, down_y(z)))
        near = near + (jnp.where(right, z, up_z(z)) + jnp.where(left, z, down_z(z)))
        return (1.0 - FILTER_OMEGA) * z + c1_filter * (zs[i] + STRENGTH * near)

    def filter_sweep(src, dst, lo, hi):
        def body(i, carry):
            dst[i] = filter_at(src, i)
            return carry

        lax.fori_loop(lo, hi, body, 0)

    filter_sweep(zs, ua, 1, 15)
    filter_sweep(ua, ub, 2, 14)
    filter_sweep(ub, ua, 3, 13)

    def last_filter(i, carry):
        sens_out[i - 4] = filter_at(ua, i)[8:40]
        return carry

    lax.fori_loop(4, 12, last_filter, 0)
    wire.flush()


def local(density, temperature, aim, sink):
    vmem = lambda *shape: pltpu.VMEM(shape, F32)
    level0 = (16, 48, 256)
    level1 = (16, 32, 128)
    level2 = (14, 24, 128)
    scratch = [vmem(*level0), vmem(10, 48, 256)] + [vmem(*level0)] * 11 + [vmem(8, 2, 48, 128)]
    scratch += [vmem(512, 256), vmem(512, 128)]
    scratch += [vmem(4, *level1)] + [vmem(*level1)] * 6 + [vmem(8, 32, 128)]
    scratch += [vmem(4, *level2)] + [vmem(*level2)] * 6 + [vmem(7, 24, 128)]
    scratch += [vmem(NN, 5, 8, 128), vmem(NW, 5, 8, 128), vmem(NN, 8, 128), vmem(NW, 8, 128)]
    scratch += [vmem(NW, 8, 128), vmem(168, 128)]
    scratch += [
        pltpu.SemaphoreType.DMA((4,)),
        pltpu.SemaphoreType.DMA((N_SEMS,)),
        pltpu.SemaphoreType.DMA((N_SEMS,)),
    ]
    block = jax.ShapeDtypeStruct((8, 32, 256), F32)
    whole = pl.BlockSpec(memory_space=pltpu.VMEM)
    return pl.pallas_call(
        kernel,
        out_shape=(block, block),
        in_specs=[whole] * 4,
        out_specs=(whole, whole),
        scratch_shapes=scratch,
        compiler_params=pltpu.CompilerParams(
            collective_id=0, has_side_effects=True, vmem_limit_bytes=48 * 2**20
        ),
    )(density, temperature, aim, sink)


def solution(mesh):
    placed = P("wide", "narrow", None)
    return jax.shard_map(
        local,
        mesh=mesh,
        in_specs=(placed,) * 4,
        out_specs=(placed, placed),
        check_vma=False,
    )
```

```python
import functools
import math

import jax
import jax.numpy as jnp
from jax import lax
from jax.experimental import pallas as pl
from jax.experimental.pallas import tpu as pltpu
from jax.sharding import PartitionSpec as P

COARSE_ITERS = 8
RADIUS = 4
FLOOR_CONDUCTION = 0.001
OMEGA = 0.7
FILTER_OMEGA = 0.8
STRENGTH = (RADIUS / (2.0 * math.sqrt(3.0))) ** 2
MESH = pl.DeviceIdType.MESH
NW, NN = 16, 8
CELLS = 128 * 256 * 256
F32 = jnp.float32
HI = lax.Precision.HIGHEST
N_SEMS = 200
UNROLL = {48: 2, 32: 4}


def near_peers(reach):
    peers = [
        (dw, dn)
        for dw in range(-reach, reach + 1)
        for dn in (-1, 0, 1)
        if (dw, dn) != (0, 0)
    ]
    return sorted(peers, key=lambda p: (p[1] != 0 and p[0] != 0, p[0] == 0, abs(p[0])))


def all_peers():
    peers = [(dw % NW, dn % NN) for dw, dn in near_peers(3)]
    peers += [(0, k) for k in range(1, NN)] + [(k, 0) for k in range(1, NW)]
    return sorted(set(peers))


def layers(lo, hi, body, unroll):
    steps = (hi - lo) // unroll

    def step(k, carry):
        for j in range(unroll):
            body(lo + k * unroll + j)
        return carry

    if steps > 1:
        lax.fori_loop(0, steps, step, 0)
    else:
        step(0, 0) if steps else None
    for i in range(lo + steps * unroll, hi):
        body(i)


class Wire:
    def __init__(self, wide, narrow, send_sem, recv_sem):
        self.wide, self.narrow = wide, narrow
        self.send_sem, self.recv_sem = send_sem, recv_sem
        self.count = 0
        self.unsent = []

    def peer(self, dw, dn):
        return (lax.rem(self.wide + (dw + NW), NW), lax.rem(self.narrow + (dn + NN), NN))

    def send(self, src, dst, dw, dn):
        copy = pltpu.make_async_remote_copy(
            src_ref=src,
            dst_ref=dst,
            send_sem=self.send_sem.at[self.count],
            recv_sem=self.recv_sem.at[self.count],
            device_id=self.peer(dw, dn),
            device_id_type=MESH,
        )
        self.count += 1
        copy.start()
        self.unsent.append(copy)
        return copy

    def flush(self, keep=0):
        done = self.unsent[: len(self.unsent) - keep]
        self.unsent = self.unsent[len(self.unsent) - keep :]
        for copy in done:
            copy.wait_send()


def cut(own, halo, width, shift):
    if shift == 0:
        return pl.ds(halo, own), pl.ds(halo, own)
    if shift > 0:
        return pl.ds(halo + own - width, width), pl.ds(halo - width, width)
    return pl.ds(halo, width), pl.ds(halo + own, width)


def up_y(v):
    return pltpu.roll(v, v.shape[0] - 1, 0)


def down_y(v):
    return pltpu.roll(v, 1, 0)


def up_z(v):
    return pltpu.roll(v, v.shape[1] - 1, 1)


def down_z(v):
    return pltpu.roll(v, 1, 1)


def coupling(u, ux, uy, uz, i):
    centre = u[i]
    fy, fz = uy[i], uz[i]
    return centre, (
        (ux[i] * u[i + 1] + ux[i - 1] * u[i - 1])
        + (fy * up_y(centre) + down_y(fy * centre))
        + (fz * up_z(centre) + down_z(fz * centre))
    )


def sweep(src, dst, rhs, ux, uy, uz, weight, lo, hi):
    def body(i):
        centre, pull = coupling(src, ux, uy, uz, i)
        dst[i] = (1.0 - OMEGA) * centre + weight[i] * (rhs[i] + pull)

    layers(lo, hi, body, UNROLL[src.shape[1]])


def residual_at(src, rhs, ux, uy, uz, diag, i):
    centre, pull = coupling(src, ux, uy, uz, i)
    return rhs[i] + pull - diag[i] * centre


def weights(sink, ux, uy, uz, diag, weight, lo, hi):
    def body(i):
        fy, fz = uy[i], uz[i]
        total = sink[i] + (ux[i] + ux[i - 1]) + (fy + down_y(fy)) + (fz + down_z(fz))
        diag[i] = total
        weight[i] = OMEGA / total

    layers(lo, hi, body, UNROLL[diag.shape[1]])


def next_x(here, above, low):
    return pltpu.roll(jnp.where(low, above, here), 64, 1)


def previous_x(here, below, low):
    return pltpu.roll(jnp.where(low, here, below), 64, 1)


def coupling2(u, ux, uy, uz, t, low):
    centre, above, below = u[t], u[min(t + 1, 6)], max(t - 1, 0)
    fy, fz = uy[t], uz[t]
    return centre, (
        (
            ux[t] * next_x(centre, above, low)
            + previous_x(ux[t] * centre, ux[below] * u[below], low)
        )
        + (fy * up_y(centre) + down_y(fy * centre))
        + (fz * up_z(centre) + down_z(fz * centre))
    )


def sweep2(src, dst, rhs, ux, uy, uz, weight, low, lo, hi):
    for t in range(lo, hi):
        centre, pull = coupling2(src, ux, uy, uz, t, low)
        dst[t] = (1.0 - OMEGA) * centre + weight[t] * (rhs[t] + pull)


def dot(a, b):
    return jnp.dot(a, b, precision=HI, preferred_element_type=F32)


def pair_matrix(rows, cols, odd):
    k = lax.broadcasted_iota(jnp.int32, (rows, cols), 0)
    j = lax.broadcasted_iota(jnp.int32, (rows, cols), 1)
    hit = (k == 2 * j + 1) if odd else (k // 2 == j)
    return jnp.where(hit, 1.0, 0.0).astype(F32)


def spread_matrix(rows, cols):
    k = lax.broadcasted_iota(jnp.int32, (rows, cols), 0)
    j = lax.broadcasted_iota(jnp.int32, (rows, cols), 1)
    return jnp.where(k == j // 2, 1.0, 0.0).astype(F32)


def conjugate(rhs, coef_ref, out_ref):
    lane = lax.broadcasted_iota(jnp.int32, (NW, 8, 128), 2)
    low, high = lane < 96, lane >= 32
    sink, ux, uy, uz = (coef_ref[:, k] for k in range(4))

    def y_up(v):
        q = pltpu.roll(v, 96, 2)
        return jnp.where(low, q, pltpu.roll(q, 7, 1))

    def y_down(v):
        q = pltpu.roll(v, 32, 2)
        return jnp.where(high, q, pltpu.roll(q, 1, 1))

    def z_up(v):
        return pltpu.roll(v, 127, 2)

    def z_down(v):
        return pltpu.roll(v, 1, 2)

    def total(v):
        return jnp.sum(jnp.sum(v, axis=0), axis=(0, 1), keepdims=True)[None]

    edge = jnp.zeros((1, 8, 128), F32)
    dx = jnp.concatenate([edge, ux[:-1]], axis=0)
    diag = sink + (ux + dx) + (uy + y_down(uy)) + (uz + z_down(uz))

    def apply(p):
        above = jnp.concatenate([p[1:], edge], axis=0)
        px = ux * p
        below = jnp.concatenate([edge, px[:-1]], axis=0)
        return diag * p - (
            (ux * above + below)
            + (uy * y_up(p) + y_down(uy * p))
            + (uz * z_up(p) + z_down(uz * p))
        )

    def body(_, carry):
        solved, residual, direction, norm_now = carry
        applied = apply(direction)
        step = norm_now / total(direction * applied)
        solved = solved + step * direction
        residual = residual - step * applied
        norm_next = total(residual * residual)
        direction = residual + (norm_next / norm_now) * direction
        return solved, residual, direction, norm_next

    start = (jnp.zeros_like(rhs), rhs, rhs, total(rhs * rhs))
    solved, residual, direction, norm_now = lax.fori_loop(0, COARSE_ITERS - 1, body, start)
    step = norm_now / total(direction * apply(direction))
    out_ref[...] = solved + step * direction


def kernel(
    dens_in, temp_in, aim_in, sink_in, adj_out, sens_out,
    dens, temp, aim, sink, ux0, uy0, uz0, d0, w0, ua, ub, v0, zs, lift0,
    stage, pairs,
    c1, f1, v1, d1, w1, p1, q1, lift1,
    c2, f2, v2, d2, w2, p2, q2, lift2,
    ga, gb, ra, rb, solved3, rows3,
    in_sem, send_sem, recv_sem,
):
    wide, narrow = lax.axis_index("wide"), lax.axis_index("narrow")
    wire = Wire(wide, narrow, send_sem, recv_sem)
    barrier = pltpu.get_barrier_semaphore()
    peers = all_peers()
    for dw, dn in peers:
        pl.semaphore_signal(barrier, inc=1, device_id=wire.peer(dw, dn), device_id_type=MESH)

    own = (pl.ds(4, 8), pl.ds(8, 32))
    loads = []
    for k, (src, dst) in enumerate(
        ((dens_in, dens.at[own]), (sink_in, sink.at[own]), (aim_in, aim.at[own]),
         (temp_in, temp.at[pl.ds(1, 8), pl.ds(8, 32)]))
    ):
        load = pltpu.make_async_copy(src, dst, in_sem.at[k])
        load.start()
        loads.append(load)
    for load in loads:
        load.wait()
    pl.semaphore_wait(barrier, len(peers))

    def halo(ref, own_x, halo_x, width_x, own_y, lead=(), corner=0):
        copies = []
        for dw, dn in near_peers(1):
            sx, tx = cut(own_x, halo_x, corner if corner and dn else width_x, dw)
            sy, ty = cut(own_y, 8, 8, dn)
            copies.append(wire.send(ref.at[lead + (sx, sy)], ref.at[lead + (tx, ty)], dw, dn))
        return copies

    first = halo(dens, 8, 4, 4, 32, corner=3)
    second = halo(sink, 8, 4, 3, 32, corner=2) + halo(aim, 8, 4, 3, 32, corner=2)
    temps = []
    for dw, dn in ((1, 0), (-1, 0), (0, 1), (0, -1)):
        sx, tx = cut(8, 1, 1, dw)
        sy, ty = cut(32, 8, 8, dn)
        temps.append(wire.send(temp.at[sx, sy], temp.at[tx, ty], dw, dn))

    goal_part = jnp.sum(aim[own] * temp[pl.ds(1, 8), pl.ds(8, 32)], axis=0)
    goal_part = jnp.sum(goal_part[:, :128] + goal_part[:, 128:], axis=0, keepdims=True)

    row0 = narrow * 32 - 8 + lax.broadcasted_iota(jnp.int32, (48, 256), 0)
    lane0 = lax.broadcasted_iota(jnp.int32, (48, 256), 1)
    hy = jnp.where((row0 == -1) | (row0 == 255), 0.0, 0.5).astype(F32)
    hz = jnp.where(lane0 == 255, 0.0, 0.5).astype(F32)

    def hx(i):
        g = wide * 8 - 4 + i
        return jnp.where((g == -1) | (g == 127), 0.0, 0.5).astype(F32)

    def conduct(i):
        s = dens[i]
        return FLOOR_CONDUCTION + (1.0 - FLOOR_CONDUCTION) * s * s * s

    s1, s1_odd = pair_matrix(256, 128, False), pair_matrix(256, 128, True)
    for copy in first:
        copy.wait_recv()

    ux0[0] = (conduct(0) + conduct(1)) * hx(0)

    def faces(i):
        c = conduct(i)
        ux0[i] = (c + conduct(i + 1)) * hx(i)
        uy0[i] = (c + up_y(c)) * hy
        uz0[i] = (c + up_z(c)) * hz

    layers(1, 15, faces, 2)

    rows = pl.ds(8, 32)
    for k in range(4):
        a, b = 4 + 2 * k, 5 + 2 * k
        stage[pl.ds(32 * k, 32)] = sink[a, rows] + sink[b, rows]
        stage[pl.ds(128 + 32 * k, 32)] = ux0[b, rows]
        stage[pl.ds(256 + 32 * k, 32)] = uy0[a, rows] + uy0[b, rows]
        stage[pl.ds(384 + 32 * k, 32)] = uz0[a, rows] + uz0[b, rows]
    pairs[pl.ds(0, 384)] = dot(stage[pl.ds(0, 384)], s1)
    pairs[pl.ds(384, 128)] = dot(stage[pl.ds(384, 128)], s1_odd)

    def even_odd(base, size):
        return (
            pairs[pl.ds(base, size // 2, stride=2)],
            pairs[pl.ds(base + 1, size // 2, stride=2)],
        )

    own1 = (pl.ds(6, 4), pl.ds(8, 16))
    for k in range(4):
        even, odd = even_odd(128 * k, 128)
        value = (even + odd, 0.5 * (even + odd), 0.5 * odd, 0.5 * (even + odd))[k]
        c1[(k,) + own1] = value.reshape(4, 16, 128)
    coarse1 = halo(c1, 4, 6, 4, 16, (slice(None),))
    far = c1.at[1, pl.ds(9, 1), pl.ds(8, 16)], c1.at[1, pl.ds(1, 1), pl.ds(8, 16)]
    coarse1.append(wire.send(*far, 2, 0))

    for copy in second:
        copy.wait_recv()
    weights(sink, ux0, uy0, uz0, d0, w0, 1, 15)

    def first0(i):
        ua[i] = w0[i] * aim[i]

    layers(1, 15, first0, 2)
    sweep(ua, ub, aim, ux0, uy0, uz0, w0, 2, 14)
    sweep(ub, ua, aim, ux0, uy0, uz0, w0, 3, 13)

    def restrict0(k, carry):
        a = 4 + 2 * k
        r = residual_at(ua, aim, ux0, uy0, uz0, d0, a) + residual_at(
            ua, aim, ux0, uy0, uz0, d0, a + 1
        )
        stage[pl.ds(pl.multiple_of(32 * k, 32), 32)] = r[8:40]
        return carry

    lax.fori_loop(0, 4, restrict0, 0)
    pairs[pl.ds(0, 128)] = dot(stage[pl.ds(0, 128)], s1)
    even, odd = even_odd(0, 128)
    f1[own1] = (even + odd).reshape(4, 16, 128)
    right1 = halo(f1, 4, 6, 4, 16, corner=3)
    v0[own] = ua[own]
    before0 = halo(v0, 8, 4, 4, 32, corner=3)

    rows1, rows2 = pl.ds(8, 16), pl.ds(8, 8)
    for k in range(2):
        a, b = 6 + 2 * k, 7 + 2 * k
        half = pl.ds(128 * k, 128)
        stage[pl.ds(0, 16), half] = c1[0, a, rows1] + c1[0, b, rows1]
        stage[pl.ds(16, 16), half] = c1[1, b, rows1]
        stage[pl.ds(32, 16), half] = c1[2, a, rows1] + c1[2, b, rows1]
        stage[pl.ds(48, 16), half] = c1[3, a, rows1] + c1[3, b, rows1]
    pairs[pl.ds(0, 48)] = dot(stage[pl.ds(0, 48)], s1)
    pairs[pl.ds(48, 16)] = dot(stage[pl.ds(48, 16)], s1_odd)
    for k in range(4):
        even, odd = even_odd(16 * k, 16)
        value = (even + odd, 0.5 * (even + odd), 0.5 * odd, 0.5 * (even + odd))[k]
        c2[k, 3, rows2] = value

    def blocks2(ref, lead=()):
        copies = []
        for dw, dn in near_peers(3):
            dst = ref.at[lead + (3 - dw, pl.ds(8 - 8 * dn, 8))]
            copies.append(wire.send(ref.at[lead + (3, rows2)], dst, dw, dn))
        return copies

    coarse2 = blocks2(c2, (slice(None),))

    k3 = lax.broadcasted_iota(jnp.int32, (128, 128), 0)
    j3 = lax.broadcasted_iota(jnp.int32, (128, 128), 1)
    pair3 = (k3 % 64) // 2 == j3 % 32
    s3 = jnp.where(pair3, 1.0, 0.0).astype(F32)
    s3_upper = jnp.where(pair3 & (k3 >= 64), 1.0, 0.0).astype(F32)
    s3_odd = jnp.where(k3 % 64 == 2 * (j3 % 32) + 1, 1.0, 0.0).astype(F32)
    sub8 = lax.broadcasted_iota(jnp.int32, (8, 128), 0)
    lane8 = lax.broadcasted_iota(jnp.int32, (8, 128), 1)
    both_y = sub8 // 2 == lane8 // 32
    odd_y = sub8 == 2 * (lane8 // 32) + 1
    mine = sub8 == narrow

    def as_tile(row):
        return jnp.where(mine, jnp.broadcast_to(row, (8, 128)), 0.0)

    def to_row(values, matrix, mask):
        return jnp.sum(jnp.where(mask, dot(values, matrix), 0.0), axis=0, keepdims=True)

    tiles3 = (
        to_row(c2[0, 3, rows2], s3, both_y),
        0.5 * to_row(c2[1, 3, rows2], s3_upper, both_y),
        0.5 * to_row(c2[2, 3, rows2], s3, odd_y),
        0.5 * to_row(c2[3, 3, rows2], s3_odd, both_y),
        goal_part,
    )
    for k in range(5):
        ga[narrow, k] = as_tile(tiles3[k])
    gather_a = [wire.send(ga.at[narrow], ga.at[narrow], 0, dn) for dn in range(1, NN)]

    for copy in coarse1:
        copy.wait_recv()
    weights(c1.at[0], c1.at[1], c1.at[2], c1.at[3], d1, w1, 2, 14)

    for copy in right1:
        copy.wait_recv()

    level1 = (c1.at[1], c1.at[2], c1.at[3])

    def first1(i):
        p1[i] = w1[i] * f1[i]

    layers(3, 13, first1, 5)
    sweep(p1, q1, f1, *level1, w1, 4, 12)
    sweep(q1, p1, f1, *level1, w1, 5, 11)

    for k in range(2):
        a = 6 + 2 * k
        r = residual_at(p1, f1, *level1, d1, a) + residual_at(p1, f1, *level1, d1, a + 1)
        stage[pl.ds(0, 16), pl.ds(128 * k, 128)] = r[8:24]
    pairs[pl.ds(0, 16)] = dot(stage[pl.ds(0, 16)], s1)
    even, odd = even_odd(0, 16)
    f2[3, rows2] = even + odd
    right2 = blocks2(f2)
    v1[own1] = p1[own1]
    before1 = halo(v1, 4, 6, 4, 16)
    for dw, src, dst in ((2, 9, 1), (-2, 6, 14)):
        before1.append(
            wire.send(v1.at[pl.ds(src, 1), rows1], v1.at[pl.ds(dst, 1), rows1], dw, 0)
        )

    for copy in gather_a:
        copy.wait_recv()
    gb[wide] = jnp.sum(ga[...], axis=0)
    gather_b = [wire.send(gb.at[wide], gb.at[wide], dw, 0) for dw in range(1, NW)]

    for copy in coarse2:
        copy.wait_recv()
    low2 = lax.broadcasted_iota(jnp.int32, (24, 128), 1) < 64
    for t in range(7):
        ux, uy, uz = c2[1, t], c2[2, t], c2[3, t]
        ux = ux + previous_x(ux, c2[1, max(t - 1, 0)], low2)
        d2[t] = c2[0, t] + ux + (uy + down_y(uy)) + (uz + down_z(uz))
        w2[t] = OMEGA / d2[t]

    for copy in right2:
        copy.wait_recv()
    level2 = (c2.at[1], c2.at[2], c2.at[3])

    for t in range(1, 6):
        p2[t] = w2[t] * f2[t]
    sweep2(p2, q2, f2, *level2, w2, low2, 2, 5)
    sweep2(q2, p2, f2, *level2, w2, low2, 2, 5)
    centre, pull = coupling2(p2, *level2, 3, low2)
    r = f2[3] + pull - d2[3] * centre
    ra[narrow] = as_tile(to_row(r[8:16], s3, both_y))
    right3 = [wire.send(ra.at[narrow], ra.at[narrow], 0, dn) for dn in range(1, NN)]
    v2[3, rows2] = p2[3, rows2]
    before2 = blocks2(v2)

    for copy in right3:
        copy.wait_recv()
    rb[wide] = jnp.sum(ra[...], axis=0)
    right3 = [wire.send(rb.at[wide], rb.at[wide], dw, 0) for dw in range(1, NW)]
    for copy in gather_b:
        copy.wait_recv()
    goal = jnp.sum(jnp.sum(gb[:, 4], axis=0), axis=(0, 1), keepdims=True)
    for copy in right3:
        copy.wait_recv()

    conjugate(rb[...], gb, solved3)

    for a in range(7):
        layer = lax.rem(wide + (a - 3 + NW), NW)
        for b in range(3):
            line = lax.rem(narrow + (b - 1 + NN), NN)
            row = jnp.broadcast_to(solved3[layer, pl.ds(line, 1)], (8, 128))
            rows3[pl.ds(24 * a + 8 * b, 8)] = jnp.where(both_y, row, 0.0)
    e3 = jnp.where(k3 % 32 == (j3 % 64) // 2, 1.0, 0.0).astype(F32)
    lift2[...] = dot(rows3[...], e3).reshape(7, 24, 128)
    for copy in before2:
        copy.wait_recv()

    for t in range(7):
        p2[t] = v2[t] + lift2[t]
    sweep2(p2, q2, f2, *level2, w2, low2, 0, 7)
    sweep2(q2, p2, f2, *level2, w2, low2, 1, 6)
    sweep2(p2, q2, f2, *level2, w2, low2, 1, 6)

    e1 = spread_matrix(128, 256)
    lift = dot(q2[pl.ds(1, 5)].reshape(120, 128), e1).reshape(5, 24, 256)
    for t in range(5):
        for half in range(2):
            part = lift[t, 4:20, 128 * half : 128 * half + 128]
            lift1[2 * t + half, pl.ds(0, 16, stride=2)] = part
            lift1[2 * t + half, pl.ds(1, 16, stride=2)] = part
    for copy in before1:
        copy.wait_recv()

    for i in range(1, 15):
        p1[i] = v1[i] + lift1[1 + i // 2]
    sweep(p1, q1, f1, *level1, w1, 2, 14)
    sweep(q1, p1, f1, *level1, w1, 3, 13)
    sweep(p1, q1, f1, *level1, w1, 4, 12)

    lift = dot(q1[pl.ds(4, 8), pl.ds(0, 32)].reshape(256, 128), e1).reshape(8, 32, 256)
    for copy in before0:
        copy.wait_recv()
    for a in range(8):
        for half in range(2):
            part = lift[a, 4:28, 128 * half : 128 * half + 128]
            lift0[a, half, pl.ds(0, 24, stride=2)] = part
            lift0[a, half, pl.ds(1, 24, stride=2)] = part

    def correct0(k):
        both = jnp.concatenate([lift0[k, 0], lift0[k, 1]], axis=1)
        ua[2 * k] = v0[2 * k] + both
        ua[2 * k + 1] = v0[2 * k + 1] + both

    layers(0, 8, correct0, 1)
    sweep(ua, ub, aim, ux0, uy0, uz0, w0, 1, 15)
    sweep(ub, ua, aim, ux0, uy0, uz0, w0, 2, 14)
    sweep(ua, ub, aim, ux0, uy0, uz0, w0, 3, 13)
    adj_out[...] = ub[own]

    for copy in temps:
        copy.wait_recv()
    scale = (-0.5 * 3.0 * (1.0 - FLOOR_CONDUCTION)) * (CELLS / goal)
    my, mz = 2.0 * hy, 2.0 * hz

    def face_x(i):
        return (temp[i - 3] - temp[i - 2]) * (ub[i] - ub[i + 1]) * (2.0 * hx(i))

    def slope(i, below):
        t, a, s = temp[i - 3], ub[i], dens[i]
        above = face_x(i)
        fy = (t - up_y(t)) * (a - up_y(a)) * my
        fz = (t - up_z(t)) * (a - up_z(a)) * mz
        raw = (above + below) + (fy + down_y(fy)) + (fz + down_z(fz))
        zs[i, pl.ds(8, 32)] = (raw * scale * s * s)[8:40]
        return above

    lax.fori_loop(4, 12, slope, face_x(3))

    scaled = halo(zs, 8, 4, 4, 32, corner=3)
    for copy in scaled:
        copy.wait_recv()
    first_layer = jnp.where(wide == 0, 4, 0)
    last_layer = jnp.where(wide == NW - 1, 11, 15)
    top, bottom = row0 == 255, row0 == 0
    right, left = lane0 == 255, lane0 == 0
    c1_filter = FILTER_OMEGA / (1.0 + 6.0 * STRENGTH)

    def filter_at(src, i):
        z = src[i]
        near = src[jnp.minimum(i + 1, last_layer)] + src[jnp.maximum(i - 1, first_layer)]
        near = near + (jnp.where(top, z, up_y(z)) + jnp.where(bottom, z, down_y(z)))
        near = near + (jnp.where(right, z, up_z(z)) + jnp.where(left, z, down_z(z)))
        return (1.0 - FILTER_OMEGA) * z + c1_filter * (zs[i] + STRENGTH * near)

    def filter_sweep(src, dst, lo, hi):
        def body(i):
            dst[i] = filter_at(src, i)

        layers(lo, hi, body, 2)

    filter_sweep(zs, ua, 1, 15)
    filter_sweep(ua, ub, 2, 14)
    filter_sweep(ub, ua, 3, 13)

    def last_filter(i):
        sens_out[i - 4] = filter_at(ua, i)[8:40]

    layers(4, 12, last_filter, 2)
    wire.flush()


def local(density, temperature, aim, sink):
    vmem = lambda *shape: pltpu.VMEM(shape, F32)
    level0 = (16, 48, 256)
    level1 = (16, 32, 128)
    level2 = (7, 24, 128)
    scratch = [vmem(*level0), vmem(10, 48, 256)] + [vmem(*level0)] * 11 + [vmem(8, 2, 48, 128)]
    scratch += [vmem(512, 256), vmem(512, 128)]
    scratch += [vmem(4, *level1)] + [vmem(*level1)] * 6 + [vmem(10, 32, 128)]
    scratch += [vmem(4, *level2)] + [vmem(*level2)] * 6 + [vmem(7, 24, 128)]
    scratch += [vmem(NN, 5, 8, 128), vmem(NW, 5, 8, 128), vmem(NN, 8, 128), vmem(NW, 8, 128)]
    scratch += [vmem(NW, 8, 128), vmem(168, 128)]
    scratch += [
        pltpu.SemaphoreType.DMA((4,)),
        pltpu.SemaphoreType.DMA((N_SEMS,)),
        pltpu.SemaphoreType.DMA((N_SEMS,)),
    ]
    block = jax.ShapeDtypeStruct((8, 32, 256), F32)
    whole = pl.BlockSpec(memory_space=pltpu.VMEM)
    return pl.pallas_call(
        kernel,
        out_shape=(block, block),
        in_specs=[pl.BlockSpec(memory_space=pl.ANY)] * 4,
        out_specs=(whole, whole),
        scratch_shapes=scratch,
        compiler_params=pltpu.CompilerParams(
            collective_id=0, has_side_effects=True, vmem_limit_bytes=48 * 2**20
        ),
    )(density, temperature, aim, sink)


def solution(mesh):
    placed = P("wide", "narrow", None)
    return jax.shard_map(
        local,
        mesh=mesh,
        in_specs=(placed,) * 4,
        out_specs=(placed, placed),
        check_vma=False,
    )
```

```python
import functools
import math

import jax
import jax.numpy as jnp
from jax import lax
from jax.experimental import pallas as pl
from jax.experimental.pallas import tpu as pltpu
from jax.sharding import PartitionSpec as P

COARSE_ITERS = 8
RADIUS = 4
FLOOR_CONDUCTION = 0.001
OMEGA = 0.7
FILTER_OMEGA = 0.8
STRENGTH = (RADIUS / (2.0 * math.sqrt(3.0))) ** 2
MESH = pl.DeviceIdType.MESH
NW, NN = 16, 8
CELLS = 128 * 256 * 256
F32 = jnp.float32
BF16 = jnp.bfloat16
N_SEMS = 200
UNROLL = {48: 2, 32: 4}


def near_peers(reach):
    peers = [
        (dw, dn)
        for dw in range(-reach, reach + 1)
        for dn in (-1, 0, 1)
        if (dw, dn) != (0, 0)
    ]
    return sorted(peers, key=lambda p: (p[1] != 0 and p[0] != 0, p[0] == 0, abs(p[0])))


def greeted():
    peers = [(dw % NW, dn % NN) for dw, dn in near_peers(3)]
    peers += [(0, k) for k in range(1, NN)] + [(k, 0) for k in range(1, NW)]
    return sorted(set(peers))


def layers(lo, hi, body, unroll):
    steps = (hi - lo) // unroll

    def step(k, carry):
        for j in range(unroll):
            body(lo + k * unroll + j)
        return carry

    if steps > 1:
        lax.fori_loop(0, steps, step, 0)
    else:
        step(0, 0) if steps else None
    for i in range(lo + steps * unroll, hi):
        body(i)


class Wire:
    def __init__(self, wide, narrow, send_sem, recv_sem):
        self.wide, self.narrow = wide, narrow
        self.send_sem, self.recv_sem = send_sem, recv_sem
        self.count = 0
        self.unsent = []

    def peer(self, dw, dn):
        return (lax.rem(self.wide + (dw + NW), NW), lax.rem(self.narrow + (dn + NN), NN))

    def send(self, src, dst, dw, dn):
        copy = pltpu.make_async_remote_copy(
            src_ref=src,
            dst_ref=dst,
            send_sem=self.send_sem.at[self.count],
            recv_sem=self.recv_sem.at[self.count],
            device_id=self.peer(dw, dn),
            device_id_type=MESH,
        )
        self.count += 1
        copy.start()
        self.unsent.append(copy)
        return copy

    def flush(self, keep=0):
        done = self.unsent[: len(self.unsent) - keep]
        self.unsent = self.unsent[len(self.unsent) - keep :]
        for copy in done:
            copy.wait_send()


def cut(own, halo, width, shift):
    if shift == 0:
        return pl.ds(halo, own), pl.ds(halo, own)
    if shift > 0:
        return pl.ds(halo + own - width, width), pl.ds(halo - width, width)
    return pl.ds(halo, width), pl.ds(halo + own, width)


def up_y(v):
    return pltpu.roll(v, v.shape[0] - 1, 0)


def down_y(v):
    return pltpu.roll(v, 1, 0)


def up_z(v):
    return pltpu.roll(v, v.shape[1] - 1, 1)


def down_z(v):
    return pltpu.roll(v, 1, 1)


def coupling(u, ux, uy, uz, i):
    centre = u[i]
    fy, fz = uy[i], uz[i]
    return centre, (
        (ux[i] * u[i + 1] + ux[i - 1] * u[i - 1])
        + (fy * up_y(centre) + down_y(fy * centre))
        + (fz * up_z(centre) + down_z(fz * centre))
    )


def sweep(src, dst, rhs, ux, uy, uz, weight, lo, hi):
    def body(i):
        centre, pull = coupling(src, ux, uy, uz, i)
        dst[i] = (1.0 - OMEGA) * centre + weight[i] * (rhs[i] + pull)

    layers(lo, hi, body, UNROLL[src.shape[1]])


def residual_at(src, rhs, ux, uy, uz, diag, i):
    centre, pull = coupling(src, ux, uy, uz, i)
    return rhs[i] + pull - diag[i] * centre


def weights(sink, ux, uy, uz, diag, weight, lo, hi):
    def body(i):
        fy, fz = uy[i], uz[i]
        total = sink[i] + (ux[i] + ux[i - 1]) + (fy + down_y(fy)) + (fz + down_z(fz))
        diag[i] = total
        weight[i] = OMEGA / total

    layers(lo, hi, body, UNROLL[diag.shape[1]])


def next_x(here, above, low):
    return pltpu.roll(jnp.where(low, above, here), 64, 1)


def previous_x(here, below, low):
    return pltpu.roll(jnp.where(low, here, below), 64, 1)


def coupling2(u, ux, uy, uz, t, low):
    centre, above, below = u[t], u[min(t + 1, 6)], max(t - 1, 0)
    fy, fz = uy[t], uz[t]
    return centre, (
        (
            ux[t] * next_x(centre, above, low)
            + previous_x(ux[t] * centre, ux[below] * u[below], low)
        )
        + (fy * up_y(centre) + down_y(fy * centre))
        + (fz * up_z(centre) + down_z(fz * centre))
    )


def sweep2(src, dst, rhs, ux, uy, uz, weight, low, lo, hi):
    for t in range(lo, hi):
        centre, pull = coupling2(src, ux, uy, uz, t, low)
        dst[t] = (1.0 - OMEGA) * centre + weight[t] * (rhs[t] + pull)


def dot(a, b):
    b = b.astype(BF16)
    high = a.astype(BF16)
    rest = a - high.astype(F32)
    middle = rest.astype(BF16)
    low = (rest - middle.astype(F32)).astype(BF16)
    products = [jnp.dot(part, b, preferred_element_type=F32) for part in (low, middle, high)]
    return products[0] + products[1] + products[2]


def pair_matrix(rows, cols, odd):
    k = lax.broadcasted_iota(jnp.int32, (rows, cols), 0)
    j = lax.broadcasted_iota(jnp.int32, (rows, cols), 1)
    hit = (k == 2 * j + 1) if odd else (k // 2 == j)
    return jnp.where(hit, 1.0, 0.0).astype(F32)


def spread_matrix(rows, cols):
    k = lax.broadcasted_iota(jnp.int32, (rows, cols), 0)
    j = lax.broadcasted_iota(jnp.int32, (rows, cols), 1)
    return jnp.where(k == j // 2, 1.0, 0.0).astype(F32)


def conjugate(rhs, coef_ref, out_ref):
    lane = lax.broadcasted_iota(jnp.int32, (NW, 8, 128), 2)
    low, high = lane < 96, lane >= 32
    sink, ux, uy, uz = (coef_ref[:, k] for k in range(4))

    def y_up(v):
        q = pltpu.roll(v, 96, 2)
        return jnp.where(low, q, pltpu.roll(q, 7, 1))

    def y_down(v):
        q = pltpu.roll(v, 32, 2)
        return jnp.where(high, q, pltpu.roll(q, 1, 1))

    def z_up(v):
        return pltpu.roll(v, 127, 2)

    def z_down(v):
        return pltpu.roll(v, 1, 2)

    def total(v):
        return jnp.sum(jnp.sum(v, axis=0), axis=(0, 1), keepdims=True)[None]

    edge = jnp.zeros((1, 8, 128), F32)
    dx = jnp.concatenate([edge, ux[:-1]], axis=0)
    diag = sink + (ux + dx) + (uy + y_down(uy)) + (uz + z_down(uz))

    def apply(p):
        above = jnp.concatenate([p[1:], edge], axis=0)
        px = ux * p
        below = jnp.concatenate([edge, px[:-1]], axis=0)
        return diag * p - (
            (ux * above + below)
            + (uy * y_up(p) + y_down(uy * p))
            + (uz * z_up(p) + z_down(uz * p))
        )

    def body(_, carry):
        solved, residual, direction, norm_now = carry
        applied = apply(direction)
        step = norm_now / total(direction * applied)
        solved = solved + step * direction
        residual = residual - step * applied
        norm_next = total(residual * residual)
        direction = residual + (norm_next / norm_now) * direction
        return solved, residual, direction, norm_next

    start = (jnp.zeros_like(rhs), rhs, rhs, total(rhs * rhs))
    solved, residual, direction, norm_now = lax.fori_loop(0, COARSE_ITERS - 1, body, start)
    step = norm_now / total(direction * apply(direction))
    out_ref[...] = solved + step * direction


def kernel(
    dens_in, temp_in, aim_in, sink_in, adj_out, sens_out,
    dens, temp, aim, sink, ux0, uy0, uz0, d0, w0, ua, ub, v0, zs, lift0,
    stage, pairs,
    c1, f1, v1, d1, w1, p1, q1, lift1,
    c2, f2, v2, d2, w2, p2, q2, lift2,
    ga, gb, ra, rb, solved3, rows3,
    in_sem, send_sem, recv_sem,
):
    wide, narrow = lax.axis_index("wide"), lax.axis_index("narrow")
    wire = Wire(wide, narrow, send_sem, recv_sem)
    barrier = pltpu.get_barrier_semaphore()
    peers = greeted()
    for dw, dn in peers:
        pl.semaphore_signal(barrier, inc=1, device_id=wire.peer(dw, dn), device_id_type=MESH)

    own = (pl.ds(4, 8), pl.ds(8, 32))
    loads = []
    for k, (src, dst) in enumerate(
        ((dens_in, dens.at[own]), (sink_in, sink.at[own]), (aim_in, aim.at[own]),
         (temp_in, temp.at[pl.ds(1, 8), pl.ds(8, 32)]))
    ):
        load = pltpu.make_async_copy(src, dst, in_sem.at[k])
        load.start()
        loads.append(load)
    for load in loads:
        load.wait()
    pl.semaphore_wait(barrier, len(peers))

    def halo(ref, own_x, halo_x, width_x, own_y, lead=(), corner=0):
        copies = []
        for dw, dn in near_peers(1):
            sx, tx = cut(own_x, halo_x, corner if corner and dn else width_x, dw)
            sy, ty = cut(own_y, 8, 8, dn)
            copies.append(wire.send(ref.at[lead + (sx, sy)], ref.at[lead + (tx, ty)], dw, dn))
        return copies

    first = halo(dens, 8, 4, 4, 32, corner=3)
    second = halo(sink, 8, 4, 3, 32, corner=2)
    third = halo(aim, 8, 4, 3, 32, corner=2)
    temps = []
    for dw, dn in ((1, 0), (-1, 0), (0, 1), (0, -1)):
        sx, tx = cut(8, 1, 1, dw)
        sy, ty = cut(32, 8, 8, dn)
        temps.append(wire.send(temp.at[sx, sy], temp.at[tx, ty], dw, dn))

    goal_part = jnp.sum(aim[own] * temp[pl.ds(1, 8), pl.ds(8, 32)], axis=0)
    goal_part = jnp.sum(goal_part[:, :128] + goal_part[:, 128:], axis=0, keepdims=True)

    row0 = narrow * 32 - 8 + lax.broadcasted_iota(jnp.int32, (48, 256), 0)
    lane0 = lax.broadcasted_iota(jnp.int32, (48, 256), 1)
    hy = jnp.where((row0 == -1) | (row0 == 255), 0.0, 0.5).astype(F32)
    hz = jnp.where(lane0 == 255, 0.0, 0.5).astype(F32)

    def hx(i):
        g = wide * 8 - 4 + i
        return jnp.where((g == -1) | (g == 127), 0.0, 0.5).astype(F32)

    def conduct(i):
        s = dens[i]
        return FLOOR_CONDUCTION + (1.0 - FLOOR_CONDUCTION) * s * s * s

    s1, s1_odd = pair_matrix(256, 128, False), pair_matrix(256, 128, True)
    for copy in first:
        copy.wait_recv()

    ux0[0] = (conduct(0) + conduct(1)) * hx(0)

    def faces(i):
        c = conduct(i)
        ux0[i] = (c + conduct(i + 1)) * hx(i)
        uy0[i] = (c + up_y(c)) * hy
        uz0[i] = (c + up_z(c)) * hz

    layers(1, 15, faces, 2)

    rows = pl.ds(8, 32)
    for k in range(4):
        a, b = 4 + 2 * k, 5 + 2 * k
        stage[pl.ds(32 * k, 32)] = sink[a, rows] + sink[b, rows]
        stage[pl.ds(128 + 32 * k, 32)] = ux0[b, rows]
        stage[pl.ds(256 + 32 * k, 32)] = uy0[a, rows] + uy0[b, rows]
        stage[pl.ds(384 + 32 * k, 32)] = uz0[a, rows] + uz0[b, rows]
    pairs[pl.ds(0, 384)] = dot(stage[pl.ds(0, 384)], s1)
    pairs[pl.ds(384, 128)] = dot(stage[pl.ds(384, 128)], s1_odd)

    def even_odd(base, size):
        return (
            pairs[pl.ds(base, size // 2, stride=2)],
            pairs[pl.ds(base + 1, size // 2, stride=2)],
        )

    own1 = (pl.ds(6, 4), pl.ds(8, 16))
    for k in range(4):
        even, odd = even_odd(128 * k, 128)
        value = (even + odd, 0.5 * (even + odd), 0.5 * odd, 0.5 * (even + odd))[k]
        c1[(k,) + own1] = value.reshape(4, 16, 128)
    coarse1 = halo(c1, 4, 6, 4, 16, (slice(None),))
    for dn in (0, 1, -1):
        sy, ty = cut(16, 8, 8, dn)
        coarse1.append(wire.send(c1.at[1, pl.ds(9, 1), sy], c1.at[1, pl.ds(1, 1), ty], 2, dn))

    rows1, rows2 = pl.ds(8, 16), pl.ds(8, 8)
    for k in range(2):
        a, b = 6 + 2 * k, 7 + 2 * k
        half = pl.ds(128 * k, 128)
        stage[pl.ds(0, 16), half] = c1[0, a, rows1] + c1[0, b, rows1]
        stage[pl.ds(16, 16), half] = c1[1, b, rows1]
        stage[pl.ds(32, 16), half] = c1[2, a, rows1] + c1[2, b, rows1]
        stage[pl.ds(48, 16), half] = c1[3, a, rows1] + c1[3, b, rows1]
    pairs[pl.ds(0, 48)] = dot(stage[pl.ds(0, 48)], s1)
    pairs[pl.ds(48, 16)] = dot(stage[pl.ds(48, 16)], s1_odd)
    for k in range(4):
        even, odd = even_odd(16 * k, 16)
        value = (even + odd, 0.5 * (even + odd), 0.5 * odd, 0.5 * (even + odd))[k]
        c2[k, 3, rows2] = value

    def blocks2(ref, lead=()):
        copies = []
        for dw, dn in near_peers(3):
            dst = ref.at[lead + (3 - dw, pl.ds(8 - 8 * dn, 8))]
            copies.append(wire.send(ref.at[lead + (3, rows2)], dst, dw, dn))
        return copies

    k3 = lax.broadcasted_iota(jnp.int32, (128, 128), 0)
    j3 = lax.broadcasted_iota(jnp.int32, (128, 128), 1)
    pair3 = (k3 % 64) // 2 == j3 % 32
    s3 = jnp.where(pair3, 1.0, 0.0).astype(F32)
    s3_upper = jnp.where(pair3 & (k3 >= 64), 1.0, 0.0).astype(F32)
    s3_odd = jnp.where(k3 % 64 == 2 * (j3 % 32) + 1, 1.0, 0.0).astype(F32)
    sub8 = lax.broadcasted_iota(jnp.int32, (8, 128), 0)
    lane8 = lax.broadcasted_iota(jnp.int32, (8, 128), 1)
    both_y = sub8 // 2 == lane8 // 32
    odd_y = sub8 == 2 * (lane8 // 32) + 1
    mine = sub8 == narrow

    def as_tile(row):
        return jnp.where(mine, jnp.broadcast_to(row, (8, 128)), 0.0)

    def to_row(values, matrix, mask):
        return jnp.sum(jnp.where(mask, dot(values, matrix), 0.0), axis=0, keepdims=True)

    tiles3 = (
        to_row(c2[0, 3, rows2], s3, both_y),
        0.5 * to_row(c2[1, 3, rows2], s3_upper, both_y),
        0.5 * to_row(c2[2, 3, rows2], s3, odd_y),
        0.5 * to_row(c2[3, 3, rows2], s3_odd, both_y),
        goal_part,
    )
    for k in range(5):
        ga[narrow, k] = as_tile(tiles3[k])
    gather_a = [wire.send(ga.at[narrow], ga.at[narrow], 0, dn) for dn in range(1, NN)]

    for copy in second:
        copy.wait_recv()
    weights(sink, ux0, uy0, uz0, d0, w0, 1, 15)
    for copy in third:
        copy.wait_recv()

    def first0(i):
        ua[i] = w0[i] * aim[i]

    layers(1, 15, first0, 2)
    sweep(ua, ub, aim, ux0, uy0, uz0, w0, 2, 14)
    sweep(ub, ua, aim, ux0, uy0, uz0, w0, 3, 13)

    def restrict0(k, carry):
        a = 4 + 2 * k
        r = residual_at(ua, aim, ux0, uy0, uz0, d0, a) + residual_at(
            ua, aim, ux0, uy0, uz0, d0, a + 1
        )
        stage[pl.ds(pl.multiple_of(32 * k, 32), 32)] = r[8:40]
        return carry

    lax.fori_loop(0, 4, restrict0, 0)
    pairs[pl.ds(0, 128)] = dot(stage[pl.ds(0, 128)], s1)
    even, odd = even_odd(0, 128)
    f1[own1] = (even + odd).reshape(4, 16, 128)
    right1 = halo(f1, 4, 6, 4, 16)
    v0[own] = ua[own]
    coarse2 = blocks2(c2, (slice(None),))
    for copy in gather_a:
        copy.wait_recv()
    gb[wide] = jnp.sum(ga[...], axis=0)


    for copy in coarse1:
        copy.wait_recv()
    weights(c1.at[0], c1.at[1], c1.at[2], c1.at[3], d1, w1, 2, 14)

    for copy in right1:
        copy.wait_recv()

    level1 = (c1.at[1], c1.at[2], c1.at[3])

    def first1(i):
        p1[i] = w1[i] * f1[i]

    layers(3, 13, first1, 5)
    sweep(p1, q1, f1, *level1, w1, 4, 12)
    sweep(q1, p1, f1, *level1, w1, 5, 11)

    for k in range(2):
        a = 6 + 2 * k
        r = residual_at(p1, f1, *level1, d1, a) + residual_at(p1, f1, *level1, d1, a + 1)
        stage[pl.ds(0, 16), pl.ds(128 * k, 128)] = r[8:24]
    pairs[pl.ds(0, 16)] = dot(stage[pl.ds(0, 16)], s1)
    even, odd = even_odd(0, 16)
    f2[3, rows2] = even + odd
    right2 = blocks2(f2)
    gather_b = [wire.send(gb.at[wide], gb.at[wide], dw, 0) for dw in range(1, NW)]
    for copy in coarse2:
        copy.wait_recv()
    low2 = lax.broadcasted_iota(jnp.int32, (24, 128), 1) < 64
    for t in range(7):
        ux, uy, uz = c2[1, t], c2[2, t], c2[3, t]
        ux = ux + previous_x(ux, c2[1, max(t - 1, 0)], low2)
        d2[t] = c2[0, t] + ux + (uy + down_y(uy)) + (uz + down_z(uz))
        w2[t] = OMEGA / d2[t]

    for copy in right2:
        copy.wait_recv()
    level2 = (c2.at[1], c2.at[2], c2.at[3])

    for t in range(1, 6):
        p2[t] = w2[t] * f2[t]
    sweep2(p2, q2, f2, *level2, w2, low2, 2, 5)
    sweep2(q2, p2, f2, *level2, w2, low2, 2, 5)
    centre, pull = coupling2(p2, *level2, 3, low2)
    r = f2[3] + pull - d2[3] * centre
    old = len(wire.unsent)
    ra[narrow] = as_tile(to_row(r[8:16], s3, both_y))
    right3 = [wire.send(ra.at[narrow], ra.at[narrow], 0, dn) for dn in range(1, NN)]
    v2[3, rows2] = p2[3, rows2]
    before2 = blocks2(v2)
    for copy in right3:
        copy.wait_recv()
    rb[wide] = jnp.sum(ra[...], axis=0)
    right3 = [wire.send(rb.at[wide], rb.at[wide], dw, 0) for dw in range(1, NW)]
    v1[own1] = p1[own1]
    before1 = halo(v1, 4, 6, 4, 16)
    for dw, src, dst in ((2, 9, 1), (-2, 6, 14)):
        for dn in (0, 1, -1):
            sy, ty = cut(16, 8, 8, dn)
            before1.append(
                wire.send(v1.at[pl.ds(src, 1), sy], v1.at[pl.ds(dst, 1), ty], dw, dn)
            )
    before0 = halo(v0, 8, 4, 4, 32, corner=3)

    wire.flush(len(wire.unsent) - old)
    for copy in gather_b:
        copy.wait_recv()
    goal = jnp.sum(jnp.sum(gb[:, 4], axis=0), axis=(0, 1), keepdims=True)
    for copy in right3:
        copy.wait_recv()

    conjugate(rb[...], gb, solved3)

    for a in range(7):
        layer = lax.rem(wide + (a - 3 + NW), NW)
        for b in range(3):
            line = lax.rem(narrow + (b - 1 + NN), NN)
            row = jnp.broadcast_to(solved3[layer, pl.ds(line, 1)], (8, 128))
            rows3[pl.ds(24 * a + 8 * b, 8)] = jnp.where(both_y, row, 0.0)
    e3 = jnp.where(k3 % 32 == (j3 % 64) // 2, 1.0, 0.0).astype(F32)
    lift2[...] = dot(rows3[...], e3).reshape(7, 24, 128)
    for copy in before2:
        copy.wait_recv()

    for t in range(7):
        p2[t] = v2[t] + lift2[t]
    sweep2(p2, q2, f2, *level2, w2, low2, 0, 7)
    sweep2(q2, p2, f2, *level2, w2, low2, 1, 6)
    sweep2(p2, q2, f2, *level2, w2, low2, 1, 6)

    e1 = spread_matrix(128, 256)
    lift = dot(q2[pl.ds(1, 5)].reshape(120, 128), e1).reshape(5, 24, 256)
    for t in range(5):
        for half in range(2):
            part = lift[t, 4:20, 128 * half : 128 * half + 128]
            lift1[2 * t + half, pl.ds(0, 16, stride=2)] = part
            lift1[2 * t + half, pl.ds(1, 16, stride=2)] = part
    for copy in before1:
        copy.wait_recv()

    for i in range(1, 15):
        p1[i] = v1[i] + lift1[1 + i // 2]
    sweep(p1, q1, f1, *level1, w1, 2, 14)
    sweep(q1, p1, f1, *level1, w1, 3, 13)
    sweep(p1, q1, f1, *level1, w1, 4, 12)

    lift = dot(q1[pl.ds(4, 8), pl.ds(0, 32)].reshape(256, 128), e1).reshape(8, 32, 256)
    for copy in before0:
        copy.wait_recv()
    for a in range(8):
        for half in range(2):
            part = lift[a, 4:28, 128 * half : 128 * half + 128]
            lift0[a, half, pl.ds(0, 24, stride=2)] = part
            lift0[a, half, pl.ds(1, 24, stride=2)] = part

    def correct0(k):
        both = jnp.concatenate([lift0[k, 0], lift0[k, 1]], axis=1)
        ua[2 * k] = v0[2 * k] + both
        ua[2 * k + 1] = v0[2 * k + 1] + both

    layers(0, 8, correct0, 1)
    sweep(ua, ub, aim, ux0, uy0, uz0, w0, 1, 15)
    sweep(ub, ua, aim, ux0, uy0, uz0, w0, 2, 14)
    sweep(ua, ub, aim, ux0, uy0, uz0, w0, 3, 13)
    adj_out[...] = ub[own]

    for copy in temps:
        copy.wait_recv()
    scale = (-0.5 * 3.0 * (1.0 - FLOOR_CONDUCTION)) * (CELLS / goal)
    my, mz = 2.0 * hy, 2.0 * hz

    def face_x(i):
        return (temp[i - 3] - temp[i - 2]) * (ub[i] - ub[i + 1]) * (2.0 * hx(i))

    def slope(i, below):
        t, a, s = temp[i - 3], ub[i], dens[i]
        above = face_x(i)
        fy = (t - up_y(t)) * (a - up_y(a)) * my
        fz = (t - up_z(t)) * (a - up_z(a)) * mz
        raw = (above + below) + (fy + down_y(fy)) + (fz + down_z(fz))
        zs[i, pl.ds(8, 32)] = (raw * scale * s * s)[8:40]
        return above

    def filter_halo(targets):
        copies = []
        for dw, dn in targets:
            sx, tx = cut(8, 4, 3 if dw and dn else 4, dw)
            sy, ty = cut(32, 8, 8, dn)
            copies.append(wire.send(zs.at[sx, sy], zs.at[tx, ty], dw, dn))
        return copies

    below = lax.fori_loop(4, 8, slope, face_x(3))
    scaled = filter_halo([(-1, 0), (-1, 1), (-1, -1)])
    lax.fori_loop(8, 12, slope, below)
    scaled += filter_halo([(1, 0), (1, 1), (1, -1), (0, 1), (0, -1)])

    for copy in scaled:
        copy.wait_recv()
    first_layer = jnp.where(wide == 0, 4, 0)
    last_layer = jnp.where(wide == NW - 1, 11, 15)
    top, bottom = row0 == 255, row0 == 0
    right, left = lane0 == 255, lane0 == 0
    c1_filter = FILTER_OMEGA / (1.0 + 6.0 * STRENGTH)

    def filter_at(src, i):
        z = src[i]
        near = src[jnp.minimum(i + 1, last_layer)] + src[jnp.maximum(i - 1, first_layer)]
        near = near + (jnp.where(top, z, up_y(z)) + jnp.where(bottom, z, down_y(z)))
        near = near + (jnp.where(right, z, up_z(z)) + jnp.where(left, z, down_z(z)))
        return (1.0 - FILTER_OMEGA) * z + c1_filter * (zs[i] + STRENGTH * near)

    def filter_sweep(src, dst, lo, hi):
        def body(i):
            dst[i] = filter_at(src, i)

        layers(lo, hi, body, 2)

    filter_sweep(zs, ua, 1, 15)
    filter_sweep(ua, ub, 2, 14)
    filter_sweep(ub, ua, 3, 13)

    def last_filter(i):
        sens_out[i - 4] = filter_at(ua, i)[8:40]

    layers(4, 12, last_filter, 2)
    wire.flush()


def local(density, temperature, aim, sink):
    vmem = lambda *shape: pltpu.VMEM(shape, F32)
    level0 = (16, 48, 256)
    level1 = (16, 32, 128)
    level2 = (7, 24, 128)
    scratch = [vmem(*level0), vmem(10, 48, 256)] + [vmem(*level0)] * 11 + [vmem(8, 2, 48, 128)]
    scratch += [vmem(512, 256), vmem(512, 128)]
    scratch += [vmem(4, *level1)] + [vmem(*level1)] * 6 + [vmem(10, 32, 128)]
    scratch += [vmem(4, *level2)] + [vmem(*level2)] * 6 + [vmem(7, 24, 128)]
    scratch += [vmem(NN, 5, 8, 128), vmem(NW, 5, 8, 128), vmem(NN, 8, 128), vmem(NW, 8, 128)]
    scratch += [vmem(NW, 8, 128), vmem(168, 128)]
    scratch += [
        pltpu.SemaphoreType.DMA((4,)),
        pltpu.SemaphoreType.DMA((N_SEMS,)),
        pltpu.SemaphoreType.DMA((N_SEMS,)),
    ]
    block = jax.ShapeDtypeStruct((8, 32, 256), F32)
    whole = pl.BlockSpec(memory_space=pltpu.VMEM)
    return pl.pallas_call(
        kernel,
        out_shape=(block, block),
        in_specs=[pl.BlockSpec(memory_space=pl.ANY)] * 4,
        out_specs=(whole, whole),
        scratch_shapes=scratch,
        compiler_params=pltpu.CompilerParams(
            collective_id=0, has_side_effects=True, vmem_limit_bytes=48 * 2**20
        ),
    )(density, temperature, aim, sink)


def solution(mesh):
    placed = P("wide", "narrow", None)
    return jax.shard_map(
        local,
        mesh=mesh,
        in_specs=(placed,) * 4,
        out_specs=(placed, placed),
        check_vma=False,
    )
```

```python
import functools
import math

import jax
import jax.numpy as jnp
from jax import lax
from jax.experimental import pallas as pl
from jax.experimental.pallas import tpu as pltpu
from jax.sharding import PartitionSpec as P

COARSE_ITERS = 8
RADIUS = 4
FLOOR_CONDUCTION = 0.001
OMEGA = 0.7
FILTER_OMEGA = 0.8
STRENGTH = (RADIUS / (2.0 * math.sqrt(3.0))) ** 2
MESH = pl.DeviceIdType.MESH
NW, NN = 16, 8
CELLS = 128 * 256 * 256
F32 = jnp.float32
BF16 = jnp.bfloat16
N_GROUPS = 16
BLANK_TILES = 200
UNROLL = {48: 4, 32: 8}


def near_peers(reach):
    peers = [
        (dw, dn)
        for dw in range(-reach, reach + 1)
        for dn in (-1, 0, 1)
        if (dw, dn) != (0, 0)
    ]
    return sorted(peers, key=lambda p: (p[1] != 0 and p[0] != 0, p[0] == 0, abs(p[0])))


def greeted():
    peers = [(dw % NW, dn % NN) for dw, dn in near_peers(3)]
    peers += [(0, k) for k in range(1, NN)] + [(k, 0) for k in range(1, NW)]
    return sorted(set(peers))


def layers(lo, hi, body, unroll):
    steps = (hi - lo) // unroll

    def step(k, carry):
        for j in range(unroll):
            body(lo + k * unroll + j)
        return carry

    if steps > 1:
        lax.fori_loop(0, steps, step, 0)
    else:
        step(0, 0) if steps else None
    for i in range(lo + steps * unroll, hi):
        body(i)


class Group:
    def __init__(self, blank, send_sem, recv_sem):
        self.blank, self.send_sem, self.recv_sem = blank, send_sem, recv_sem
        self.tiles = 0

    def wait(self, sem):
        whole = self.blank.at[pl.ds(0, self.tiles)]
        pltpu.make_async_copy(whole, whole, sem).wait()

    def wait_recv(self):
        self.wait(self.recv_sem)


class Wire:
    def __init__(self, wide, narrow, blank, send_sem, recv_sem):
        self.wide, self.narrow, self.blank = wide, narrow, blank
        self.send_sem, self.recv_sem = send_sem, recv_sem
        self.groups = []
        self.sent = 0

    def peer(self, dw, dn):
        return (lax.rem(self.wide + (dw + NW), NW), lax.rem(self.narrow + (dn + NN), NN))

    def group(self):
        k = len(self.groups)
        self.groups.append(Group(self.blank, self.send_sem.at[k], self.recv_sem.at[k]))
        return self.groups[-1]

    def send(self, group, src, dst, dw, dn):
        pltpu.make_async_remote_copy(
            src_ref=src,
            dst_ref=dst,
            send_sem=group.send_sem,
            recv_sem=group.recv_sem,
            device_id=self.peer(dw, dn),
            device_id_type=MESH,
        ).start()
        group.tiles += math.prod(src.shape) // 1024

    def flush(self, last):
        for group in self.groups[self.sent : last]:
            group.wait(group.send_sem)
        self.sent = last


def cut(own, halo, width, shift):
    if shift == 0:
        return pl.ds(halo, own), pl.ds(halo, own)
    if shift > 0:
        return pl.ds(halo + own - width, width), pl.ds(halo - width, width)
    return pl.ds(halo, width), pl.ds(halo + own, width)


def up_y(v):
    return pltpu.roll(v, v.shape[0] - 1, 0)


def down_y(v):
    return pltpu.roll(v, 1, 0)


def up_z(v):
    return pltpu.roll(v, v.shape[1] - 1, 1)


def down_z(v):
    return pltpu.roll(v, 1, 1)


def coupling(u, ux, uy, uz, i):
    centre = u[i]
    fy, fz = uy[i], uz[i]
    return centre, (
        (ux[i] * u[i + 1] + ux[i - 1] * u[i - 1])
        + (fy * up_y(centre) + down_y(fy * centre))
        + (fz * up_z(centre) + down_z(fz * centre))
    )


def sweep(src, dst, rhs, ux, uy, uz, weight, lo, hi):
    def body(i):
        centre, pull = coupling(src, ux, uy, uz, i)
        dst[i] = (1.0 - OMEGA) * centre + weight[i] * (rhs[i] + pull)

    layers(lo, hi, body, UNROLL[src.shape[1]])


def residual_at(src, rhs, ux, uy, uz, diag, i):
    centre, pull = coupling(src, ux, uy, uz, i)
    return rhs[i] + pull - diag[i] * centre


def weights(sink, ux, uy, uz, diag, weight, lo, hi):
    def body(i):
        fy, fz = uy[i], uz[i]
        total = sink[i] + (ux[i] + ux[i - 1]) + (fy + down_y(fy)) + (fz + down_z(fz))
        diag[i] = total
        weight[i] = OMEGA / total

    layers(lo, hi, body, UNROLL[diag.shape[1]])


def next_x(here, above, low):
    return pltpu.roll(jnp.where(low, above, here), 64, 1)


def previous_x(here, below, low):
    return pltpu.roll(jnp.where(low, here, below), 64, 1)


def coupling2(u, ux, uy, uz, t, low):
    centre, above, below = u[t], u[min(t + 1, 6)], max(t - 1, 0)
    fy, fz = uy[t], uz[t]
    return centre, (
        (
            ux[t] * next_x(centre, above, low)
            + previous_x(ux[t] * centre, ux[below] * u[below], low)
        )
        + (fy * up_y(centre) + down_y(fy * centre))
        + (fz * up_z(centre) + down_z(fz * centre))
    )


def sweep2(src, dst, rhs, ux, uy, uz, weight, low, lo, hi):
    for t in range(lo, hi):
        centre, pull = coupling2(src, ux, uy, uz, t, low)
        dst[t] = (1.0 - OMEGA) * centre + weight[t] * (rhs[t] + pull)


def dot(a, b):
    b = b.astype(BF16)
    high = a.astype(BF16)
    rest = a - high.astype(F32)
    middle = rest.astype(BF16)
    low = (rest - middle.astype(F32)).astype(BF16)
    products = [jnp.dot(part, b, preferred_element_type=F32) for part in (low, middle, high)]
    return products[0] + products[1] + products[2]


def pair_matrix(rows, cols, odd):
    k = lax.broadcasted_iota(jnp.int32, (rows, cols), 0)
    j = lax.broadcasted_iota(jnp.int32, (rows, cols), 1)
    hit = (k == 2 * j + 1) if odd else (k // 2 == j)
    return jnp.where(hit, 1.0, 0.0).astype(F32)


def spread_matrix(rows, cols):
    k = lax.broadcasted_iota(jnp.int32, (rows, cols), 0)
    j = lax.broadcasted_iota(jnp.int32, (rows, cols), 1)
    return jnp.where(k == j // 2, 1.0, 0.0).astype(F32)


def conjugate(rhs, coef_ref, out_ref):
    lane = lax.broadcasted_iota(jnp.int32, (NW, 8, 128), 2)
    low, high = lane < 96, lane >= 32
    sink, ux, uy, uz = (coef_ref[:, k] for k in range(4))

    def y_up(v):
        q = pltpu.roll(v, 96, 2)
        return jnp.where(low, q, pltpu.roll(q, 7, 1))

    def y_down(v):
        q = pltpu.roll(v, 32, 2)
        return jnp.where(high, q, pltpu.roll(q, 1, 1))

    def z_up(v):
        return pltpu.roll(v, 127, 2)

    def z_down(v):
        return pltpu.roll(v, 1, 2)

    def total(v):
        return jnp.sum(jnp.sum(v, axis=0), axis=(0, 1), keepdims=True)[None]

    edge = jnp.zeros((1, 8, 128), F32)
    dx = jnp.concatenate([edge, ux[:-1]], axis=0)
    diag = sink + (ux + dx) + (uy + y_down(uy)) + (uz + z_down(uz))

    def apply(p):
        above = jnp.concatenate([p[1:], edge], axis=0)
        px = ux * p
        below = jnp.concatenate([edge, px[:-1]], axis=0)
        return diag * p - (
            (ux * above + below)
            + (uy * y_up(p) + y_down(uy * p))
            + (uz * z_up(p) + z_down(uz * p))
        )

    def body(_, carry):
        solved, residual, direction, norm_now = carry
        applied = apply(direction)
        step = norm_now / total(direction * applied)
        solved = solved + step * direction
        residual = residual - step * applied
        norm_next = total(residual * residual)
        direction = residual + (norm_next / norm_now) * direction
        return solved, residual, direction, norm_next

    start = (jnp.zeros_like(rhs), rhs, rhs, total(rhs * rhs))
    solved, residual, direction, norm_now = lax.fori_loop(0, COARSE_ITERS - 1, body, start)
    step = norm_now / total(direction * apply(direction))
    out_ref[...] = solved + step * direction


def kernel(
    dens_in, temp_in, aim_in, sink_in, adj_out, sens_out,
    dens, temp, aim, sink, ux0, uy0, uz0, d0, w0, ua, ub, v0, zs, lift0,
    stage, pairs,
    c1, f1, v1, d1, w1, p1, q1, lift1,
    c2, f2, v2, d2, w2, p2, q2, lift2,
    ga, gb, ra, rb, solved3, rows3, blank,
    in_sem, send_sem, recv_sem,
):
    wide, narrow = lax.axis_index("wide"), lax.axis_index("narrow")
    wire = Wire(wide, narrow, blank, send_sem, recv_sem)
    barrier = pltpu.get_barrier_semaphore()
    peers = greeted()
    for dw, dn in peers:
        pl.semaphore_signal(barrier, inc=1, device_id=wire.peer(dw, dn), device_id_type=MESH)

    own = (pl.ds(4, 8), pl.ds(8, 32))
    loads = []
    for k, (src, dst) in enumerate(
        ((dens_in, dens.at[own]), (sink_in, sink.at[own]), (aim_in, aim.at[own]),
         (temp_in, temp.at[pl.ds(1, 8), pl.ds(8, 32)]))
    ):
        load = pltpu.make_async_copy(src, dst, in_sem.at[k])
        load.start()
        loads.append(load)
    for load in loads:
        load.wait()
    pl.semaphore_wait(barrier, len(peers))

    def halo(ref, own_x, halo_x, width_x, own_y, lead=(), corner=0):
        group = wire.group()
        for dw, dn in near_peers(1):
            sx, tx = cut(own_x, halo_x, corner if corner and dn else width_x, dw)
            sy, ty = cut(own_y, 8, 8, dn)
            wire.send(group, ref.at[lead + (sx, sy)], ref.at[lead + (tx, ty)], dw, dn)
        return group

    first = halo(dens, 8, 4, 4, 32, corner=3)
    second = halo(sink, 8, 4, 3, 32, corner=2)
    third = halo(aim, 8, 4, 3, 32, corner=2)
    temps = wire.group()
    for dw, dn in ((1, 0), (-1, 0), (0, 1), (0, -1)):
        sx, tx = cut(8, 1, 1, dw)
        sy, ty = cut(32, 8, 8, dn)
        wire.send(temps, temp.at[sx, sy], temp.at[tx, ty], dw, dn)

    goal_part = jnp.sum(aim[own] * temp[pl.ds(1, 8), pl.ds(8, 32)], axis=0)
    goal_part = jnp.sum(goal_part[:, :128] + goal_part[:, 128:], axis=0, keepdims=True)

    row0 = narrow * 32 - 8 + lax.broadcasted_iota(jnp.int32, (48, 256), 0)
    lane0 = lax.broadcasted_iota(jnp.int32, (48, 256), 1)
    hy = jnp.where((row0 == -1) | (row0 == 255), 0.0, 0.5).astype(F32)
    hz = jnp.where(lane0 == 255, 0.0, 0.5).astype(F32)

    def hx(i):
        g = wide * 8 - 4 + i
        return jnp.where((g == -1) | (g == 127), 0.0, 0.5).astype(F32)

    def conduct(i):
        s = dens[i]
        return FLOOR_CONDUCTION + (1.0 - FLOOR_CONDUCTION) * s * s * s

    s1, s1_odd = pair_matrix(256, 128, False), pair_matrix(256, 128, True)
    first.wait_recv()

    ux0[0] = (conduct(0) + conduct(1)) * hx(0)

    def faces(i):
        c = conduct(i)
        ux0[i] = (c + conduct(i + 1)) * hx(i)
        uy0[i] = (c + up_y(c)) * hy
        uz0[i] = (c + up_z(c)) * hz

    layers(1, 15, faces, 4)

    rows = pl.ds(8, 32)
    for k in range(4):
        a, b = 4 + 2 * k, 5 + 2 * k
        stage[pl.ds(32 * k, 32)] = sink[a, rows] + sink[b, rows]
        stage[pl.ds(128 + 32 * k, 32)] = ux0[b, rows]
        stage[pl.ds(256 + 32 * k, 32)] = uy0[a, rows] + uy0[b, rows]
        stage[pl.ds(384 + 32 * k, 32)] = uz0[a, rows] + uz0[b, rows]
    pairs[pl.ds(0, 384)] = dot(stage[pl.ds(0, 384)], s1)
    pairs[pl.ds(384, 128)] = dot(stage[pl.ds(384, 128)], s1_odd)

    def even_odd(base, size):
        return (
            pairs[pl.ds(base, size // 2, stride=2)],
            pairs[pl.ds(base + 1, size // 2, stride=2)],
        )

    own1 = (pl.ds(6, 4), pl.ds(8, 16))
    for k in range(4):
        even, odd = even_odd(128 * k, 128)
        value = (even + odd, 0.5 * (even + odd), 0.5 * odd, 0.5 * (even + odd))[k]
        c1[(k,) + own1] = value.reshape(4, 16, 128)
    coarse1 = halo(c1, 4, 6, 4, 16, (slice(None),))
    for dn in (0, 1, -1):
        sy, ty = cut(16, 8, 8, dn)
        wire.send(coarse1, c1.at[1, pl.ds(9, 1), sy], c1.at[1, pl.ds(1, 1), ty], 2, dn)

    rows1, rows2 = pl.ds(8, 16), pl.ds(8, 8)
    for k in range(2):
        a, b = 6 + 2 * k, 7 + 2 * k
        half = pl.ds(128 * k, 128)
        stage[pl.ds(0, 16), half] = c1[0, a, rows1] + c1[0, b, rows1]
        stage[pl.ds(16, 16), half] = c1[1, b, rows1]
        stage[pl.ds(32, 16), half] = c1[2, a, rows1] + c1[2, b, rows1]
        stage[pl.ds(48, 16), half] = c1[3, a, rows1] + c1[3, b, rows1]
    pairs[pl.ds(0, 48)] = dot(stage[pl.ds(0, 48)], s1)
    pairs[pl.ds(48, 16)] = dot(stage[pl.ds(48, 16)], s1_odd)
    for k in range(4):
        even, odd = even_odd(16 * k, 16)
        value = (even + odd, 0.5 * (even + odd), 0.5 * odd, 0.5 * (even + odd))[k]
        c2[k, 3, rows2] = value

    def blocks2(ref, lead=()):
        group = wire.group()
        for dw, dn in near_peers(3):
            dst = ref.at[lead + (3 - dw, pl.ds(8 - 8 * dn, 8))]
            wire.send(group, ref.at[lead + (3, rows2)], dst, dw, dn)
        return group

    k3 = lax.broadcasted_iota(jnp.int32, (128, 128), 0)
    j3 = lax.broadcasted_iota(jnp.int32, (128, 128), 1)
    pair3 = (k3 % 64) // 2 == j3 % 32
    s3 = jnp.where(pair3, 1.0, 0.0).astype(F32)
    s3_upper = jnp.where(pair3 & (k3 >= 64), 1.0, 0.0).astype(F32)
    s3_odd = jnp.where(k3 % 64 == 2 * (j3 % 32) + 1, 1.0, 0.0).astype(F32)
    sub8 = lax.broadcasted_iota(jnp.int32, (8, 128), 0)
    lane8 = lax.broadcasted_iota(jnp.int32, (8, 128), 1)
    both_y = sub8 // 2 == lane8 // 32
    odd_y = sub8 == 2 * (lane8 // 32) + 1
    mine = sub8 == narrow

    def as_tile(row):
        return jnp.where(mine, jnp.broadcast_to(row, (8, 128)), 0.0)

    def to_row(values, matrix, mask):
        return jnp.sum(jnp.where(mask, dot(values, matrix), 0.0), axis=0, keepdims=True)

    tiles3 = (
        to_row(c2[0, 3, rows2], s3, both_y),
        0.5 * to_row(c2[1, 3, rows2], s3_upper, both_y),
        0.5 * to_row(c2[2, 3, rows2], s3, odd_y),
        0.5 * to_row(c2[3, 3, rows2], s3_odd, both_y),
        goal_part,
    )
    for k in range(5):
        ga[narrow, k] = as_tile(tiles3[k])
    def along_narrow(ref):
        group = wire.group()
        for dn in range(1, NN):
            wire.send(group, ref.at[narrow], ref.at[narrow], 0, dn)
        return group

    def along_wide(ref):
        group = wire.group()
        for dw in range(1, NW):
            wire.send(group, ref.at[wide], ref.at[wide], dw, 0)
        return group

    gather_a = along_narrow(ga)

    second.wait_recv()
    weights(sink, ux0, uy0, uz0, d0, w0, 1, 15)
    third.wait_recv()

    def first0(i):
        ua[i] = w0[i] * aim[i]

    layers(1, 15, first0, 4)
    sweep(ua, ub, aim, ux0, uy0, uz0, w0, 2, 14)
    sweep(ub, ua, aim, ux0, uy0, uz0, w0, 3, 13)

    def restrict0(k, carry):
        a = 4 + 2 * k
        r = residual_at(ua, aim, ux0, uy0, uz0, d0, a) + residual_at(
            ua, aim, ux0, uy0, uz0, d0, a + 1
        )
        stage[pl.ds(pl.multiple_of(32 * k, 32), 32)] = r[8:40]
        return carry

    lax.fori_loop(0, 4, restrict0, 0)
    pairs[pl.ds(0, 128)] = dot(stage[pl.ds(0, 128)], s1)
    even, odd = even_odd(0, 128)
    f1[own1] = (even + odd).reshape(4, 16, 128)
    right1 = halo(f1, 4, 6, 4, 16)
    v0[own] = ua[own]
    coarse2 = blocks2(c2, (slice(None),))
    gather_a.wait_recv()
    gb[wide] = jnp.sum(ga[...], axis=0)


    coarse1.wait_recv()
    weights(c1.at[0], c1.at[1], c1.at[2], c1.at[3], d1, w1, 2, 14)

    right1.wait_recv()

    level1 = (c1.at[1], c1.at[2], c1.at[3])

    def first1(i):
        p1[i] = w1[i] * f1[i]

    layers(3, 13, first1, 5)
    sweep(p1, q1, f1, *level1, w1, 4, 12)
    sweep(q1, p1, f1, *level1, w1, 5, 11)

    for k in range(2):
        a = 6 + 2 * k
        r = residual_at(p1, f1, *level1, d1, a) + residual_at(p1, f1, *level1, d1, a + 1)
        stage[pl.ds(0, 16), pl.ds(128 * k, 128)] = r[8:24]
    pairs[pl.ds(0, 16)] = dot(stage[pl.ds(0, 16)], s1)
    even, odd = even_odd(0, 16)
    f2[3, rows2] = even + odd
    right2 = blocks2(f2)
    gather_b = along_wide(gb)
    coarse2.wait_recv()
    low2 = lax.broadcasted_iota(jnp.int32, (24, 128), 1) < 64
    for t in range(7):
        ux, uy, uz = c2[1, t], c2[2, t], c2[3, t]
        ux = ux + previous_x(ux, c2[1, max(t - 1, 0)], low2)
        d2[t] = c2[0, t] + ux + (uy + down_y(uy)) + (uz + down_z(uz))
        w2[t] = OMEGA / d2[t]

    right2.wait_recv()
    level2 = (c2.at[1], c2.at[2], c2.at[3])

    for t in range(1, 6):
        p2[t] = w2[t] * f2[t]
    sweep2(p2, q2, f2, *level2, w2, low2, 2, 5)
    sweep2(q2, p2, f2, *level2, w2, low2, 2, 5)
    centre, pull = coupling2(p2, *level2, 3, low2)
    r = f2[3] + pull - d2[3] * centre
    old = len(wire.groups)
    ra[narrow] = as_tile(to_row(r[8:16], s3, both_y))
    right3 = along_narrow(ra)
    v2[3, rows2] = p2[3, rows2]
    before2 = blocks2(v2)
    right3.wait_recv()
    rb[wide] = jnp.sum(ra[...], axis=0)
    right3 = along_wide(rb)
    v1[own1] = p1[own1]
    before1 = halo(v1, 4, 6, 4, 16)
    for dw, src, dst in ((2, 9, 1), (-2, 6, 14)):
        for dn in (0, 1, -1):
            sy, ty = cut(16, 8, 8, dn)
            wire.send(before1, v1.at[pl.ds(src, 1), sy], v1.at[pl.ds(dst, 1), ty], dw, dn)
    before0 = halo(v0, 8, 4, 4, 32, corner=3)

    wire.flush(old)
    gather_b.wait_recv()
    goal = jnp.sum(jnp.sum(gb[:, 4], axis=0), axis=(0, 1), keepdims=True)
    right3.wait_recv()

    conjugate(rb[...], gb, solved3)

    for a in range(7):
        layer = lax.rem(wide + (a - 3 + NW), NW)
        for b in range(3):
            line = lax.rem(narrow + (b - 1 + NN), NN)
            row = jnp.broadcast_to(solved3[layer, pl.ds(line, 1)], (8, 128))
            rows3[pl.ds(24 * a + 8 * b, 8)] = jnp.where(both_y, row, 0.0)
    e3 = jnp.where(k3 % 32 == (j3 % 64) // 2, 1.0, 0.0).astype(F32)
    lift2[...] = dot(rows3[...], e3).reshape(7, 24, 128)
    before2.wait_recv()

    for t in range(7):
        p2[t] = v2[t] + lift2[t]
    sweep2(p2, q2, f2, *level2, w2, low2, 0, 7)
    sweep2(q2, p2, f2, *level2, w2, low2, 1, 6)
    sweep2(p2, q2, f2, *level2, w2, low2, 1, 6)

    e1 = spread_matrix(128, 256)
    lift = dot(q2[pl.ds(1, 5)].reshape(120, 128), e1).reshape(5, 24, 256)
    for t in range(5):
        for half in range(2):
            part = lift[t, 4:20, 128 * half : 128 * half + 128]
            lift1[2 * t + half, pl.ds(0, 16, stride=2)] = part
            lift1[2 * t + half, pl.ds(1, 16, stride=2)] = part
    before1.wait_recv()

    for i in range(1, 15):
        p1[i] = v1[i] + lift1[1 + i // 2]
    sweep(p1, q1, f1, *level1, w1, 2, 14)
    sweep(q1, p1, f1, *level1, w1, 3, 13)
    sweep(p1, q1, f1, *level1, w1, 4, 12)

    lift = dot(q1[pl.ds(4, 8), pl.ds(0, 32)].reshape(256, 128), e1).reshape(8, 32, 256)
    before0.wait_recv()
    for a in range(8):
        for half in range(2):
            part = lift[a, 4:28, 128 * half : 128 * half + 128]
            lift0[a, half, pl.ds(0, 24, stride=2)] = part
            lift0[a, half, pl.ds(1, 24, stride=2)] = part

    def correct0(k):
        both = jnp.concatenate([lift0[k, 0], lift0[k, 1]], axis=1)
        ua[2 * k] = v0[2 * k] + both
        ua[2 * k + 1] = v0[2 * k + 1] + both

    layers(0, 8, correct0, 4)
    sweep(ua, ub, aim, ux0, uy0, uz0, w0, 1, 15)
    sweep(ub, ua, aim, ux0, uy0, uz0, w0, 2, 14)
    sweep(ua, ub, aim, ux0, uy0, uz0, w0, 3, 13)
    adj_out[...] = ub[own]

    temps.wait_recv()
    scale = (-0.5 * 3.0 * (1.0 - FLOOR_CONDUCTION)) * (CELLS / goal)
    my, mz = 2.0 * hy, 2.0 * hz

    def face_x(i):
        return (temp[i - 3] - temp[i - 2]) * (ub[i] - ub[i + 1]) * (2.0 * hx(i))

    def slope(i, below):
        t, a, s = temp[i - 3], ub[i], dens[i]
        above = face_x(i)
        fy = (t - up_y(t)) * (a - up_y(a)) * my
        fz = (t - up_z(t)) * (a - up_z(a)) * mz
        raw = (above + below) + (fy + down_y(fy)) + (fz + down_z(fz))
        zs[i, pl.ds(8, 32)] = (raw * scale * s * s)[8:40]
        return above

    scaled = wire.group()

    def filter_halo(targets):
        for dw, dn in targets:
            sx, tx = cut(8, 4, 3 if dw and dn else 4, dw)
            sy, ty = cut(32, 8, 8, dn)
            wire.send(scaled, zs.at[sx, sy], zs.at[tx, ty], dw, dn)

    below = lax.fori_loop(4, 8, slope, face_x(3))
    filter_halo([(-1, 0), (-1, 1), (-1, -1)])
    lax.fori_loop(8, 12, slope, below)
    filter_halo([(1, 0), (1, 1), (1, -1), (0, 1), (0, -1)])

    scaled.wait_recv()
    first_layer = jnp.where(wide == 0, 4, 0)
    last_layer = jnp.where(wide == NW - 1, 11, 15)
    top, bottom = row0 == 255, row0 == 0
    right, left = lane0 == 255, lane0 == 0
    c1_filter = FILTER_OMEGA / (1.0 + 6.0 * STRENGTH)

    def filter_at(src, i):
        z = src[i]
        near = src[jnp.minimum(i + 1, last_layer)] + src[jnp.maximum(i - 1, first_layer)]
        near = near + (jnp.where(top, z, up_y(z)) + jnp.where(bottom, z, down_y(z)))
        near = near + (jnp.where(right, z, up_z(z)) + jnp.where(left, z, down_z(z)))
        return (1.0 - FILTER_OMEGA) * z + c1_filter * (zs[i] + STRENGTH * near)

    def filter_sweep(src, dst, lo, hi):
        def body(i):
            dst[i] = filter_at(src, i)

        layers(lo, hi, body, 4)

    filter_sweep(zs, ua, 1, 15)
    filter_sweep(ua, ub, 2, 14)
    filter_sweep(ub, ua, 3, 13)

    def last_filter(i):
        sens_out[i - 4] = filter_at(ua, i)[8:40]

    layers(4, 12, last_filter, 4)
    wire.flush(len(wire.groups))


def local(density, temperature, aim, sink):
    vmem = lambda *shape: pltpu.VMEM(shape, F32)
    level0 = (16, 48, 256)
    level1 = (16, 32, 128)
    level2 = (7, 24, 128)
    scratch = [vmem(*level0), vmem(10, 48, 256)] + [vmem(*level0)] * 11 + [vmem(8, 2, 48, 128)]
    scratch += [vmem(512, 256), vmem(512, 128)]
    scratch += [vmem(4, *level1)] + [vmem(*level1)] * 6 + [vmem(10, 32, 128)]
    scratch += [vmem(4, *level2)] + [vmem(*level2)] * 6 + [vmem(7, 24, 128)]
    scratch += [vmem(NN, 5, 8, 128), vmem(NW, 5, 8, 128), vmem(NN, 8, 128), vmem(NW, 8, 128)]
    scratch += [vmem(NW, 8, 128), vmem(168, 128), vmem(BLANK_TILES, 8, 128)]
    scratch += [
        pltpu.SemaphoreType.DMA((4,)),
        pltpu.SemaphoreType.DMA((N_GROUPS,)),
        pltpu.SemaphoreType.DMA((N_GROUPS,)),
    ]
    block = jax.ShapeDtypeStruct((8, 32, 256), F32)
    whole = pl.BlockSpec(memory_space=pltpu.VMEM)
    return pl.pallas_call(
        kernel,
        out_shape=(block, block),
        in_specs=[pl.BlockSpec(memory_space=pl.ANY)] * 4,
        out_specs=(whole, whole),
        scratch_shapes=scratch,
        compiler_params=pltpu.CompilerParams(
            collective_id=0, has_side_effects=True, vmem_limit_bytes=62 * 2**20
        ),
    )(density, temperature, aim, sink)


def solution(mesh):
    placed = P("wide", "narrow", None)
    return jax.shard_map(
        local,
        mesh=mesh,
        in_specs=(placed,) * 4,
        out_specs=(placed, placed),
        check_vma=False,
    )
```

```python
import functools
import math

import jax
import jax.numpy as jnp
from jax import lax
from jax.experimental import pallas as pl
from jax.experimental.pallas import tpu as pltpu
from jax.sharding import PartitionSpec as P

COARSE_ITERS = 8
RADIUS = 4
FLOOR_CONDUCTION = 0.001
OMEGA = 0.7
FILTER_OMEGA = 0.8
STRENGTH = (RADIUS / (2.0 * math.sqrt(3.0))) ** 2
MESH = pl.DeviceIdType.MESH
NW, NN = 16, 8
CELLS = 128 * 256 * 256
F32 = jnp.float32
BF16 = jnp.bfloat16
N_GROUPS = 18
BLANK_TILES = 200
UNROLL = {48: 4, 32: 8}


def near_peers(reach):
    peers = [
        (dw, dn)
        for dw in range(-reach, reach + 1)
        for dn in (-1, 0, 1)
        if (dw, dn) != (0, 0)
    ]
    return sorted(peers, key=lambda p: (p[1] != 0 and p[0] != 0, p[0] == 0, abs(p[0])))


def greeted():
    peers = [(dw % NW, dn % NN) for dw, dn in near_peers(3)]
    peers += [(0, k) for k in range(1, NN)] + [(k, 0) for k in range(1, NW)]
    return sorted(set(peers), key=lambda p: -min(p[0], NW - p[0]) - min(p[1], NN - p[1]))


def layers(lo, hi, body, unroll):
    steps = (hi - lo) // unroll

    def step(k, carry):
        for j in range(unroll):
            body(lo + k * unroll + j)
        return carry

    if steps > 1:
        lax.fori_loop(0, steps, step, 0)
    else:
        step(0, 0) if steps else None
    for i in range(lo + steps * unroll, hi):
        body(i)


class Group:
    def __init__(self, blank, send_sem, recv_sem):
        self.blank, self.send_sem, self.recv_sem = blank, send_sem, recv_sem
        self.tiles = 0

    def wait(self, sem):
        whole = self.blank.at[pl.ds(0, self.tiles)]
        pltpu.make_async_copy(whole, whole, sem).wait()

    def wait_recv(self):
        self.wait(self.recv_sem)


class Wire:
    def __init__(self, wide, narrow, blank, send_sem, recv_sem):
        self.wide, self.narrow, self.blank = wide, narrow, blank
        self.send_sem, self.recv_sem = send_sem, recv_sem
        self.groups = []
        self.sent = 0

    def peer(self, dw, dn):
        return (lax.rem(self.wide + (dw + NW), NW), lax.rem(self.narrow + (dn + NN), NN))

    def group(self):
        k = len(self.groups)
        self.groups.append(Group(self.blank, self.send_sem.at[k], self.recv_sem.at[k]))
        return self.groups[-1]

    def send(self, group, src, dst, dw, dn):
        pltpu.make_async_remote_copy(
            src_ref=src,
            dst_ref=dst,
            send_sem=group.send_sem,
            recv_sem=group.recv_sem,
            device_id=self.peer(dw, dn),
            device_id_type=MESH,
        ).start()
        group.tiles += math.prod(src.shape) // 1024

    def flush(self, last):
        for group in self.groups[self.sent : last]:
            group.wait(group.send_sem)
        self.sent = last


def cut(own, halo, width, shift):
    if shift == 0:
        return pl.ds(halo, own), pl.ds(halo, own)
    if shift > 0:
        return pl.ds(halo + own - width, width), pl.ds(halo - width, width)
    return pl.ds(halo, width), pl.ds(halo + own, width)


def up_y(v):
    return pltpu.roll(v, v.shape[0] - 1, 0)


def down_y(v):
    return pltpu.roll(v, 1, 0)


def up_z(v):
    return pltpu.roll(v, v.shape[1] - 1, 1)


def down_z(v):
    return pltpu.roll(v, 1, 1)


def coupling(u, ux, uy, uz, i):
    centre = u[i]
    fy, fz = uy[i], uz[i]
    return centre, (
        (ux[i] * u[i + 1] + ux[i - 1] * u[i - 1])
        + (fy * up_y(centre) + down_y(fy * centre))
        + (fz * up_z(centre) + down_z(fz * centre))
    )


def sweep(src, dst, rhs, ux, uy, uz, weight, lo, hi):
    def body(i):
        centre, pull = coupling(src, ux, uy, uz, i)
        dst[i] = (1.0 - OMEGA) * centre + weight[i] * (rhs[i] + pull)

    layers(lo, hi, body, UNROLL[src.shape[1]])


def residual_at(src, rhs, ux, uy, uz, diag, i):
    centre, pull = coupling(src, ux, uy, uz, i)
    return rhs[i] + pull - diag[i] * centre


def weights(sink, ux, uy, uz, diag, weight, lo, hi):
    def body(i):
        fy, fz = uy[i], uz[i]
        total = sink[i] + (ux[i] + ux[i - 1]) + (fy + down_y(fy)) + (fz + down_z(fz))
        diag[i] = total
        weight[i] = OMEGA / total

    layers(lo, hi, body, UNROLL[diag.shape[1]])


def next_x(here, above, low):
    return pltpu.roll(jnp.where(low, above, here), 64, 1)


def previous_x(here, below, low):
    return pltpu.roll(jnp.where(low, here, below), 64, 1)


def coupling2(u, ux, uy, uz, t, low):
    centre, above, below = u[t], u[min(t + 1, 6)], max(t - 1, 0)
    fy, fz = uy[t], uz[t]
    return centre, (
        (
            ux[t] * next_x(centre, above, low)
            + previous_x(ux[t] * centre, ux[below] * u[below], low)
        )
        + (fy * up_y(centre) + down_y(fy * centre))
        + (fz * up_z(centre) + down_z(fz * centre))
    )


def sweep2(src, dst, rhs, ux, uy, uz, weight, low, lo, hi):
    for t in range(lo, hi):
        centre, pull = coupling2(src, ux, uy, uz, t, low)
        dst[t] = (1.0 - OMEGA) * centre + weight[t] * (rhs[t] + pull)


def dot(a, b):
    b = b.astype(BF16)
    high = a.astype(BF16)
    rest = a - high.astype(F32)
    middle = rest.astype(BF16)
    low = (rest - middle.astype(F32)).astype(BF16)
    products = [jnp.dot(part, b, preferred_element_type=F32) for part in (low, middle, high)]
    return products[0] + products[1] + products[2]


def pair_matrix(rows, cols, odd):
    k = lax.broadcasted_iota(jnp.int32, (rows, cols), 0)
    j = lax.broadcasted_iota(jnp.int32, (rows, cols), 1)
    hit = (k == 2 * j + 1) if odd else (k // 2 == j)
    return jnp.where(hit, 1.0, 0.0).astype(F32)


def spread_matrix(rows, cols):
    k = lax.broadcasted_iota(jnp.int32, (rows, cols), 0)
    j = lax.broadcasted_iota(jnp.int32, (rows, cols), 1)
    return jnp.where(k == j // 2, 1.0, 0.0).astype(F32)


def conjugate(rhs, coef_ref, out_ref):
    lane = lax.broadcasted_iota(jnp.int32, (NW, 8, 128), 2)
    low, high = lane < 96, lane >= 32
    sink, ux, uy, uz = (coef_ref[:, k] for k in range(4))

    def y_up(v):
        q = pltpu.roll(v, 96, 2)
        return jnp.where(low, q, pltpu.roll(q, 7, 1))

    def y_down(v):
        q = pltpu.roll(v, 32, 2)
        return jnp.where(high, q, pltpu.roll(q, 1, 1))

    def z_up(v):
        return pltpu.roll(v, 127, 2)

    def z_down(v):
        return pltpu.roll(v, 1, 2)

    def total(v):
        parts = [v[k] for k in range(NW)]
        while len(parts) > 1:
            parts = [x + y for x, y in zip(parts[::2], parts[1::2])]
        return jnp.sum(parts[0], axis=(0, 1), keepdims=True)[None]

    edge = jnp.zeros((1, 8, 128), F32)
    dx = jnp.concatenate([edge, ux[:-1]], axis=0)
    diag = sink + (ux + dx) + (uy + y_down(uy)) + (uz + z_down(uz))

    def apply(p):
        above = jnp.concatenate([p[1:], edge], axis=0)
        px = ux * p
        below = jnp.concatenate([edge, px[:-1]], axis=0)
        return diag * p - (
            (ux * above + below)
            + (uy * y_up(p) + y_down(uy * p))
            + (uz * z_up(p) + z_down(uz * p))
        )

    def body(_, carry):
        solved, residual, direction, norm_now = carry
        applied = apply(direction)
        step = norm_now / total(direction * applied)
        solved = solved + step * direction
        residual = residual - step * applied
        norm_next = total(residual * residual)
        direction = residual + (norm_next / norm_now) * direction
        return solved, residual, direction, norm_next

    start = (jnp.zeros_like(rhs), rhs, rhs, total(rhs * rhs))
    solved, residual, direction, norm_now = lax.fori_loop(0, COARSE_ITERS - 1, body, start)
    step = norm_now / total(direction * apply(direction))
    out_ref[...] = solved + step * direction


def kernel(
    dens_in, temp_in, aim_in, sink_in, adj_out, sens_out,
    dens, temp, aim, sink, ux0, uy0, uz0, d0, w0, ua, ub, v0, zs, lift0,
    stage, pairs,
    c1, f1, v1, d1, w1, p1, q1, lift1,
    c2, f2, v2, d2, w2, p2, q2, lift2,
    ga, gb, ra, rb, solved3, rows3, blank,
    in_sem, send_sem, recv_sem,
):
    wide, narrow = lax.axis_index("wide"), lax.axis_index("narrow")
    wire = Wire(wide, narrow, blank, send_sem, recv_sem)
    barrier = pltpu.get_barrier_semaphore()
    peers = greeted()
    for dw, dn in peers:
        pl.semaphore_signal(barrier, inc=1, device_id=wire.peer(dw, dn), device_id_type=MESH)

    own = (pl.ds(4, 8), pl.ds(8, 32))
    loads = []
    for k, (src, dst) in enumerate(
        ((dens_in, dens.at[own]), (sink_in, sink.at[own]), (aim_in, aim.at[own]),
         (temp_in, temp.at[pl.ds(1, 8), pl.ds(8, 32)]))
    ):
        load = pltpu.make_async_copy(src, dst, in_sem.at[k])
        load.start()
        loads.append(load)
    for load in loads:
        load.wait()
    pl.semaphore_wait(barrier, len(peers))

    def halo(ref, own_x, halo_x, width_x, own_y, lead=(), corner=0, group=None, targets=None):
        group = group or wire.group()
        for dw, dn in targets or near_peers(1):
            sx, tx = cut(own_x, halo_x, corner if corner and dn else width_x, dw)
            sy, ty = cut(own_y, 8, 8, dn)
            wire.send(group, ref.at[lead + (sx, sy)], ref.at[lead + (tx, ty)], dw, dn)
        return group

    sides = [(0, 1), (0, -1)]
    ends = [p for p in near_peers(1) if p[0]]
    beside = wire.group()
    for ref in (dens, sink, aim):
        halo(ref, 8, 4, 4, 32, group=beside, targets=sides)
    first = halo(dens, 8, 4, 4, 32, corner=3, targets=ends)
    second = halo(sink, 8, 4, 3, 32, corner=2, targets=ends)
    third = halo(aim, 8, 4, 3, 32, corner=2, targets=ends)
    temps = wire.group()
    for dw, dn in ((1, 0), (-1, 0), (0, 1), (0, -1)):
        sx, tx = cut(8, 1, 1, dw)
        sy, ty = cut(32, 8, 8, dn)
        wire.send(temps, temp.at[sx, sy], temp.at[tx, ty], dw, dn)

    goal_part = jnp.sum(aim[own] * temp[pl.ds(1, 8), pl.ds(8, 32)], axis=0)
    goal_part = jnp.sum(goal_part[:, :128] + goal_part[:, 128:], axis=0, keepdims=True)

    row0 = narrow * 32 - 8 + lax.broadcasted_iota(jnp.int32, (48, 256), 0)
    lane0 = lax.broadcasted_iota(jnp.int32, (48, 256), 1)
    hy = jnp.where((row0 == -1) | (row0 == 255), 0.0, 0.5).astype(F32)
    hz = jnp.where(lane0 == 255, 0.0, 0.5).astype(F32)

    def hx(i):
        g = wide * 8 - 4 + i
        return jnp.where((g == -1) | (g == 127), 0.0, 0.5).astype(F32)

    def conduct(i):
        s = dens[i]
        return FLOOR_CONDUCTION + (1.0 - FLOOR_CONDUCTION) * s * s * s

    s1, s1_odd = pair_matrix(256, 128, False), pair_matrix(256, 128, True)
    def faces(i):
        c = conduct(i)
        ux0[i] = (c + conduct(i + 1)) * hx(i)
        uy0[i] = (c + up_y(c)) * hy
        uz0[i] = (c + up_z(c)) * hz

    def first0(i):
        ua[i] = w0[i] * aim[i]

    level0 = (ux0, uy0, uz0)

    beside.wait_recv()
    layers(4, 11, faces, 4)
    weights(sink, *level0, d0, w0, 5, 11)
    layers(5, 11, first0, 3)
    sweep(ua, ub, aim, *level0, w0, 6, 10)
    sweep(ub, ua, aim, *level0, w0, 7, 9)

    first.wait_recv()
    ux0[0] = (conduct(0) + conduct(1)) * hx(0)
    layers(1, 4, faces, 3)
    layers(11, 15, faces, 4)

    rows = pl.ds(8, 32)
    for k in range(4):
        a, b = 4 + 2 * k, 5 + 2 * k
        stage[pl.ds(32 * k, 32)] = sink[a, rows] + sink[b, rows]
        stage[pl.ds(128 + 32 * k, 32)] = ux0[b, rows]
        stage[pl.ds(256 + 32 * k, 32)] = uy0[a, rows] + uy0[b, rows]
        stage[pl.ds(384 + 32 * k, 32)] = uz0[a, rows] + uz0[b, rows]
    pairs[pl.ds(0, 384)] = dot(stage[pl.ds(0, 384)], s1)
    pairs[pl.ds(384, 128)] = dot(stage[pl.ds(384, 128)], s1_odd)

    def even_odd(base, size):
        return (
            pairs[pl.ds(base, size // 2, stride=2)],
            pairs[pl.ds(base + 1, size // 2, stride=2)],
        )

    own1 = (pl.ds(6, 4), pl.ds(8, 16))
    for k in range(4):
        even, odd = even_odd(128 * k, 128)
        value = (even + odd, 0.5 * (even + odd), 0.5 * odd, 0.5 * (even + odd))[k]
        c1[(k,) + own1] = value.reshape(4, 16, 128)
    coarse1 = halo(c1, 4, 6, 4, 16, (slice(None),))
    for dn in (0, 1, -1):
        sy, ty = cut(16, 8, 8, dn)
        wire.send(coarse1, c1.at[1, pl.ds(9, 1), sy], c1.at[1, pl.ds(1, 1), ty], 2, dn)

    rows1, rows2 = pl.ds(8, 16), pl.ds(8, 8)
    for k in range(2):
        a, b = 6 + 2 * k, 7 + 2 * k
        half = pl.ds(128 * k, 128)
        stage[pl.ds(0, 16), half] = c1[0, a, rows1] + c1[0, b, rows1]
        stage[pl.ds(16, 16), half] = c1[1, b, rows1]
        stage[pl.ds(32, 16), half] = c1[2, a, rows1] + c1[2, b, rows1]
        stage[pl.ds(48, 16), half] = c1[3, a, rows1] + c1[3, b, rows1]
    pairs[pl.ds(0, 48)] = dot(stage[pl.ds(0, 48)], s1)
    pairs[pl.ds(48, 16)] = dot(stage[pl.ds(48, 16)], s1_odd)
    for k in range(4):
        even, odd = even_odd(16 * k, 16)
        value = (even + odd, 0.5 * (even + odd), 0.5 * odd, 0.5 * (even + odd))[k]
        c2[k, 3, rows2] = value

    def blocks2(ref, lead=()):
        group = wire.group()
        for dw, dn in near_peers(3):
            dst = ref.at[lead + (3 - dw, pl.ds(8 - 8 * dn, 8))]
            wire.send(group, ref.at[lead + (3, rows2)], dst, dw, dn)
        return group

    k3 = lax.broadcasted_iota(jnp.int32, (128, 128), 0)
    j3 = lax.broadcasted_iota(jnp.int32, (128, 128), 1)
    pair3 = (k3 % 64) // 2 == j3 % 32
    s3 = jnp.where(pair3, 1.0, 0.0).astype(F32)
    s3_upper = jnp.where(pair3 & (k3 >= 64), 1.0, 0.0).astype(F32)
    s3_odd = jnp.where(k3 % 64 == 2 * (j3 % 32) + 1, 1.0, 0.0).astype(F32)
    sub8 = lax.broadcasted_iota(jnp.int32, (8, 128), 0)
    lane8 = lax.broadcasted_iota(jnp.int32, (8, 128), 1)
    both_y = sub8 // 2 == lane8 // 32
    odd_y = sub8 == 2 * (lane8 // 32) + 1
    mine = sub8 == narrow

    def as_tile(row):
        return jnp.where(mine, jnp.broadcast_to(row, (8, 128)), 0.0)

    def to_row(values, matrix, mask):
        return jnp.sum(jnp.where(mask, dot(values, matrix), 0.0), axis=0, keepdims=True)

    tiles3 = (
        to_row(c2[0, 3, rows2], s3, both_y),
        0.5 * to_row(c2[1, 3, rows2], s3_upper, both_y),
        0.5 * to_row(c2[2, 3, rows2], s3, odd_y),
        0.5 * to_row(c2[3, 3, rows2], s3_odd, both_y),
        goal_part,
    )
    for k in range(5):
        ga[narrow, k] = as_tile(tiles3[k])
    def along_narrow(ref):
        group = wire.group()
        for dn in range(1, NN):
            wire.send(group, ref.at[narrow], ref.at[narrow], 0, dn)
        return group

    def along_wide(ref):
        group = wire.group()
        for dw in range(1, NW):
            wire.send(group, ref.at[wide], ref.at[wide], dw, 0)
        return group

    gather_a = along_narrow(ga)

    second.wait_recv()
    weights(sink, *level0, d0, w0, 1, 5)
    weights(sink, *level0, d0, w0, 11, 15)
    third.wait_recv()
    layers(1, 5, first0, 4)
    layers(11, 15, first0, 4)
    sweep(ua, ub, aim, *level0, w0, 2, 6)
    sweep(ua, ub, aim, *level0, w0, 10, 14)
    sweep(ub, ua, aim, *level0, w0, 3, 7)
    sweep(ub, ua, aim, *level0, w0, 9, 13)

    def restrict0(k, carry):
        a = 4 + 2 * k
        r = residual_at(ua, aim, ux0, uy0, uz0, d0, a) + residual_at(
            ua, aim, ux0, uy0, uz0, d0, a + 1
        )
        stage[pl.ds(pl.multiple_of(32 * k, 32), 32)] = r[8:40]
        return carry

    lax.fori_loop(0, 4, restrict0, 0)
    pairs[pl.ds(0, 128)] = dot(stage[pl.ds(0, 128)], s1)
    even, odd = even_odd(0, 128)
    f1[own1] = (even + odd).reshape(4, 16, 128)
    right1 = halo(f1, 4, 6, 4, 16)
    v0[own] = ua[own]
    coarse2 = blocks2(c2, (slice(None),))
    gather_a.wait_recv()
    gb[wide] = jnp.sum(ga[...], axis=0)


    coarse1.wait_recv()
    weights(c1.at[0], c1.at[1], c1.at[2], c1.at[3], d1, w1, 2, 14)

    right1.wait_recv()

    level1 = (c1.at[1], c1.at[2], c1.at[3])

    def first1(i):
        p1[i] = w1[i] * f1[i]

    layers(3, 13, first1, 5)
    sweep(p1, q1, f1, *level1, w1, 4, 12)
    sweep(q1, p1, f1, *level1, w1, 5, 11)

    for k in range(2):
        a = 6 + 2 * k
        r = residual_at(p1, f1, *level1, d1, a) + residual_at(p1, f1, *level1, d1, a + 1)
        stage[pl.ds(0, 16), pl.ds(128 * k, 128)] = r[8:24]
    pairs[pl.ds(0, 16)] = dot(stage[pl.ds(0, 16)], s1)
    even, odd = even_odd(0, 16)
    f2[3, rows2] = even + odd
    right2 = blocks2(f2)
    before0 = halo(v0, 8, 4, 4, 32, corner=3)
    gather_b = along_wide(gb)
    coarse2.wait_recv()
    low2 = lax.broadcasted_iota(jnp.int32, (24, 128), 1) < 64
    for t in range(7):
        ux, uy, uz = c2[1, t], c2[2, t], c2[3, t]
        ux = ux + previous_x(ux, c2[1, max(t - 1, 0)], low2)
        d2[t] = c2[0, t] + ux + (uy + down_y(uy)) + (uz + down_z(uz))
        w2[t] = OMEGA / d2[t]

    right2.wait_recv()
    level2 = (c2.at[1], c2.at[2], c2.at[3])

    for t in range(1, 6):
        p2[t] = w2[t] * f2[t]
    sweep2(p2, q2, f2, *level2, w2, low2, 2, 5)
    sweep2(q2, p2, f2, *level2, w2, low2, 2, 5)
    centre, pull = coupling2(p2, *level2, 3, low2)
    r = f2[3] + pull - d2[3] * centre
    old = len(wire.groups)
    ra[narrow] = as_tile(to_row(r[8:16], s3, both_y))
    right3 = along_narrow(ra)
    v2[3, rows2] = p2[3, rows2]
    before2 = blocks2(v2)
    right3.wait_recv()
    rb[wide] = jnp.sum(ra[...], axis=0)
    right3 = along_wide(rb)
    v1[own1] = p1[own1]
    before1 = halo(v1, 4, 6, 4, 16)
    for dw, src, dst in ((2, 9, 1), (-2, 6, 14)):
        for dn in (0, 1, -1):
            sy, ty = cut(16, 8, 8, dn)
            wire.send(before1, v1.at[pl.ds(src, 1), sy], v1.at[pl.ds(dst, 1), ty], dw, dn)
    wire.flush(old)
    gather_b.wait_recv()
    goal = jnp.sum(jnp.sum(gb[:, 4], axis=0), axis=(0, 1), keepdims=True)
    right3.wait_recv()

    conjugate(rb[...], gb, solved3)

    for a in range(7):
        layer = lax.rem(wide + (a - 3 + NW), NW)
        for b in range(3):
            line = lax.rem(narrow + (b - 1 + NN), NN)
            row = jnp.broadcast_to(solved3[layer, pl.ds(line, 1)], (8, 128))
            rows3[pl.ds(24 * a + 8 * b, 8)] = jnp.where(both_y, row, 0.0)
    e3 = jnp.where(k3 % 32 == (j3 % 64) // 2, 1.0, 0.0).astype(F32)
    lift2[...] = dot(rows3[...], e3).reshape(7, 24, 128)
    before2.wait_recv()

    for t in range(7):
        p2[t] = v2[t] + lift2[t]
    sweep2(p2, q2, f2, *level2, w2, low2, 0, 7)
    sweep2(q2, p2, f2, *level2, w2, low2, 1, 6)
    sweep2(p2, q2, f2, *level2, w2, low2, 1, 6)

    e1 = spread_matrix(128, 256)
    lift = dot(q2[pl.ds(1, 5)].reshape(120, 128), e1).reshape(5, 24, 256)
    for t in range(5):
        for half in range(2):
            part = lift[t, 4:20, 128 * half : 128 * half + 128]
            lift1[2 * t + half, pl.ds(0, 16, stride=2)] = part
            lift1[2 * t + half, pl.ds(1, 16, stride=2)] = part
    before1.wait_recv()

    for i in range(1, 15):
        p1[i] = v1[i] + lift1[1 + i // 2]
    sweep(p1, q1, f1, *level1, w1, 2, 14)
    sweep(q1, p1, f1, *level1, w1, 3, 13)
    sweep(p1, q1, f1, *level1, w1, 4, 12)

    lift = dot(q1[pl.ds(4, 8), pl.ds(0, 32)].reshape(256, 128), e1).reshape(8, 32, 256)
    before0.wait_recv()
    for a in range(8):
        for half in range(2):
            part = lift[a, 4:28, 128 * half : 128 * half + 128]
            lift0[a, half, pl.ds(0, 24, stride=2)] = part
            lift0[a, half, pl.ds(1, 24, stride=2)] = part

    def correct0(k):
        both = jnp.concatenate([lift0[k, 0], lift0[k, 1]], axis=1)
        ua[2 * k] = v0[2 * k] + both
        ua[2 * k + 1] = v0[2 * k + 1] + both

    layers(0, 8, correct0, 4)
    sweep(ua, ub, aim, ux0, uy0, uz0, w0, 1, 15)
    sweep(ub, ua, aim, ux0, uy0, uz0, w0, 2, 14)

    temps.wait_recv()
    scale = (-0.5 * 3.0 * (1.0 - FLOOR_CONDUCTION)) * (CELLS / goal)
    my, mz = 2.0 * hy, 2.0 * hz

    def face_x(i):
        return (temp[i - 3] - temp[i - 2]) * (ub[i] - ub[i + 1]) * (2.0 * hx(i))

    def slope(i, below):
        t, a, s = temp[i - 3], ub[i], dens[i]
        above = face_x(i)
        fy = (t - up_y(t)) * (a - up_y(a)) * my
        fz = (t - up_z(t)) * (a - up_z(a)) * mz
        raw = (above + below) + (fy + down_y(fy)) + (fz + down_z(fz))
        zs[i, pl.ds(8, 32)] = (raw * scale * s * s)[8:40]
        return above

    sweep(ua, ub, aim, *level0, w0, 3, 9)
    below = face_x(3)
    for i in range(4, 8):
        below = slope(i, below)
    scaled = halo(zs, 8, 4, 4, 32, corner=3, targets=[p for p in ends if p[0] < 0])
    sweep(ua, ub, aim, *level0, w0, 9, 13)
    for i in range(8, 12):
        below = slope(i, below)
    halo(zs, 8, 4, 4, 32, corner=3, group=scaled, targets=[p for p in ends if p[0] > 0])
    scaled_beside = halo(zs, 8, 4, 4, 32, targets=sides)
    adj_out[...] = ub[own]

    first_layer = jnp.where(wide == 0, 4, 0)
    last_layer = jnp.where(wide == NW - 1, 11, 15)
    top, bottom = row0 == 255, row0 == 0
    right, left = lane0 == 255, lane0 == 0
    c1_filter = FILTER_OMEGA / (1.0 + 6.0 * STRENGTH)

    def filter_at(src, i):
        z = src[i]
        near = src[jnp.minimum(i + 1, last_layer)] + src[jnp.maximum(i - 1, first_layer)]
        near = near + (jnp.where(top, z, up_y(z)) + jnp.where(bottom, z, down_y(z)))
        near = near + (jnp.where(right, z, up_z(z)) + jnp.where(left, z, down_z(z)))
        return (1.0 - FILTER_OMEGA) * z + c1_filter * (zs[i] + STRENGTH * near)

    def filter_sweep(src, dst, lo, hi):
        def body(i):
            dst[i] = filter_at(src, i)

        layers(lo, hi, body, 4)

    scaled_beside.wait_recv()
    filter_sweep(zs, ua, 5, 11)
    filter_sweep(ua, ub, 6, 10)
    filter_sweep(ub, ua, 7, 9)
    scaled.wait_recv()
    filter_sweep(zs, ua, 1, 5)
    filter_sweep(zs, ua, 11, 15)
    filter_sweep(ua, ub, 2, 6)
    filter_sweep(ua, ub, 10, 14)
    filter_sweep(ub, ua, 3, 7)
    filter_sweep(ub, ua, 9, 13)

    def last_filter(i):
        sens_out[i - 4] = filter_at(ua, i)[8:40]

    layers(4, 12, last_filter, 4)
    wire.flush(len(wire.groups))


def local(density, temperature, aim, sink):
    vmem = lambda *shape: pltpu.VMEM(shape, F32)
    level0 = (16, 48, 256)
    level1 = (16, 32, 128)
    level2 = (7, 24, 128)
    scratch = [vmem(*level0), vmem(10, 48, 256)] + [vmem(*level0)] * 11 + [vmem(8, 2, 48, 128)]
    scratch += [vmem(512, 256), vmem(512, 128)]
    scratch += [vmem(4, *level1)] + [vmem(*level1)] * 6 + [vmem(10, 32, 128)]
    scratch += [vmem(4, *level2)] + [vmem(*level2)] * 6 + [vmem(7, 24, 128)]
    scratch += [vmem(NN, 5, 8, 128), vmem(NW, 5, 8, 128), vmem(NN, 8, 128), vmem(NW, 8, 128)]
    scratch += [vmem(NW, 8, 128), vmem(168, 128), vmem(BLANK_TILES, 8, 128)]
    scratch += [
        pltpu.SemaphoreType.DMA((4,)),
        pltpu.SemaphoreType.DMA((N_GROUPS,)),
        pltpu.SemaphoreType.DMA((N_GROUPS,)),
    ]
    block = jax.ShapeDtypeStruct((8, 32, 256), F32)
    whole = pl.BlockSpec(memory_space=pltpu.VMEM)
    return pl.pallas_call(
        kernel,
        out_shape=(block, block),
        in_specs=[pl.BlockSpec(memory_space=pl.ANY)] * 4,
        out_specs=(whole, whole),
        scratch_shapes=scratch,
        compiler_params=pltpu.CompilerParams(
            collective_id=0, has_side_effects=True, vmem_limit_bytes=62 * 2**20
        ),
    )(density, temperature, aim, sink)


def solution(mesh):
    placed = P("wide", "narrow", None)
    return jax.shard_map(
        local,
        mesh=mesh,
        in_specs=(placed,) * 4,
        out_specs=(placed, placed),
        check_vma=False,
    )
```

```python
import functools
import math

import jax
import jax.numpy as jnp
from jax import lax
from jax.experimental import pallas as pl
from jax.experimental.pallas import tpu as pltpu
from jax.sharding import PartitionSpec as P

COARSE_ITERS = 8
RADIUS = 4
FLOOR_CONDUCTION = 0.001
OMEGA = 0.7
FILTER_OMEGA = 0.8
STRENGTH = (RADIUS / (2.0 * math.sqrt(3.0))) ** 2
MESH = pl.DeviceIdType.MESH
NW, NN = 16, 8
CELLS = 128 * 256 * 256
F32 = jnp.float32
BF16 = jnp.bfloat16
N_GROUPS = 19
BLANK_TILES = 200
UNROLL = {48: 4, 32: 8}


def near_peers(reach):
    peers = [
        (dw, dn)
        for dw in range(-reach, reach + 1)
        for dn in (-1, 0, 1)
        if (dw, dn) != (0, 0)
    ]
    return sorted(peers, key=lambda p: (p[1] != 0 and p[0] != 0, p[0] == 0, abs(p[0])))


def greeted():
    peers = [(dw % NW, dn % NN) for dw, dn in near_peers(3)]
    peers += [(0, k) for k in range(1, NN)] + [(k, 0) for k in range(1, NW)]
    return sorted(set(peers), key=lambda p: -min(p[0], NW - p[0]) - min(p[1], NN - p[1]))


def layers(lo, hi, body, unroll):
    steps = (hi - lo) // unroll

    def step(k, carry):
        for j in range(unroll):
            body(lo + k * unroll + j)
        return carry

    if steps > 1:
        lax.fori_loop(0, steps, step, 0)
    else:
        step(0, 0) if steps else None
    for i in range(lo + steps * unroll, hi):
        body(i)


class Group:
    def __init__(self, blank, send_sem, recv_sem):
        self.blank, self.send_sem, self.recv_sem = blank, send_sem, recv_sem
        self.tiles = 0

    def wait(self, sem):
        whole = self.blank.at[pl.ds(0, self.tiles)]
        pltpu.make_async_copy(whole, whole, sem).wait()

    def wait_recv(self):
        self.wait(self.recv_sem)


class Wire:
    def __init__(self, wide, narrow, blank, send_sem, recv_sem):
        self.wide, self.narrow, self.blank = wide, narrow, blank
        self.send_sem, self.recv_sem = send_sem, recv_sem
        self.groups = []
        self.sent = 0

    def peer(self, dw, dn):
        return (lax.rem(self.wide + (dw + NW), NW), lax.rem(self.narrow + (dn + NN), NN))

    def group(self):
        k = len(self.groups)
        self.groups.append(Group(self.blank, self.send_sem.at[k], self.recv_sem.at[k]))
        return self.groups[-1]

    def send(self, group, src, dst, dw, dn):
        pltpu.make_async_remote_copy(
            src_ref=src,
            dst_ref=dst,
            send_sem=group.send_sem,
            recv_sem=group.recv_sem,
            device_id=self.peer(dw, dn),
            device_id_type=MESH,
        ).start()
        group.tiles += math.prod(src.shape) // 1024

    def flush(self, last):
        for group in self.groups[self.sent : last]:
            group.wait(group.send_sem)
        self.sent = last


def cut(own, halo, width, shift):
    if shift == 0:
        return pl.ds(halo, own), pl.ds(halo, own)
    if shift > 0:
        return pl.ds(halo + own - width, width), pl.ds(halo - width, width)
    return pl.ds(halo, width), pl.ds(halo + own, width)


def up_y(v):
    return pltpu.roll(v, v.shape[0] - 1, 0)


def down_y(v):
    return pltpu.roll(v, 1, 0)


def up_z(v):
    return pltpu.roll(v, v.shape[1] - 1, 1)


def down_z(v):
    return pltpu.roll(v, 1, 1)


def coupling(u, ux, uy, uz, i):
    centre = u[i]
    fy, fz = uy[i], uz[i]
    return centre, (
        (ux[i] * u[i + 1] + ux[i - 1] * u[i - 1])
        + (fy * up_y(centre) + down_y(fy * centre))
        + (fz * up_z(centre) + down_z(fz * centre))
    )


def sweep(src, dst, rhs, ux, uy, uz, weight, lo, hi):
    def body(i):
        centre, pull = coupling(src, ux, uy, uz, i)
        dst[i] = (1.0 - OMEGA) * centre + weight[i] * (rhs[i] + pull)

    layers(lo, hi, body, UNROLL[src.shape[1]])


def residual_at(src, rhs, ux, uy, uz, diag, i):
    centre, pull = coupling(src, ux, uy, uz, i)
    return rhs[i] + pull - diag[i] * centre


def weights(sink, ux, uy, uz, diag, weight, lo, hi):
    def body(i):
        fy, fz = uy[i], uz[i]
        total = sink[i] + (ux[i] + ux[i - 1]) + (fy + down_y(fy)) + (fz + down_z(fz))
        diag[i] = total
        weight[i] = OMEGA / total

    layers(lo, hi, body, UNROLL[diag.shape[1]])


def next_x(here, above, low):
    return pltpu.roll(jnp.where(low, above, here), 64, 1)


def previous_x(here, below, low):
    return pltpu.roll(jnp.where(low, here, below), 64, 1)


def coupling2(u, ux, uy, uz, t, low):
    centre, above, below = u[t], u[min(t + 1, 6)], max(t - 1, 0)
    fy, fz = uy[t], uz[t]
    return centre, (
        (
            ux[t] * next_x(centre, above, low)
            + previous_x(ux[t] * centre, ux[below] * u[below], low)
        )
        + (fy * up_y(centre) + down_y(fy * centre))
        + (fz * up_z(centre) + down_z(fz * centre))
    )


def sweep2(src, dst, rhs, ux, uy, uz, weight, low, lo, hi):
    for t in range(lo, hi):
        centre, pull = coupling2(src, ux, uy, uz, t, low)
        dst[t] = (1.0 - OMEGA) * centre + weight[t] * (rhs[t] + pull)


def dot(a, b):
    b = b.astype(BF16)
    high = a.astype(BF16)
    rest = a - high.astype(F32)
    middle = rest.astype(BF16)
    low = (rest - middle.astype(F32)).astype(BF16)
    products = [jnp.dot(part, b, preferred_element_type=F32) for part in (low, middle, high)]
    return products[0] + products[1] + products[2]


def pair_matrix(rows, cols, odd):
    k = lax.broadcasted_iota(jnp.int32, (rows, cols), 0)
    j = lax.broadcasted_iota(jnp.int32, (rows, cols), 1)
    hit = (k == 2 * j + 1) if odd else (k // 2 == j)
    return jnp.where(hit, 1.0, 0.0).astype(F32)


def spread_matrix(rows, cols):
    k = lax.broadcasted_iota(jnp.int32, (rows, cols), 0)
    j = lax.broadcasted_iota(jnp.int32, (rows, cols), 1)
    return jnp.where(k == j // 2, 1.0, 0.0).astype(F32)


def conjugate(rhs, coef_ref, out_ref):
    lane = lax.broadcasted_iota(jnp.int32, (NW, 8, 128), 2)
    low, high = lane < 96, lane >= 32
    sink, ux, uy, uz = (coef_ref[:, k] for k in range(4))

    def y_up(v):
        q = pltpu.roll(v, 96, 2)
        return jnp.where(low, q, pltpu.roll(q, 7, 1))

    def y_down(v):
        q = pltpu.roll(v, 32, 2)
        return jnp.where(high, q, pltpu.roll(q, 1, 1))

    def z_up(v):
        return pltpu.roll(v, 127, 2)

    def z_down(v):
        return pltpu.roll(v, 1, 2)

    def total(v):
        parts = [v[k] for k in range(NW)]
        while len(parts) > 1:
            parts = [x + y for x, y in zip(parts[::2], parts[1::2])]
        return jnp.sum(parts[0], axis=(0, 1), keepdims=True)[None]

    edge = jnp.zeros((1, 8, 128), F32)
    dx = jnp.concatenate([edge, ux[:-1]], axis=0)
    diag = sink + (ux + dx) + (uy + y_down(uy)) + (uz + z_down(uz))

    def apply(p):
        above = jnp.concatenate([p[1:], edge], axis=0)
        px = ux * p
        below = jnp.concatenate([edge, px[:-1]], axis=0)
        return diag * p - (
            (ux * above + below)
            + (uy * y_up(p) + y_down(uy * p))
            + (uz * z_up(p) + z_down(uz * p))
        )

    def body(_, carry):
        solved, residual, direction, norm_now = carry
        applied = apply(direction)
        step = norm_now / total(direction * applied)
        solved = solved + step * direction
        residual = residual - step * applied
        norm_next = total(residual * residual)
        direction = residual + (norm_next / norm_now) * direction
        return solved, residual, direction, norm_next

    start = (jnp.zeros_like(rhs), rhs, rhs, total(rhs * rhs))
    solved, residual, direction, norm_now = lax.fori_loop(0, COARSE_ITERS - 1, body, start)
    step = norm_now / total(direction * apply(direction))
    out_ref[...] = solved + step * direction


def kernel(
    dens_in, temp_in, aim_in, sink_in, outs,
    dens, temp, aim, sink, ux0, uy0, uz0, d0, w0, ua, ub, v0, zs, lift0,
    stage, pairs,
    c1, f1, v1, d1, w1, p1, q1, lift1,
    c2, f2, v2, d2, w2, p2, q2, lift2,
    ga, gb, ra, rb, solved3, rows3, blank, corner_out, corner_in,
    in_sem, send_sem, recv_sem,
):
    wide, narrow = lax.axis_index("wide"), lax.axis_index("narrow")
    wire = Wire(wide, narrow, blank, send_sem, recv_sem)
    barrier = pltpu.get_barrier_semaphore()
    peers = greeted()
    for dw, dn in peers:
        pl.semaphore_signal(barrier, inc=1, device_id=wire.peer(dw, dn), device_id_type=MESH)

    own = (pl.ds(4, 8), pl.ds(8, 32))
    loads = []
    for k, (src, dst) in enumerate(
        ((dens_in, dens.at[own]), (sink_in, sink.at[own]), (aim_in, aim.at[own]),
         (temp_in, temp.at[pl.ds(1, 8), pl.ds(8, 32)]))
    ):
        load = pltpu.make_async_copy(src, dst, in_sem.at[k])
        load.start()
        loads.append(load)
    for load in loads:
        load.wait()
    pl.semaphore_wait(barrier, len(peers))

    def halo(ref, own_x, halo_x, width_x, own_y, lead=(), corner=0, group=None, targets=None):
        group = group or wire.group()
        for dw, dn in targets or near_peers(1):
            sx, tx = cut(own_x, halo_x, corner if corner and dn else width_x, dw)
            sy, ty = cut(own_y, 8, 8, dn)
            wire.send(group, ref.at[lead + (sx, sy)], ref.at[lead + (tx, ty)], dw, dn)
        return group

    sides = [(0, 1), (0, -1)]
    ends = [p for p in near_peers(1) if p[0]]
    beside = wire.group()
    for ref in (dens, sink, aim):
        halo(ref, 8, 4, 4, 32, group=beside, targets=sides)
    straight = [p for p in ends if not p[1]]
    corners = [p for p in ends if p[1]]
    first = halo(dens, 8, 4, 4, 32, targets=straight)

    row8 = lax.broadcasted_iota(jnp.int32, (8, 256), 0)
    packed = wire.group()
    for q, (dw, dn) in enumerate(corners):
        edge = pl.ds(32, 8) if dn > 0 else pl.ds(8, 8)
        for j in range(3):
            layer = (9 if dw > 0 else 4) + j
            d, s, a = dens[layer, edge], sink[layer, edge], aim[layer, edge]
            if dn > 0:
                rest = jnp.where(row8 >= 3, pltpu.roll(s, 5, 0), pltpu.roll(a, 3, 0))
                corner_out[q, j] = jnp.where(row8 >= 5, d, rest)
            else:
                rest = jnp.where(row8 < 5, pltpu.roll(s, 3, 0), pltpu.roll(a, 5, 0))
                corner_out[q, j] = jnp.where(row8 < 3, d, rest)
        wire.send(packed, corner_out.at[q], corner_in.at[q], dw, dn)
    second = halo(sink, 8, 4, 3, 32, targets=straight)
    third = halo(aim, 8, 4, 3, 32, targets=straight)
    temps = wire.group()
    for dw, dn in ((1, 0), (-1, 0), (0, 1), (0, -1)):
        sx, tx = cut(8, 1, 1, dw)
        sy, ty = cut(32, 8, 8, dn)
        wire.send(temps, temp.at[sx, sy], temp.at[tx, ty], dw, dn)

    goal_part = jnp.sum(aim[own] * temp[pl.ds(1, 8), pl.ds(8, 32)], axis=0)
    goal_part = jnp.sum(goal_part[:, :128] + goal_part[:, 128:], axis=0, keepdims=True)

    row0 = narrow * 32 - 8 + lax.broadcasted_iota(jnp.int32, (48, 256), 0)
    lane0 = lax.broadcasted_iota(jnp.int32, (48, 256), 1)
    hy = jnp.where((row0 == -1) | (row0 == 255), 0.0, 0.5).astype(F32)
    hz = jnp.where(lane0 == 255, 0.0, 0.5).astype(F32)

    def hx(i):
        g = wide * 8 - 4 + i
        return jnp.where((g == -1) | (g == 127), 0.0, 0.5).astype(F32)

    def conduct(i):
        s = dens[i]
        return FLOOR_CONDUCTION + (1.0 - FLOOR_CONDUCTION) * s * s * s

    s1, s1_odd = pair_matrix(256, 128, False), pair_matrix(256, 128, True)
    def faces(i):
        c = conduct(i)
        ux0[i] = (c + conduct(i + 1)) * hx(i)
        uy0[i] = (c + up_y(c)) * hy
        uz0[i] = (c + up_z(c)) * hz

    def first0(i):
        ua[i] = w0[i] * aim[i]

    level0 = (ux0, uy0, uz0)

    beside.wait_recv()
    layers(4, 11, faces, 4)
    weights(sink, *level0, d0, w0, 5, 11)
    layers(5, 11, first0, 3)
    sweep(ua, ub, aim, *level0, w0, 6, 10)
    sweep(ub, ua, aim, *level0, w0, 7, 9)

    first.wait_recv()
    packed.wait_recv()
    for q, (dw, dn) in enumerate(corners):
        edge = pl.ds(0, 8) if dn > 0 else pl.ds(40, 8)
        for j in range(3):
            layer = (1 if dw > 0 else 12) + j
            tile = corner_in[q, j]
            dens[layer, edge] = tile
            if j != (0 if dw > 0 else 2):
                sink[layer, edge] = pltpu.roll(tile, 3 if dn > 0 else 5, 0)
                aim[layer, edge] = pltpu.roll(tile, 5 if dn > 0 else 3, 0)
    ux0[0] = (conduct(0) + conduct(1)) * hx(0)
    layers(1, 4, faces, 3)
    layers(11, 15, faces, 4)

    rows = pl.ds(8, 32)
    for k in range(4):
        a, b = 4 + 2 * k, 5 + 2 * k
        stage[pl.ds(32 * k, 32)] = sink[a, rows] + sink[b, rows]
        stage[pl.ds(128 + 32 * k, 32)] = ux0[b, rows]
        stage[pl.ds(256 + 32 * k, 32)] = uy0[a, rows] + uy0[b, rows]
        stage[pl.ds(384 + 32 * k, 32)] = uz0[a, rows] + uz0[b, rows]
    pairs[pl.ds(0, 384)] = dot(stage[pl.ds(0, 384)], s1)
    pairs[pl.ds(384, 128)] = dot(stage[pl.ds(384, 128)], s1_odd)

    def even_odd(base, size):
        return (
            pairs[pl.ds(base, size // 2, stride=2)],
            pairs[pl.ds(base + 1, size // 2, stride=2)],
        )

    own1 = (pl.ds(6, 4), pl.ds(8, 16))
    for k in range(4):
        even, odd = even_odd(128 * k, 128)
        value = (even + odd, 0.5 * (even + odd), 0.5 * odd, 0.5 * (even + odd))[k]
        c1[(k,) + own1] = value.reshape(4, 16, 128)
    coarse1 = halo(c1, 4, 6, 4, 16, (slice(None),))
    for dn in (0, 1, -1):
        sy, ty = cut(16, 8, 8, dn)
        wire.send(coarse1, c1.at[1, pl.ds(9, 1), sy], c1.at[1, pl.ds(1, 1), ty], 2, dn)

    rows1, rows2 = pl.ds(8, 16), pl.ds(8, 8)
    for k in range(2):
        a, b = 6 + 2 * k, 7 + 2 * k
        half = pl.ds(128 * k, 128)
        stage[pl.ds(0, 16), half] = c1[0, a, rows1] + c1[0, b, rows1]
        stage[pl.ds(16, 16), half] = c1[1, b, rows1]
        stage[pl.ds(32, 16), half] = c1[2, a, rows1] + c1[2, b, rows1]
        stage[pl.ds(48, 16), half] = c1[3, a, rows1] + c1[3, b, rows1]
    pairs[pl.ds(0, 48)] = dot(stage[pl.ds(0, 48)], s1)
    pairs[pl.ds(48, 16)] = dot(stage[pl.ds(48, 16)], s1_odd)
    for k in range(4):
        even, odd = even_odd(16 * k, 16)
        value = (even + odd, 0.5 * (even + odd), 0.5 * odd, 0.5 * (even + odd))[k]
        c2[k, 3, rows2] = value

    def blocks2(ref, lead=()):
        group = wire.group()
        for dw, dn in near_peers(3):
            dst = ref.at[lead + (3 - dw, pl.ds(8 - 8 * dn, 8))]
            wire.send(group, ref.at[lead + (3, rows2)], dst, dw, dn)
        return group

    k3 = lax.broadcasted_iota(jnp.int32, (128, 128), 0)
    j3 = lax.broadcasted_iota(jnp.int32, (128, 128), 1)
    pair3 = (k3 % 64) // 2 == j3 % 32
    s3 = jnp.where(pair3, 1.0, 0.0).astype(F32)
    s3_upper = jnp.where(pair3 & (k3 >= 64), 1.0, 0.0).astype(F32)
    s3_odd = jnp.where(k3 % 64 == 2 * (j3 % 32) + 1, 1.0, 0.0).astype(F32)
    sub8 = lax.broadcasted_iota(jnp.int32, (8, 128), 0)
    lane8 = lax.broadcasted_iota(jnp.int32, (8, 128), 1)
    both_y = sub8 // 2 == lane8 // 32
    odd_y = sub8 == 2 * (lane8 // 32) + 1
    mine = sub8 == narrow

    def as_tile(row):
        return jnp.where(mine, jnp.broadcast_to(row, (8, 128)), 0.0)

    def to_row(values, matrix, mask):
        return jnp.sum(jnp.where(mask, dot(values, matrix), 0.0), axis=0, keepdims=True)

    tiles3 = (
        to_row(c2[0, 3, rows2], s3, both_y),
        0.5 * to_row(c2[1, 3, rows2], s3_upper, both_y),
        0.5 * to_row(c2[2, 3, rows2], s3, odd_y),
        0.5 * to_row(c2[3, 3, rows2], s3_odd, both_y),
        goal_part,
    )
    for k in range(5):
        ga[narrow, k] = as_tile(tiles3[k])
    def along_narrow(ref):
        group = wire.group()
        for dn in range(1, NN):
            wire.send(group, ref.at[narrow], ref.at[narrow], 0, dn)
        return group

    def along_wide(ref):
        group = wire.group()
        for dw in range(1, NW):
            wire.send(group, ref.at[wide], ref.at[wide], dw, 0)
        return group

    gather_a = along_narrow(ga)

    second.wait_recv()
    weights(sink, *level0, d0, w0, 1, 5)
    weights(sink, *level0, d0, w0, 11, 15)
    third.wait_recv()
    layers(1, 5, first0, 4)
    layers(11, 15, first0, 4)
    sweep(ua, ub, aim, *level0, w0, 2, 6)
    sweep(ua, ub, aim, *level0, w0, 10, 14)
    sweep(ub, ua, aim, *level0, w0, 3, 7)
    sweep(ub, ua, aim, *level0, w0, 9, 13)

    def restrict0(k, carry):
        a = 4 + 2 * k
        r = residual_at(ua, aim, ux0, uy0, uz0, d0, a) + residual_at(
            ua, aim, ux0, uy0, uz0, d0, a + 1
        )
        stage[pl.ds(pl.multiple_of(32 * k, 32), 32)] = r[8:40]
        return carry

    lax.fori_loop(0, 4, restrict0, 0)
    pairs[pl.ds(0, 128)] = dot(stage[pl.ds(0, 128)], s1)
    even, odd = even_odd(0, 128)
    f1[own1] = (even + odd).reshape(4, 16, 128)
    right1 = halo(f1, 4, 6, 4, 16)
    v0[own] = ua[own]
    coarse2 = blocks2(c2, (slice(None),))
    gather_a.wait_recv()
    gb[wide] = jnp.sum(ga[...], axis=0)


    coarse1.wait_recv()
    weights(c1.at[0], c1.at[1], c1.at[2], c1.at[3], d1, w1, 2, 14)

    right1.wait_recv()

    level1 = (c1.at[1], c1.at[2], c1.at[3])

    def first1(i):
        p1[i] = w1[i] * f1[i]

    layers(3, 13, first1, 5)
    sweep(p1, q1, f1, *level1, w1, 4, 12)
    sweep(q1, p1, f1, *level1, w1, 5, 11)

    for k in range(2):
        a = 6 + 2 * k
        r = residual_at(p1, f1, *level1, d1, a) + residual_at(p1, f1, *level1, d1, a + 1)
        stage[pl.ds(0, 16), pl.ds(128 * k, 128)] = r[8:24]
    pairs[pl.ds(0, 16)] = dot(stage[pl.ds(0, 16)], s1)
    even, odd = even_odd(0, 16)
    f2[3, rows2] = even + odd
    right2 = blocks2(f2)
    before0 = halo(v0, 8, 4, 4, 32, corner=3)
    gather_b = along_wide(gb)
    coarse2.wait_recv()
    low2 = lax.broadcasted_iota(jnp.int32, (24, 128), 1) < 64
    for t in range(7):
        ux, uy, uz = c2[1, t], c2[2, t], c2[3, t]
        ux = ux + previous_x(ux, c2[1, max(t - 1, 0)], low2)
        d2[t] = c2[0, t] + ux + (uy + down_y(uy)) + (uz + down_z(uz))
        w2[t] = OMEGA / d2[t]

    right2.wait_recv()
    level2 = (c2.at[1], c2.at[2], c2.at[3])

    for t in range(1, 6):
        p2[t] = w2[t] * f2[t]
    sweep2(p2, q2, f2, *level2, w2, low2, 2, 5)
    sweep2(q2, p2, f2, *level2, w2, low2, 2, 5)
    centre, pull = coupling2(p2, *level2, 3, low2)
    r = f2[3] + pull - d2[3] * centre
    old = len(wire.groups)
    ra[narrow] = as_tile(to_row(r[8:16], s3, both_y))
    right3 = along_narrow(ra)
    v2[3, rows2] = p2[3, rows2]
    before2 = blocks2(v2)
    right3.wait_recv()
    rb[wide] = jnp.sum(ra[...], axis=0)
    right3 = along_wide(rb)
    v1[own1] = p1[own1]
    before1 = halo(v1, 4, 6, 4, 16)
    for dw, src, dst in ((2, 9, 1), (-2, 6, 14)):
        for dn in (0, 1, -1):
            sy, ty = cut(16, 8, 8, dn)
            wire.send(before1, v1.at[pl.ds(src, 1), sy], v1.at[pl.ds(dst, 1), ty], dw, dn)
    wire.flush(old)
    gather_b.wait_recv()
    goal = jnp.sum(jnp.sum(gb[:, 4], axis=0), axis=(0, 1), keepdims=True)
    right3.wait_recv()

    conjugate(rb[...], gb, solved3)

    for a in range(7):
        layer = lax.rem(wide + (a - 3 + NW), NW)
        for b in range(3):
            line = lax.rem(narrow + (b - 1 + NN), NN)
            row = jnp.broadcast_to(solved3[layer, pl.ds(line, 1)], (8, 128))
            rows3[pl.ds(24 * a + 8 * b, 8)] = jnp.where(both_y, row, 0.0)
    e3 = jnp.where(k3 % 32 == (j3 % 64) // 2, 1.0, 0.0).astype(F32)
    lift2[...] = dot(rows3[...], e3).reshape(7, 24, 128)
    before2.wait_recv()

    for t in range(7):
        p2[t] = v2[t] + lift2[t]
    sweep2(p2, q2, f2, *level2, w2, low2, 0, 7)
    sweep2(q2, p2, f2, *level2, w2, low2, 1, 6)
    sweep2(p2, q2, f2, *level2, w2, low2, 1, 6)

    e1 = spread_matrix(128, 256)
    lift = dot(q2[pl.ds(1, 5)].reshape(120, 128), e1).reshape(5, 24, 256)
    for t in range(5):
        for half in range(2):
            part = lift[t, 4:20, 128 * half : 128 * half + 128]
            lift1[2 * t + half, pl.ds(0, 16, stride=2)] = part
            lift1[2 * t + half, pl.ds(1, 16, stride=2)] = part
    before1.wait_recv()

    for i in range(1, 15):
        p1[i] = v1[i] + lift1[1 + i // 2]
    sweep(p1, q1, f1, *level1, w1, 2, 14)
    sweep(q1, p1, f1, *level1, w1, 3, 13)
    sweep(p1, q1, f1, *level1, w1, 4, 12)

    lift = dot(q1[pl.ds(4, 8), pl.ds(0, 32)].reshape(256, 128), e1).reshape(8, 32, 256)
    before0.wait_recv()
    for a in range(8):
        for half in range(2):
            part = lift[a, 4:28, 128 * half : 128 * half + 128]
            lift0[a, half, pl.ds(0, 24, stride=2)] = part
            lift0[a, half, pl.ds(1, 24, stride=2)] = part

    def correct0(k):
        both = jnp.concatenate([lift0[k, 0], lift0[k, 1]], axis=1)
        ua[2 * k] = v0[2 * k] + both
        ua[2 * k + 1] = v0[2 * k + 1] + both

    layers(0, 8, correct0, 4)
    sweep(ua, ub, aim, ux0, uy0, uz0, w0, 1, 15)
    sweep(ub, ua, aim, ux0, uy0, uz0, w0, 2, 14)

    temps.wait_recv()
    scale = (-0.5 * 3.0 * (1.0 - FLOOR_CONDUCTION)) * (CELLS / goal)
    my, mz = 2.0 * hy, 2.0 * hz

    def face_x(i):
        return (temp[i - 3] - temp[i - 2]) * (ub[i] - ub[i + 1]) * (2.0 * hx(i))

    def slope(i, below):
        t, a, s = temp[i - 3], ub[i], dens[i]
        above = face_x(i)
        fy = (t - up_y(t)) * (a - up_y(a)) * my
        fz = (t - up_z(t)) * (a - up_z(a)) * mz
        raw = (above + below) + (fy + down_y(fy)) + (fz + down_z(fz))
        zs[i, pl.ds(8, 32)] = (raw * scale * s * s)[8:40]
        return above

    sweep(ua, ub, aim, *level0, w0, 3, 9)
    below = face_x(3)
    for i in range(4, 8):
        below = slope(i, below)
    scaled = halo(zs, 8, 4, 4, 32, corner=3, targets=[p for p in ends if p[0] < 0])
    sweep(ua, ub, aim, *level0, w0, 9, 13)
    for i in range(8, 12):
        below = slope(i, below)
    halo(zs, 8, 4, 4, 32, corner=3, group=scaled, targets=[p for p in ends if p[0] > 0])
    scaled_beside = halo(zs, 8, 4, 4, 32, targets=sides)
    v0[own] = ub[own]
    store_adj = pltpu.make_async_copy(v0.at[own], outs.at[0], in_sem.at[0])
    store_adj.start()

    first_layer = jnp.where(wide == 0, 4, 0)
    last_layer = jnp.where(wide == NW - 1, 11, 15)
    top, bottom = row0 == 255, row0 == 0
    right, left = lane0 == 255, lane0 == 0
    c1_filter = FILTER_OMEGA / (1.0 + 6.0 * STRENGTH)

    def filter_at(src, i):
        z = src[i]
        near = src[jnp.minimum(i + 1, last_layer)] + src[jnp.maximum(i - 1, first_layer)]
        near = near + (jnp.where(top, z, up_y(z)) + jnp.where(bottom, z, down_y(z)))
        near = near + (jnp.where(right, z, up_z(z)) + jnp.where(left, z, down_z(z)))
        return (1.0 - FILTER_OMEGA) * z + c1_filter * (zs[i] + STRENGTH * near)

    def filter_sweep(src, dst, lo, hi):
        def body(i):
            dst[i] = filter_at(src, i)

        layers(lo, hi, body, 4)

    scaled_beside.wait_recv()
    filter_sweep(zs, ua, 5, 11)
    filter_sweep(ua, ub, 6, 10)
    filter_sweep(ub, ua, 7, 9)
    scaled.wait_recv()
    filter_sweep(zs, ua, 1, 5)
    filter_sweep(zs, ua, 11, 15)
    filter_sweep(ua, ub, 2, 6)
    filter_sweep(ua, ub, 10, 14)
    filter_sweep(ub, ua, 3, 7)
    filter_sweep(ub, ua, 9, 13)

    def last_filter(i):
        ub[i] = filter_at(ua, i)

    stores = [store_adj]
    for k in range(2):
        layers(4 + 4 * k, 8 + 4 * k, last_filter, 4)
        part = ub.at[pl.ds(4 + 4 * k, 4), pl.ds(8, 32)]
        store = pltpu.make_async_copy(part, outs.at[1, pl.ds(4 * k, 4)], in_sem.at[1 + k])
        store.start()
        stores.append(store)
    wire.flush(len(wire.groups))
    for store in stores:
        store.wait()


def local(density, temperature, aim, sink):
    vmem = lambda *shape: pltpu.VMEM(shape, F32)
    level0 = (16, 48, 256)
    level1 = (16, 32, 128)
    level2 = (7, 24, 128)
    scratch = [vmem(*level0), vmem(10, 48, 256)] + [vmem(*level0)] * 11 + [vmem(8, 2, 48, 128)]
    scratch += [vmem(512, 256), vmem(512, 128)]
    scratch += [vmem(4, *level1)] + [vmem(*level1)] * 6 + [vmem(10, 32, 128)]
    scratch += [vmem(4, *level2)] + [vmem(*level2)] * 6 + [vmem(7, 24, 128)]
    scratch += [vmem(NN, 5, 8, 128), vmem(NW, 5, 8, 128), vmem(NN, 8, 128), vmem(NW, 8, 128)]
    scratch += [vmem(NW, 8, 128), vmem(168, 128), vmem(BLANK_TILES, 8, 128)]
    scratch += [vmem(4, 3, 8, 256)] * 2
    scratch += [
        pltpu.SemaphoreType.DMA((4,)),
        pltpu.SemaphoreType.DMA((N_GROUPS,)),
        pltpu.SemaphoreType.DMA((N_GROUPS,)),
    ]
    block = jax.ShapeDtypeStruct((2, 8, 32, 256), F32)
    both = pl.pallas_call(
        kernel,
        out_shape=block,
        in_specs=[pl.BlockSpec(memory_space=pl.ANY)] * 4,
        out_specs=pl.BlockSpec(memory_space=pl.ANY),
        scratch_shapes=scratch,
        compiler_params=pltpu.CompilerParams(
            collective_id=0, has_side_effects=True, vmem_limit_bytes=62 * 2**20
        ),
    )(density, temperature, aim, sink)
    return both[0], both[1]


def solution(mesh):
    placed = P("wide", "narrow", None)
    return jax.shard_map(
        local,
        mesh=mesh,
        in_specs=(placed,) * 4,
        out_specs=(placed, placed),
        check_vma=False,
    )
```

```python
import functools
import math

import jax
import jax.numpy as jnp
from jax import lax
from jax.experimental import pallas as pl
from jax.experimental.pallas import tpu as pltpu
from jax.sharding import PartitionSpec as P

COARSE_ITERS = 8
RADIUS = 4
FLOOR_CONDUCTION = 0.001
OMEGA = 0.7
FILTER_OMEGA = 0.8
STRENGTH = (RADIUS / (2.0 * math.sqrt(3.0))) ** 2
MESH = pl.DeviceIdType.MESH
NW, NN = 16, 8
CELLS = 128 * 256 * 256
F32 = jnp.float32
BF16 = jnp.bfloat16
N_GROUPS = 19
BLANK_TILES = 200
UNROLL = {48: 4, 32: 8}


def near_peers(reach):
    peers = [
        (dw, dn)
        for dw in range(-reach, reach + 1)
        for dn in (-1, 0, 1)
        if (dw, dn) != (0, 0)
    ]
    return sorted(peers, key=lambda p: (p[1] != 0 and p[0] != 0, p[0] == 0, abs(p[0])))


def greeted():
    peers = [(dw % NW, dn % NN) for dw, dn in near_peers(3)]
    peers += [(0, k) for k in range(1, NN)] + [(k, 0) for k in range(1, NW)]
    return sorted(set(peers), key=lambda p: -min(p[0], NW - p[0]) - min(p[1], NN - p[1]))


def layers(lo, hi, body, unroll):
    steps = (hi - lo) // unroll

    def step(k, carry):
        for j in range(unroll):
            body(lo + k * unroll + j)
        return carry

    if steps > 1:
        lax.fori_loop(0, steps, step, 0)
    else:
        step(0, 0) if steps else None
    for i in range(lo + steps * unroll, hi):
        body(i)


class Group:
    def __init__(self, blank, send_sem, recv_sem):
        self.blank, self.send_sem, self.recv_sem = blank, send_sem, recv_sem
        self.tiles = 0

    def wait(self, sem):
        whole = self.blank.at[pl.ds(0, self.tiles)]
        pltpu.make_async_copy(whole, whole, sem).wait()

    def wait_recv(self):
        self.wait(self.recv_sem)


class Wire:
    def __init__(self, wide, narrow, blank, send_sem, recv_sem):
        self.wide, self.narrow, self.blank = wide, narrow, blank
        self.send_sem, self.recv_sem = send_sem, recv_sem
        self.groups = []
        self.sent = 0

    def peer(self, dw, dn):
        return (lax.rem(self.wide + (dw + NW), NW), lax.rem(self.narrow + (dn + NN), NN))

    def group(self):
        k = len(self.groups)
        self.groups.append(Group(self.blank, self.send_sem.at[k], self.recv_sem.at[k]))
        return self.groups[-1]

    def send(self, group, src, dst, dw, dn):
        pltpu.make_async_remote_copy(
            src_ref=src,
            dst_ref=dst,
            send_sem=group.send_sem,
            recv_sem=group.recv_sem,
            device_id=self.peer(dw, dn),
            device_id_type=MESH,
        ).start()
        group.tiles += math.prod(src.shape) // 1024

    def flush(self, last):
        for group in self.groups[self.sent : last]:
            group.wait(group.send_sem)
        self.sent = last


def cut(own, halo, width, shift):
    if shift == 0:
        return pl.ds(halo, own), pl.ds(halo, own)
    if shift > 0:
        return pl.ds(halo + own - width, width), pl.ds(halo - width, width)
    return pl.ds(halo, width), pl.ds(halo + own, width)


def up_y(v):
    return pltpu.roll(v, v.shape[0] - 1, 0)


def down_y(v):
    return pltpu.roll(v, 1, 0)


def up_z(v):
    return pltpu.roll(v, v.shape[1] - 1, 1)


def down_z(v):
    return pltpu.roll(v, 1, 1)


def coupling(u, ux, uy, uz, i):
    centre = u[i]
    fy, fz = uy[i], uz[i]
    return centre, (
        (ux[i] * u[i + 1] + ux[i - 1] * u[i - 1])
        + (fy * up_y(centre) + down_y(fy * centre))
        + (fz * up_z(centre) + down_z(fz * centre))
    )


def sweep(src, dst, rhs, ux, uy, uz, weight, lo, hi):
    def body(i):
        centre, pull = coupling(src, ux, uy, uz, i)
        dst[i] = (1.0 - OMEGA) * centre + weight[i] * (rhs[i] + pull)

    layers(lo, hi, body, UNROLL[src.shape[1]])


def residual_at(src, rhs, ux, uy, uz, diag, i):
    centre, pull = coupling(src, ux, uy, uz, i)
    return rhs[i] + pull - diag[i] * centre


def weights(sink, ux, uy, uz, diag, weight, lo, hi):
    def body(i):
        fy, fz = uy[i], uz[i]
        total = sink[i] + (ux[i] + ux[i - 1]) + (fy + down_y(fy)) + (fz + down_z(fz))
        diag[i] = total
        weight[i] = OMEGA / total

    layers(lo, hi, body, UNROLL[diag.shape[1]])


def next_x(here, above, low):
    return pltpu.roll(jnp.where(low, above, here), 64, 1)


def previous_x(here, below, low):
    return pltpu.roll(jnp.where(low, here, below), 64, 1)


def coupling2(u, ux, uy, uz, t, low):
    centre, above, below = u[t], u[min(t + 1, 6)], max(t - 1, 0)
    fy, fz = uy[t], uz[t]
    return centre, (
        (
            ux[t] * next_x(centre, above, low)
            + previous_x(ux[t] * centre, ux[below] * u[below], low)
        )
        + (fy * up_y(centre) + down_y(fy * centre))
        + (fz * up_z(centre) + down_z(fz * centre))
    )


def sweep2(src, dst, rhs, ux, uy, uz, weight, low, lo, hi):
    for t in range(lo, hi):
        centre, pull = coupling2(src, ux, uy, uz, t, low)
        dst[t] = (1.0 - OMEGA) * centre + weight[t] * (rhs[t] + pull)


def dot(a, b):
    b = b.astype(BF16)
    high = a.astype(BF16)
    rest = a - high.astype(F32)
    middle = rest.astype(BF16)
    low = (rest - middle.astype(F32)).astype(BF16)
    products = [jnp.dot(part, b, preferred_element_type=F32) for part in (low, middle, high)]
    return products[0] + products[1] + products[2]


def pair_matrix(rows, cols, odd):
    k = lax.broadcasted_iota(jnp.int32, (rows, cols), 0)
    j = lax.broadcasted_iota(jnp.int32, (rows, cols), 1)
    hit = (k == 2 * j + 1) if odd else (k // 2 == j)
    return jnp.where(hit, 1.0, 0.0).astype(F32)


def spread_matrix(rows, cols):
    k = lax.broadcasted_iota(jnp.int32, (rows, cols), 0)
    j = lax.broadcasted_iota(jnp.int32, (rows, cols), 1)
    return jnp.where(k == j // 2, 1.0, 0.0).astype(F32)


def conjugate(rhs, coef_ref, out_ref):
    lane = lax.broadcasted_iota(jnp.int32, (NW, 8, 128), 2)
    low, high = lane < 96, lane >= 32
    sink, ux, uy, uz = (coef_ref[:, k] for k in range(4))

    def y_up(v):
        q = pltpu.roll(v, 96, 2)
        return jnp.where(low, q, pltpu.roll(q, 7, 1))

    def y_down(v):
        q = pltpu.roll(v, 32, 2)
        return jnp.where(high, q, pltpu.roll(q, 1, 1))

    def z_up(v):
        return pltpu.roll(v, 127, 2)

    def z_down(v):
        return pltpu.roll(v, 1, 2)

    def total(v):
        parts = [v[k] for k in range(NW)]
        while len(parts) > 1:
            parts = [x + y for x, y in zip(parts[::2], parts[1::2])]
        return jnp.sum(parts[0], axis=(0, 1), keepdims=True)[None]

    edge = jnp.zeros((1, 8, 128), F32)
    dx = jnp.concatenate([edge, ux[:-1]], axis=0)
    diag = sink + (ux + dx) + (uy + y_down(uy)) + (uz + z_down(uz))

    def apply(p):
        above = jnp.concatenate([p[1:], edge], axis=0)
        px = ux * p
        below = jnp.concatenate([edge, px[:-1]], axis=0)
        return diag * p - (
            (ux * above + below)
            + (uy * y_up(p) + y_down(uy * p))
            + (uz * z_up(p) + z_down(uz * p))
        )

    def body(_, carry):
        solved, residual, direction, norm_now = carry
        applied = apply(direction)
        step = norm_now / total(direction * applied)
        solved = solved + step * direction
        residual = residual - step * applied
        norm_next = total(residual * residual)
        direction = residual + (norm_next / norm_now) * direction
        return solved, residual, direction, norm_next

    start = (jnp.zeros_like(rhs), rhs, rhs, total(rhs * rhs))
    solved, residual, direction, norm_now = lax.fori_loop(0, COARSE_ITERS - 1, body, start)
    step = norm_now / total(direction * apply(direction))
    out_ref[...] = solved + step * direction


def kernel(
    dens_in, temp_in, aim_in, sink_in, outs,
    dens, temp, aim, sink, ux0, uy0, uz0, d0, w0, ua, ub, v0, zs, lift0,
    stage, pairs,
    c1, f1, v1, d1, w1, p1, q1, lift1,
    c2, f2, v2, d2, w2, p2, q2, lift2,
    ga, gb, ra, rb, solved3, rows3, blank, corner_out, corner_in,
    in_sem, send_sem, recv_sem,
):
    wide, narrow = lax.axis_index("wide"), lax.axis_index("narrow")
    wire = Wire(wide, narrow, blank, send_sem, recv_sem)
    barrier = pltpu.get_barrier_semaphore()
    peers = greeted()
    for dw, dn in peers:
        pl.semaphore_signal(barrier, inc=1, device_id=wire.peer(dw, dn), device_id_type=MESH)

    own = (pl.ds(4, 8), pl.ds(8, 32))
    loads = []
    for k, (src, dst) in enumerate(
        ((dens_in, dens.at[own]), (sink_in, sink.at[own]), (aim_in, aim.at[own]),
         (temp_in, temp.at[pl.ds(1, 8), pl.ds(8, 32)]))
    ):
        load = pltpu.make_async_copy(src, dst, in_sem.at[k])
        load.start()
        loads.append(load)
    for load in loads:
        load.wait()
    pl.semaphore_wait(barrier, len(peers))

    def halo(ref, own_x, halo_x, width_x, own_y, lead=(), corner=0, group=None, targets=None):
        group = group or wire.group()
        for dw, dn in targets or near_peers(1):
            sx, tx = cut(own_x, halo_x, corner if corner and dn else width_x, dw)
            sy, ty = cut(own_y, 8, 8, dn)
            wire.send(group, ref.at[lead + (sx, sy)], ref.at[lead + (tx, ty)], dw, dn)
        return group

    sides = [(0, 1), (0, -1)]
    ends = [p for p in near_peers(1) if p[0]]
    beside = wire.group()
    for ref in (dens, sink, aim):
        halo(ref, 8, 4, 4, 32, group=beside, targets=sides)
    straight = [p for p in ends if not p[1]]
    corners = [p for p in ends if p[1]]
    first = halo(dens, 8, 4, 4, 32, targets=straight)

    row8 = lax.broadcasted_iota(jnp.int32, (8, 256), 0)
    packed = wire.group()
    for q, (dw, dn) in enumerate(corners):
        edge = pl.ds(32, 8) if dn > 0 else pl.ds(8, 8)
        for j in range(3):
            layer = (9 if dw > 0 else 4) + j
            d, s, a = dens[layer, edge], sink[layer, edge], aim[layer, edge]
            if dn > 0:
                rest = jnp.where(row8 >= 3, pltpu.roll(s, 5, 0), pltpu.roll(a, 3, 0))
                corner_out[q, j] = jnp.where(row8 >= 5, d, rest)
            else:
                rest = jnp.where(row8 < 5, pltpu.roll(s, 3, 0), pltpu.roll(a, 5, 0))
                corner_out[q, j] = jnp.where(row8 < 3, d, rest)
        wire.send(packed, corner_out.at[q], corner_in.at[q], dw, dn)
    second = halo(sink, 8, 4, 3, 32, targets=straight)
    third = halo(aim, 8, 4, 3, 32, targets=straight)
    temps = wire.group()
    for dw, dn in ((1, 0), (-1, 0), (0, 1), (0, -1)):
        sx, tx = cut(8, 1, 1, dw)
        sy, ty = cut(32, 8, 8, dn)
        wire.send(temps, temp.at[sx, sy], temp.at[tx, ty], dw, dn)

    goal_part = jnp.sum(aim[own] * temp[pl.ds(1, 8), pl.ds(8, 32)], axis=0)
    goal_part = jnp.sum(goal_part[:, :128] + goal_part[:, 128:], axis=0, keepdims=True)

    row0 = narrow * 32 - 8 + lax.broadcasted_iota(jnp.int32, (48, 256), 0)
    lane0 = lax.broadcasted_iota(jnp.int32, (48, 256), 1)
    hy = jnp.where((row0 == -1) | (row0 == 255), 0.0, 0.5).astype(F32)
    hz = jnp.where(lane0 == 255, 0.0, 0.5).astype(F32)

    def hx(i):
        g = wide * 8 - 4 + i
        return jnp.where((g == -1) | (g == 127), 0.0, 0.5).astype(F32)

    def conduct(i):
        s = dens[i]
        return FLOOR_CONDUCTION + (1.0 - FLOOR_CONDUCTION) * s * s * s

    s1, s1_odd = pair_matrix(256, 128, False), pair_matrix(256, 128, True)
    def faces(i):
        c = conduct(i)
        ux0[i] = (c + conduct(i + 1)) * hx(i)
        uy0[i] = (c + up_y(c)) * hy
        uz0[i] = (c + up_z(c)) * hz

    def first0(i):
        ua[i] = w0[i] * aim[i]

    level0 = (ux0, uy0, uz0)

    beside.wait_recv()
    layers(4, 11, faces, 4)
    weights(sink, *level0, d0, w0, 5, 11)
    layers(5, 11, first0, 3)
    sweep(ua, ub, aim, *level0, w0, 6, 10)
    sweep(ub, ua, aim, *level0, w0, 7, 9)

    first.wait_recv()
    packed.wait_recv()
    for q, (dw, dn) in enumerate(corners):
        edge = pl.ds(0, 8) if dn > 0 else pl.ds(40, 8)
        for j in range(3):
            layer = (1 if dw > 0 else 12) + j
            tile = corner_in[q, j]
            dens[layer, edge] = tile
            if j != (0 if dw > 0 else 2):
                sink[layer, edge] = pltpu.roll(tile, 3 if dn > 0 else 5, 0)
                aim[layer, edge] = pltpu.roll(tile, 5 if dn > 0 else 3, 0)
    ux0[0] = (conduct(0) + conduct(1)) * hx(0)
    layers(1, 4, faces, 3)
    layers(11, 15, faces, 4)

    rows = pl.ds(8, 32)
    for k in range(4):
        a, b = 4 + 2 * k, 5 + 2 * k
        stage[pl.ds(32 * k, 32)] = sink[a, rows] + sink[b, rows]
        stage[pl.ds(128 + 32 * k, 32)] = ux0[b, rows]
        stage[pl.ds(256 + 32 * k, 32)] = uy0[a, rows] + uy0[b, rows]
        stage[pl.ds(384 + 32 * k, 32)] = uz0[a, rows] + uz0[b, rows]
    pairs[pl.ds(0, 384)] = dot(stage[pl.ds(0, 384)], s1)
    pairs[pl.ds(384, 128)] = dot(stage[pl.ds(384, 128)], s1_odd)

    def even_odd(base, size):
        return (
            pairs[pl.ds(base, size // 2, stride=2)],
            pairs[pl.ds(base + 1, size // 2, stride=2)],
        )

    own1 = (pl.ds(6, 4), pl.ds(8, 16))
    for k in range(4):
        even, odd = even_odd(128 * k, 128)
        value = (even + odd, 0.5 * (even + odd), 0.5 * odd, 0.5 * (even + odd))[k]
        c1[(k,) + own1] = value.reshape(4, 16, 128)
    coarse1 = halo(c1, 4, 6, 4, 16, (slice(None),))
    for dn in (0, 1, -1):
        sy, ty = cut(16, 8, 8, dn)
        wire.send(coarse1, c1.at[1, pl.ds(9, 1), sy], c1.at[1, pl.ds(1, 1), ty], 2, dn)

    rows1, rows2 = pl.ds(8, 16), pl.ds(8, 8)
    for k in range(2):
        a, b = 6 + 2 * k, 7 + 2 * k
        half = pl.ds(128 * k, 128)
        stage[pl.ds(0, 16), half] = c1[0, a, rows1] + c1[0, b, rows1]
        stage[pl.ds(16, 16), half] = c1[1, b, rows1]
        stage[pl.ds(32, 16), half] = c1[2, a, rows1] + c1[2, b, rows1]
        stage[pl.ds(48, 16), half] = c1[3, a, rows1] + c1[3, b, rows1]
    pairs[pl.ds(0, 48)] = dot(stage[pl.ds(0, 48)], s1)
    pairs[pl.ds(48, 16)] = dot(stage[pl.ds(48, 16)], s1_odd)
    for k in range(4):
        even, odd = even_odd(16 * k, 16)
        value = (even + odd, 0.5 * (even + odd), 0.5 * odd, 0.5 * (even + odd))[k]
        c2[k, 3, rows2] = value

    def blocks2(ref, lead=()):
        group = wire.group()
        for dw, dn in near_peers(3):
            dst = ref.at[lead + (3 - dw, pl.ds(8 - 8 * dn, 8))]
            wire.send(group, ref.at[lead + (3, rows2)], dst, dw, dn)
        return group

    k3 = lax.broadcasted_iota(jnp.int32, (128, 128), 0)
    j3 = lax.broadcasted_iota(jnp.int32, (128, 128), 1)
    pair3 = (k3 % 64) // 2 == j3 % 32
    s3 = jnp.where(pair3, 1.0, 0.0).astype(F32)
    s3_upper = jnp.where(pair3 & (k3 >= 64), 1.0, 0.0).astype(F32)
    s3_odd = jnp.where(k3 % 64 == 2 * (j3 % 32) + 1, 1.0, 0.0).astype(F32)
    sub8 = lax.broadcasted_iota(jnp.int32, (8, 128), 0)
    lane8 = lax.broadcasted_iota(jnp.int32, (8, 128), 1)
    both_y = sub8 // 2 == lane8 // 32
    odd_y = sub8 == 2 * (lane8 // 32) + 1
    mine = sub8 == narrow

    def as_tile(row):
        return jnp.where(mine, jnp.broadcast_to(row, (8, 128)), 0.0)

    def to_row(values, matrix, mask):
        return jnp.sum(jnp.where(mask, dot(values, matrix), 0.0), axis=0, keepdims=True)

    tiles3 = (
        to_row(c2[0, 3, rows2], s3, both_y),
        0.5 * to_row(c2[1, 3, rows2], s3_upper, both_y),
        0.5 * to_row(c2[2, 3, rows2], s3, odd_y),
        0.5 * to_row(c2[3, 3, rows2], s3_odd, both_y),
        goal_part,
    )
    for k in range(5):
        ga[narrow, k] = as_tile(tiles3[k])
    def along_narrow(ref):
        group = wire.group()
        for dn in range(1, NN):
            wire.send(group, ref.at[narrow], ref.at[narrow], 0, dn)
        return group

    def along_wide(ref):
        group = wire.group()
        for dw in range(1, NW):
            wire.send(group, ref.at[wide], ref.at[wide], dw, 0)
        return group

    gather_a = along_narrow(ga)

    second.wait_recv()
    weights(sink, *level0, d0, w0, 1, 5)
    weights(sink, *level0, d0, w0, 11, 15)
    third.wait_recv()
    layers(1, 5, first0, 4)
    layers(11, 15, first0, 4)
    sweep(ua, ub, aim, *level0, w0, 2, 6)
    sweep(ua, ub, aim, *level0, w0, 10, 14)
    sweep(ub, ua, aim, *level0, w0, 3, 7)
    sweep(ub, ua, aim, *level0, w0, 9, 13)

    for k in range(4):
        a = 4 + 2 * k
        r = residual_at(ua, aim, ux0, uy0, uz0, d0, a) + residual_at(
            ua, aim, ux0, uy0, uz0, d0, a + 1
        )
        stage[pl.ds(32 * k, 32)] = r[8:40]
    pairs[pl.ds(0, 128)] = dot(stage[pl.ds(0, 128)], s1)
    even, odd = even_odd(0, 128)
    f1[own1] = (even + odd).reshape(4, 16, 128)
    right1 = halo(f1, 4, 6, 4, 16)
    v0[own] = ua[own]
    coarse2 = blocks2(c2, (slice(None),))
    gather_a.wait_recv()
    gb[wide] = jnp.sum(ga[...], axis=0)


    coarse1.wait_recv()
    weights(c1.at[0], c1.at[1], c1.at[2], c1.at[3], d1, w1, 2, 14)

    right1.wait_recv()

    level1 = (c1.at[1], c1.at[2], c1.at[3])

    def first1(i):
        p1[i] = w1[i] * f1[i]

    layers(3, 13, first1, 5)
    sweep(p1, q1, f1, *level1, w1, 4, 12)
    sweep(q1, p1, f1, *level1, w1, 5, 11)

    for k in range(2):
        a = 6 + 2 * k
        r = residual_at(p1, f1, *level1, d1, a) + residual_at(p1, f1, *level1, d1, a + 1)
        stage[pl.ds(0, 16), pl.ds(128 * k, 128)] = r[8:24]
    pairs[pl.ds(0, 16)] = dot(stage[pl.ds(0, 16)], s1)
    even, odd = even_odd(0, 16)
    f2[3, rows2] = even + odd
    right2 = blocks2(f2)
    before0 = halo(v0, 8, 4, 4, 32, corner=3)
    gather_b = along_wide(gb)
    coarse2.wait_recv()
    low2 = lax.broadcasted_iota(jnp.int32, (24, 128), 1) < 64
    for t in range(7):
        ux, uy, uz = c2[1, t], c2[2, t], c2[3, t]
        ux = ux + previous_x(ux, c2[1, max(t - 1, 0)], low2)
        d2[t] = c2[0, t] + ux + (uy + down_y(uy)) + (uz + down_z(uz))
        w2[t] = OMEGA / d2[t]

    right2.wait_recv()
    level2 = (c2.at[1], c2.at[2], c2.at[3])

    for t in range(1, 6):
        p2[t] = w2[t] * f2[t]
    sweep2(p2, q2, f2, *level2, w2, low2, 2, 5)
    sweep2(q2, p2, f2, *level2, w2, low2, 2, 5)
    centre, pull = coupling2(p2, *level2, 3, low2)
    r = f2[3] + pull - d2[3] * centre
    old = len(wire.groups)
    ra[narrow] = as_tile(to_row(r[8:16], s3, both_y))
    right3 = along_narrow(ra)
    v2[3, rows2] = p2[3, rows2]
    before2 = blocks2(v2)
    right3.wait_recv()
    rb[wide] = jnp.sum(ra[...], axis=0)
    right3 = along_wide(rb)
    v1[own1] = p1[own1]
    before1 = halo(v1, 4, 6, 4, 16)
    for dw, src, dst in ((2, 9, 1), (-2, 6, 14)):
        for dn in (0, 1, -1):
            sy, ty = cut(16, 8, 8, dn)
            wire.send(before1, v1.at[pl.ds(src, 1), sy], v1.at[pl.ds(dst, 1), ty], dw, dn)
    wire.flush(old)
    gather_b.wait_recv()
    goal = jnp.sum(jnp.sum(gb[:, 4], axis=0), axis=(0, 1), keepdims=True)
    right3.wait_recv()

    conjugate(rb[...], gb, solved3)

    for a in range(7):
        layer = lax.rem(wide + (a - 3 + NW), NW)
        for b in range(3):
            line = lax.rem(narrow + (b - 1 + NN), NN)
            row = jnp.broadcast_to(solved3[layer, pl.ds(line, 1)], (8, 128))
            rows3[pl.ds(24 * a + 8 * b, 8)] = jnp.where(both_y, row, 0.0)
    e3 = jnp.where(k3 % 32 == (j3 % 64) // 2, 1.0, 0.0).astype(F32)
    lift2[...] = dot(rows3[...], e3).reshape(7, 24, 128)
    before2.wait_recv()

    for t in range(7):
        p2[t] = v2[t] + lift2[t]
    sweep2(p2, q2, f2, *level2, w2, low2, 0, 7)
    sweep2(q2, p2, f2, *level2, w2, low2, 1, 6)
    sweep2(p2, q2, f2, *level2, w2, low2, 1, 6)

    e1 = spread_matrix(128, 256)
    lift = dot(q2[pl.ds(1, 5)].reshape(120, 128), e1).reshape(5, 24, 256)
    for t in range(5):
        for half in range(2):
            part = lift[t, 4:20, 128 * half : 128 * half + 128]
            lift1[2 * t + half, pl.ds(0, 16, stride=2)] = part
            lift1[2 * t + half, pl.ds(1, 16, stride=2)] = part
    before1.wait_recv()

    for i in range(1, 15):
        p1[i] = v1[i] + lift1[1 + i // 2]
    sweep(p1, q1, f1, *level1, w1, 2, 14)
    sweep(q1, p1, f1, *level1, w1, 3, 13)
    sweep(p1, q1, f1, *level1, w1, 4, 12)

    lift = dot(q1[pl.ds(4, 8), pl.ds(0, 32)].reshape(256, 128), e1).reshape(8, 32, 256)
    before0.wait_recv()
    for a in range(8):
        for half in range(2):
            part = lift[a, 4:28, 128 * half : 128 * half + 128]
            lift0[a, half, pl.ds(0, 24, stride=2)] = part
            lift0[a, half, pl.ds(1, 24, stride=2)] = part

    def correct0(k):
        both = jnp.concatenate([lift0[k, 0], lift0[k, 1]], axis=1)
        ua[2 * k] = v0[2 * k] + both
        ua[2 * k + 1] = v0[2 * k + 1] + both

    layers(0, 8, correct0, 4)
    sweep(ua, ub, aim, ux0, uy0, uz0, w0, 1, 15)
    sweep(ub, ua, aim, ux0, uy0, uz0, w0, 2, 14)

    temps.wait_recv()
    scale = (-0.5 * 3.0 * (1.0 - FLOOR_CONDUCTION)) * (CELLS / goal)
    my, mz = 2.0 * hy, 2.0 * hz

    def face_x(i):
        return (temp[i - 3] - temp[i - 2]) * (ub[i] - ub[i + 1]) * (2.0 * hx(i))

    def slope(i, below):
        t, a, s = temp[i - 3], ub[i], dens[i]
        above = face_x(i)
        fy = (t - up_y(t)) * (a - up_y(a)) * my
        fz = (t - up_z(t)) * (a - up_z(a)) * mz
        raw = (above + below) + (fy + down_y(fy)) + (fz + down_z(fz))
        zs[i, pl.ds(8, 32)] = (raw * scale * s * s)[8:40]
        return above

    sweep(ua, ub, aim, *level0, w0, 3, 9)
    below = face_x(3)
    for i in range(4, 8):
        below = slope(i, below)
    scaled = halo(zs, 8, 4, 4, 32, corner=3, targets=[p for p in ends if p[0] < 0])
    sweep(ua, ub, aim, *level0, w0, 9, 13)
    for i in range(8, 12):
        below = slope(i, below)
    halo(zs, 8, 4, 4, 32, corner=3, group=scaled, targets=[p for p in ends if p[0] > 0])
    scaled_beside = halo(zs, 8, 4, 4, 32, targets=sides)
    v0[own] = ub[own]
    store_adj = pltpu.make_async_copy(v0.at[own], outs.at[0], in_sem.at[0])
    store_adj.start()

    first_layer = jnp.where(wide == 0, 4, 0)
    last_layer = jnp.where(wide == NW - 1, 11, 15)
    top, bottom = row0 == 255, row0 == 0
    right, left = lane0 == 255, lane0 == 0
    c1_filter = FILTER_OMEGA / (1.0 + 6.0 * STRENGTH)

    def filter_at(src, i):
        z = src[i]
        near = src[jnp.minimum(i + 1, last_layer)] + src[jnp.maximum(i - 1, first_layer)]
        near = near + (jnp.where(top, z, up_y(z)) + jnp.where(bottom, z, down_y(z)))
        near = near + (jnp.where(right, z, up_z(z)) + jnp.where(left, z, down_z(z)))
        return (1.0 - FILTER_OMEGA) * z + c1_filter * (zs[i] + STRENGTH * near)

    def filter_sweep(src, dst, lo, hi):
        def body(i):
            dst[i] = filter_at(src, i)

        layers(lo, hi, body, 4)

    scaled_beside.wait_recv()
    filter_sweep(zs, ua, 5, 11)
    filter_sweep(ua, ub, 6, 10)
    filter_sweep(ub, ua, 7, 9)
    scaled.wait_recv()
    filter_sweep(zs, ua, 1, 5)
    filter_sweep(zs, ua, 11, 15)
    filter_sweep(ua, ub, 2, 6)
    filter_sweep(ua, ub, 10, 14)
    filter_sweep(ub, ua, 3, 7)
    filter_sweep(ub, ua, 9, 13)

    def last_filter(i):
        ub[i] = filter_at(ua, i)

    stores = [store_adj]
    for k in range(2):
        layers(4 + 4 * k, 8 + 4 * k, last_filter, 4)
        part = ub.at[pl.ds(4 + 4 * k, 4), pl.ds(8, 32)]
        store = pltpu.make_async_copy(part, outs.at[1, pl.ds(4 * k, 4)], in_sem.at[1 + k])
        store.start()
        stores.append(store)
    wire.flush(len(wire.groups))
    for store in stores:
        store.wait()


def local(density, temperature, aim, sink):
    vmem = lambda *shape: pltpu.VMEM(shape, F32)
    level0 = (16, 48, 256)
    level1 = (16, 32, 128)
    level2 = (7, 24, 128)
    scratch = [vmem(*level0), vmem(10, 48, 256)] + [vmem(*level0)] * 11 + [vmem(8, 2, 48, 128)]
    scratch += [vmem(512, 256), vmem(512, 128)]
    scratch += [vmem(4, *level1)] + [vmem(*level1)] * 6 + [vmem(10, 32, 128)]
    scratch += [vmem(4, *level2)] + [vmem(*level2)] * 6 + [vmem(7, 24, 128)]
    scratch += [vmem(NN, 5, 8, 128), vmem(NW, 5, 8, 128), vmem(NN, 8, 128), vmem(NW, 8, 128)]
    scratch += [vmem(NW, 8, 128), vmem(168, 128), vmem(BLANK_TILES, 8, 128)]
    scratch += [vmem(4, 3, 8, 256)] * 2
    scratch += [
        pltpu.SemaphoreType.DMA((4,)),
        pltpu.SemaphoreType.DMA((N_GROUPS,)),
        pltpu.SemaphoreType.DMA((N_GROUPS,)),
    ]
    block = jax.ShapeDtypeStruct((2, 8, 32, 256), F32)
    both = pl.pallas_call(
        kernel,
        out_shape=block,
        in_specs=[pl.BlockSpec(memory_space=pl.ANY)] * 4,
        out_specs=pl.BlockSpec(memory_space=pl.ANY),
        scratch_shapes=scratch,
        compiler_params=pltpu.CompilerParams(
            collective_id=0, has_side_effects=True, vmem_limit_bytes=62 * 2**20
        ),
    )(density, temperature, aim, sink)
    return both[0], both[1]


def solution(mesh):
    placed = P("wide", "narrow", None)
    return jax.shard_map(
        local,
        mesh=mesh,
        in_specs=(placed,) * 4,
        out_specs=(placed, placed),
        check_vma=False,
    )
```
